32 devices in a mesh: dp: 8 (over y, x, core), tensor: 4 (over z).
Axes of the slice: x: 2, y: 2, z: 4, core: 2. Of those that a mesh axis runs over, the one named last changes fastest.
Arguments:
- subword_embedding_rows: bfloat16 [32000, 512], P('dp'), may hold values from -6 to 6
- entry_subword_index: int32 [512, 8], P(('dp', 'tensor')), may hold values from 0 to 31999
- entry_lengths: int32 [512], P(('dp', 'tensor')), may hold values from 1 to 8
- entry_counts: int32 [512], P(('dp', 'tensor')), may hold values from 1 to 131071, as said below
- encoder_triple: bfloat16 [512, 1536], replicated, may hold values from -0.25 to 0.25
- encoder_merge: bfloat16 [512, 512], replicated, may hold values from -0.5 to 0.5
- encoder_expand: bfloat16 [512, 2048], replicated, may hold values from -0.25 to 0.25
- encoder_reduce: bfloat16 [2048, 512], replicated, may hold values from -0.125 to 0.125
- embed_project: bfloat16 [512, 2048], replicated, may hold values from -0.25 to 0.25
- normone_gain: float32 [512], replicated, may hold values from 0.1 to 1.9
- normtwo_gain: float32 [512], replicated, may hold values from 0.1 to 1.9
- frozen_query: bfloat16 [2048, 2048], P('dp', 'tensor'), may hold values from -0.125 to 0.125
- frozen_key: bfloat16 [2048, 256], P('dp', 'tensor'), may hold values from -0.125 to 0.125
- frozen_value: bfloat16 [2048, 256], P('dp', 'tensor'), may hold values from -0.125 to 0.125
- frozen_output: bfloat16 [2048, 2048], P('dp', 'tensor'), may hold values from -1.5 to 1.5
- frozen_gate: bfloat16 [2048, 5632], P('dp', 'tensor'), may hold values from -0.125 to 0.125
- frozen_upward: bfloat16 [2048, 5632], P('dp', 'tensor'), may hold values from -0.125 to 0.125
- frozen_downward: bfloat16 [2048, 5632], P('dp', 'tensor'), may hold values from -0.078125 to 0.078125
- prenorm_gain: float32 [2048], replicated, may hold values from 0.1 to 1.9
- midnorm_gain: float32 [2048], replicated, may hold values from 0.1 to 1.9
- text_tokens: int32 [8192], P(('dp', 'tensor')), may hold values from 0 to 511
- cotangent: bfloat16 [8192, 2048], P(('dp', 'tensor')), may hold values from -6 to 6
Outputs:
- layer_output: bfloat16 [8192, 2048], P(('dp', 'tensor'))
- entry_vectors: bfloat16 [512, 2048], P(('dp', 'tensor'))
- subword_grad: float32 [32000, 512], P(('dp', 'tensor'))
- triple_grad: float32 [512, 1536], P(('dp', 'tensor'))
- merge_grad: float32 [512, 512], P(('dp', 'tensor'))
- expand_grad: float32 [512, 2048], P(('dp', 'tensor'))
- reduce_grad: float32 [2048, 512], P(('dp', 'tensor'))
- project_grad: float32 [512, 2048], P(('dp', 'tensor'))
- normone_grad: float32 [512], P(('dp', 'tensor'))
- normtwo_grad: float32 [512], P(('dp', 'tensor'))
The draws below stay inside these ranges and needn't reach their ends.
Inputs may be any that keep to these rules, and one draw needn't show every extreme that they name: `entry_counts`: each entry's frequency lies between a power of two below 2^17 and twice it.
All inputs are finite; a program needn't handle non-finite values.
Results may differ from the reference program's by a relative error of at most 0.025.
Values may be sent and summed in bfloat16 or wider, within the bound.
No kernel may reach another device: no remote copies, remote signals or barrier semaphores. Data moves between devices by JAX's collectives and lax.ppermute only.
A program may use at most 256 MiB of HBM per device.

```python
import math
import jax
import jax.numpy as jnp
import numpy as np
from jax import lax

D = 2048
H = 32
KVH = 4
HD = 64
FF = 5632
SUBWORD_VOCAB = 32000
HYPER_WIDTH = 512
EH = 8
EHD = 64
EFF = 2048
SUBWORD_SLOTS = 8
SEQ = 1024
ENTRY_COUNT = 512
TOKENS = 8192


def draw_entry_counts(key, part):
    key = jax.random.fold_in(key, 5)
    split_one, split_two = jax.random.split(key)
    powers = jax.random.randint(split_one, (ENTRY_COUNT,), 0, 17)
    shifted = jnp.left_shift(jnp.ones((ENTRY_COUNT,), jnp.int32), powers)
    offsets = jax.random.randint(split_two, (ENTRY_COUNT,), 0, 65536)
    return shifted + offsets % shifted


def place_ends(array, stream_key, least, top_value):
    place = [jax.random.randint(jax.random.fold_in(stream_key, axis), (), 0, length) for axis, length in enumerate(array.shape)]
    main_axis = array.shape.index(max(array.shape))
    beside = place[:main_axis] + [(place[main_axis] + 1) % array.shape[main_axis]] + place[main_axis + 1:]
    return array.at[tuple(place)].set(least).at[tuple(beside)].set(top_value)


def shard_levels(rng, extent, pieces, least, top_value):
    loudness = 1.0
    for axis_at, shards_of in pieces:
        heights = jax.random.uniform(jax.random.fold_in(jax.random.fold_in(rng, 6), axis_at), (shards_of,), jnp.float32, least / len(pieces), top_value / len(pieces))
        loudness = loudness * jnp.repeat(jnp.exp(heights), extent[axis_at] // shards_of).reshape((-1,) + (1,) * (len(extent) - 1 - axis_at))
    return loudness


def rank_bounds(number_of, lean):
    portions = [(1 << 20) // math.isqrt(rank ** lean) + 1 for rank in range(1, number_of + 1)]
    deviation = 1 + sum(portions) // (1 << 30)
    return np.cumsum(np.array([max(1, weight // deviation) for weight in portions]))


def skewed_ids(own_key, dims, count, lean):
    grid = rank_bounds(count, lean)
    lot = jax.random.randint(jax.random.fold_in(own_key, 1), dims, 0, int(grid[count - 1]))
    rank = jnp.searchsorted(jnp.asarray(grid, jnp.int32), lot, side="right")
    return jax.random.permutation(jax.random.fold_in(own_key, 2), count)[rank].astype(jnp.int32)


def centred(rng, shape, scale, limit, cuts=(), held_as=jnp.bfloat16):
    result = jax.random.normal(rng, shape, jnp.float32) * scale
    if len(cuts) > 0:
        result = shard_levels(rng, shape, cuts, -0.22, 0.18) * result
    return jnp.clip(result, min=-limit, max=limit).astype(held_as)


def setup_inputs(seed: int = 0) -> dict:
    streams_of = jax.random.split(jax.random.key(seed), 23)
    subword_embedding_rows = centred(streams_of[0], (SUBWORD_VOCAB, HYPER_WIDTH), 1.0, 6.0, ((0, 8),))
    entry_subword_index = place_ends(jax.random.randint(streams_of[1], (ENTRY_COUNT, SUBWORD_SLOTS), 0, SUBWORD_VOCAB), jax.random.fold_in(streams_of[1], 1), 0, SUBWORD_VOCAB - 1).astype(jnp.int32)
    entry_lengths = place_ends(jax.random.randint(streams_of[2], (ENTRY_COUNT,), 1, SUBWORD_SLOTS + 1), jax.random.fold_in(streams_of[2], 1), 1, SUBWORD_SLOTS).astype(jnp.int32)
    entry_counts = draw_entry_counts(jax.random.fold_in(streams_of[22], 71), 0)
    encoder_triple = centred(streams_of[4], (HYPER_WIDTH, 3 * HYPER_WIDTH), HYPER_WIDTH ** -0.5, 0.25)
    encoder_merge = centred(streams_of[5], (HYPER_WIDTH, HYPER_WIDTH), (HYPER_WIDTH // 4) ** -0.5, 0.5)
    encoder_expand = centred(streams_of[6], (HYPER_WIDTH, EFF), HYPER_WIDTH ** -0.5, 0.25)
    encoder_reduce = centred(streams_of[7], (EFF, HYPER_WIDTH), EFF ** -0.5, 0.125)
    embed_project = centred(streams_of[8], (HYPER_WIDTH, D), HYPER_WIDTH ** -0.5, 0.25)
    normone_gain = jnp.clip(1.0 + 0.18 * jax.random.normal(streams_of[9], (HYPER_WIDTH,), jnp.float32), 0.1, 1.9)
    normtwo_gain = jnp.clip(1.0 + 0.18 * jax.random.normal(streams_of[10], (HYPER_WIDTH,), jnp.float32), 0.1, 1.9)
    frozen_query = centred(streams_of[11], (D, H * HD), D ** -0.5, 0.125, ((0, 8), (1, 4)))
    frozen_key = centred(streams_of[12], (D, KVH * HD), D ** -0.5, 0.125, ((0, 8), (1, 4)))
    frozen_value = centred(streams_of[13], (D, KVH * HD), D ** -0.5, 0.125, ((0, 8), (1, 4)))
    frozen_output = centred(streams_of[14], (D, H * HD), 16 ** -0.5, 1.5, ((0, 8), (1, 4)))
    frozen_gate = centred(streams_of[15], (D, FF), D ** -0.5, 0.125, ((0, 8), (1, 4)))
    frozen_upward = centred(streams_of[16], (D, FF), D ** -0.5, 0.125, ((0, 8), (1, 4)))
    frozen_downward = centred(streams_of[17], (D, FF), FF ** -0.5, 0.078125, ((0, 8), (1, 4)))
    prenorm_gain = jnp.clip(1.0 + 0.18 * jax.random.normal(streams_of[18], (D,), jnp.float32), 0.1, 1.9)
    midnorm_gain = jnp.clip(1.0 + 0.18 * jax.random.normal(streams_of[19], (D,), jnp.float32), 0.1, 1.9)
    text_tokens = place_ends(skewed_ids(streams_of[20], (TOKENS,), ENTRY_COUNT, 1), jax.random.fold_in(streams_of[20], 3), 0, ENTRY_COUNT - 1).astype(jnp.int32)
    cotangent = centred(streams_of[21], (TOKENS, D), 1.0, 6.0, ((0, 32),))
    return {"subword_embedding_rows": subword_embedding_rows, "entry_subword_index": entry_subword_index, "entry_lengths": entry_lengths, "entry_counts": entry_counts, "encoder_triple": encoder_triple, "encoder_merge": encoder_merge, "encoder_expand": encoder_expand, "encoder_reduce": encoder_reduce, "embed_project": embed_project, "normone_gain": normone_gain, "normtwo_gain": normtwo_gain, "frozen_query": frozen_query, "frozen_key": frozen_key, "frozen_value": frozen_value, "frozen_output": frozen_output, "frozen_gate": frozen_gate, "frozen_upward": frozen_upward, "frozen_downward": frozen_downward, "prenorm_gain": prenorm_gain, "midnorm_gain": midnorm_gain, "text_tokens": text_tokens, "cotangent": cotangent}


HIGH = lax.Precision.HIGHEST
NEG = -1000000000.0
EPS = 1e-05
THETA = 10000.0

@jax.custom_vjp
def low(v):
    return lax.optimization_barrier(v.astype(jnp.bfloat16)).astype(jnp.float32)

@jax.custom_vjp
def low_back(v):
    return v

def low_keep(v):
    return (low(v), None)

def low_pass(kept, grad):
    return (grad,)

def back_keep(v):
    return (v, None)

def back_low(kept, grad):
    return (low(grad),)
low.defvjp(low_keep, low_pass)
low_back.defvjp(back_keep, back_low)

def both_ways(values):
    return low(low_back(values))

def layer_norm(values, gain):
    center = values - lax.optimization_barrier(jnp.mean(values, axis=-1, keepdims=True))
    spread = lax.optimization_barrier(jnp.mean(center * center, axis=-1, keepdims=True))
    return center * lax.rsqrt(spread + EPS) * gain

def rms_norm(values, gain):
    return values * lax.rsqrt(lax.optimization_barrier(jnp.mean(values * values, axis=-1, keepdims=True)) + EPS) * gain

def rope_tables(length, width):
    half_width = width // 2
    inverse = THETA ** (-(2.0 * jnp.arange(half_width, dtype=jnp.float32)) / width)
    angles = jnp.arange(length, dtype=jnp.float32)[:, None] * inverse[None, :]
    return (jnp.cos(angles), jnp.sin(angles))

def rotate(values, cosine, sine):
    half_width = values.shape[-1] // 2
    former = values[..., :half_width]
    latter = values[..., half_width:]
    return jnp.concatenate([former * cosine - latter * sine, latter * cosine + former * sine], axis=-1)

def matmul(left, right):
    return jnp.dot(left, right, precision=HIGH)

def times_trans(left, right):
    return lax.dot_general(left, right, (((1,), (1,)), ((), ())), precision=HIGH)

def encoder(table, entry_subword_index, entry_lengths, triple_w, merge_w, expand_w, reduce_w, project_w, gain_one, gain_two):
    entries = entry_subword_index.shape[0]
    rows_in = low_back(jnp.take(table, entry_subword_index, axis=0))
    valid = jnp.arange(SUBWORD_SLOTS)[None, :] < entry_lengths[:, None]
    first_in = low(layer_norm(rows_in, gain_one))
    triple = both_ways(jnp.einsum('nse,ef->nsf', first_in, triple_w, precision=HIGH))
    queries = triple[..., :HYPER_WIDTH].reshape(entries, SUBWORD_SLOTS, EH, EHD)
    keyset = triple[..., HYPER_WIDTH:2 * HYPER_WIDTH].reshape(entries, SUBWORD_SLOTS, EH, EHD)
    valset = triple[..., 2 * HYPER_WIDTH:].reshape(entries, SUBWORD_SLOTS, EH, EHD)
    scores = low_back(jnp.einsum('nqhd,nkhd->nhqk', queries, keyset, precision=HIGH) * EHD ** (-0.5))
    scores = jnp.where(valid[:, None, None, :], scores, NEG)
    probs = low(jax.nn.softmax(scores, axis=-1))
    mixed = both_ways(jnp.einsum('nhqk,nkhd->nqhd', probs, valset, precision=HIGH).reshape(entries, SUBWORD_SLOTS, HYPER_WIDTH))
    resid_one = rows_in + low_back(jnp.einsum('nse,ef->nsf', mixed, merge_w, precision=HIGH))
    second_in = low(layer_norm(resid_one, gain_two))
    expanded = low_back(jnp.einsum('nse,ef->nsf', second_in, expand_w, precision=HIGH))
    activated = low(jax.nn.gelu(expanded, approximate=False))
    resid_two = resid_one + low_back(jnp.einsum('nsf,fe->nse', activated, reduce_w, precision=HIGH))
    pooled = lax.optimization_barrier(jnp.sum(jnp.where(valid[:, :, None], resid_two, 0.0), axis=1)) / entry_lengths.astype(jnp.float32)[:, None]
    pooled = low(pooled)
    return both_ways(matmul(pooled, project_w))

def frozen_layer(resid_in, frozen, gains, cosine, sine):
    full_query, full_key, full_value, full_output, full_gate, full_upward, full_downward = frozen
    length = resid_in.shape[0]

    def to_heads(values, count):
        return values.reshape(length, count, HD).transpose(1, 0, 2)
    seq_one = low(rms_norm(resid_in, gains[0]))
    queries = low(rotate(to_heads(low_back(matmul(seq_one, full_query)), H), cosine, sine))
    keyset = low(rotate(to_heads(low_back(matmul(seq_one, full_key)), KVH), cosine, sine))
    valset = both_ways(to_heads(matmul(seq_one, full_value), KVH))
    share = H // KVH
    keys_wide = jnp.repeat(keyset, share, axis=0)
    values_wide = jnp.repeat(valset, share, axis=0)
    scores = low_back(jnp.einsum('hqd,hkd->hqk', queries, keys_wide, precision=HIGH) * HD ** (-0.5))
    causal = jnp.arange(length)[:, None] >= jnp.arange(length)[None, :]
    scores = jnp.where(causal[None], scores, NEG)
    probs = low(jax.nn.softmax(scores, axis=-1))
    mixed = both_ways(jnp.einsum('hqk,hkd->hqd', probs, values_wide, precision=HIGH))
    mixed = mixed.transpose(1, 0, 2).reshape(length, H * HD)
    resid_mid = resid_in + low_back(times_trans(mixed, full_output))
    seq_two = low(rms_norm(resid_mid, gains[1]))
    gate = low_back(matmul(seq_two, full_gate))
    upward = low_back(matmul(seq_two, full_upward))
    swiglu = low(jax.nn.silu(gate) * upward)
    return resid_mid + low_back(times_trans(swiglu, full_downward))

def reference(subword_embedding_rows, entry_subword_index, entry_lengths, entry_counts, encoder_triple, encoder_merge, encoder_expand, encoder_reduce, embed_project, normone_gain, normtwo_gain, frozen_query, frozen_key, frozen_value, frozen_output, frozen_gate, frozen_upward, frozen_downward, prenorm_gain, midnorm_gain, text_tokens, cotangent):
    single = jnp.float32
    token_weight = low(1.0 / jnp.log(1.0 + entry_counts.astype(single)))
    frozen = tuple((weight.astype(single) for weight in (frozen_query, frozen_key, frozen_value, frozen_output, frozen_gate, frozen_upward, frozen_downward)))
    gains = (prenorm_gain.astype(single), midnorm_gain.astype(single))
    cosine, sine = rope_tables(SEQ, HD)
    seq_tokens = text_tokens.reshape(-1, SEQ)
    seq_cot = cotangent.astype(single).reshape(-1, SEQ, D)

    def forward(table, triple_w, merge_w, expand_w, reduce_w, project_w, gain_one, gain_two):
        vectors = encoder(table, entry_subword_index, entry_lengths, triple_w, merge_w, expand_w, reduce_w, project_w, gain_one, gain_two)

        def one_sequence(total, pair):
            tokens, weights_cot = pair
            resid_in = low_back(jnp.take(vectors, tokens, axis=0))
            final = frozen_layer(resid_in, frozen, gains, cosine, sine)
            weighted = jnp.take(token_weight, tokens, axis=0)[:, None] * weights_cot
            return (total + jnp.sum(weighted * final), low(final))
        total, final_vectors = lax.scan(jax.checkpoint(one_sequence), jnp.zeros((), single), (seq_tokens, seq_cot))
        return (total, (vectors, final_vectors))
    params = (subword_embedding_rows.astype(single), encoder_triple.astype(single), encoder_merge.astype(single), encoder_expand.astype(single), encoder_reduce.astype(single), embed_project.astype(single), normone_gain.astype(single), normtwo_gain.astype(single))
    loss, backward, extras = jax.vjp(forward, *params, has_aux=True)
    grads = backward(jnp.ones_like(loss))
    vectors, final_vectors = extras
    return (final_vectors.reshape(-1, D).astype(jnp.bfloat16), vectors.astype(jnp.bfloat16), grads[0], grads[1], grads[2], grads[3], grads[4], grads[5], grads[6], grads[7])
```

```python
from functools import partial

import jax
import jax.numpy as jnp
from jax import lax
from jax.sharding import PartitionSpec as P

HD = 64
HYPER_WIDTH = 512
EH = 8
EHD = 64
SUBWORD_SLOTS = 8


NEG = -1000000000.0
EPS = 1e-05
THETA = 10000.0


def layer_norm(values, gain):
    center = values - jnp.mean(values, axis=-1, keepdims=True)
    spread = jnp.mean(center * center, axis=-1, keepdims=True)
    return center * lax.rsqrt(spread + EPS) * gain


def rms_norm(values, gain):
    return values * lax.rsqrt(jnp.mean(values * values, axis=-1, keepdims=True) + EPS) * gain


def rope_tables(length, width):
    half_width = width // 2
    inverse = THETA ** (-(2.0 * jnp.arange(half_width, dtype=jnp.float32)) / width)
    angles = jnp.arange(length, dtype=jnp.float32)[:, None] * inverse[None, :]
    return (jnp.cos(angles), jnp.sin(angles))


def rotate(values, cosine, sine):
    half_width = values.shape[-1] // 2
    former = values[..., :half_width]
    latter = values[..., half_width:]
    return jnp.concatenate(
        [former * cosine - latter * sine, latter * cosine + former * sine], axis=-1
    )


def matmul(left, right):
    return jnp.dot(left, right, preferred_element_type=jnp.float32)


def times_trans(left, right):
    return lax.dot_general(
        left, right, (((1,), (1,)), ((), ())), preferred_element_type=jnp.float32
    )


def trans_times(left, right):
    return lax.dot_general(
        left, right, (((0,), (0,)), ((), ())), preferred_element_type=jnp.float32
    )


def ring(values, shift=1):
    size = lax.axis_size("tensor")
    return lax.ppermute(values, "tensor", [(i, (i + shift) % size) for i in range(size)])


def in_order(blocks, first):
    size = len(blocks)
    stacked = jnp.stack(blocks)
    return [
        lax.dynamic_index_in_dim(stacked, lax.rem(first - at + size, size), 0, keepdims=False)
        for at in range(size)
    ]


def per_device(
    subword_embedding_rows,
    entry_subword_index,
    entry_lengths,
    entry_counts,
    encoder_triple,
    encoder_merge,
    encoder_expand,
    encoder_reduce,
    embed_project,
    normone_gain,
    normtwo_gain,
    frozen_query,
    frozen_key,
    frozen_value,
    frozen_output,
    frozen_gate,
    frozen_upward,
    frozen_downward,
    prenorm_gain,
    midnorm_gain,
    text_tokens,
    cotangent,
):
    bfloat = jnp.bfloat16
    single = jnp.float32
    dp_size = lax.axis_size("dp")
    tensor_size = lax.axis_size("tensor")
    dp_at = lax.axis_index("dp")
    tensor_at = lax.axis_index("tensor")
    device_at = dp_at * tensor_size + tensor_at
    entries = entry_subword_index.shape[0]
    entry_total = entries * dp_size * tensor_size
    flat_rows = entries * SUBWORD_SLOTS
    table_rows = subword_embedding_rows.shape[0]
    model_width = embed_project.shape[1]

    with jax.named_scope("ids"):
        packed = jnp.concatenate([entry_subword_index, entry_counts[:, None]], axis=1)
        packed_dp = lax.all_gather(packed, "dp", axis=0, tiled=False)
        packed_all = lax.all_gather(
            jnp.concatenate([packed_dp.reshape(-1), text_tokens]), "tensor", axis=0, tiled=False
        )
    with jax.named_scope("qkv_weights"):
        frozen_triple = jnp.concatenate([frozen_query, frozen_key, frozen_value], axis=1)
        full_triple = lax.all_gather(frozen_triple, "dp", axis=0, tiled=True)
    with jax.named_scope("output_weights"):
        wide_output = lax.all_gather(frozen_output, "tensor", axis=1, tiled=True)
        full_output = lax.all_gather(wide_output, "dp", axis=0, tiled=True)
    with jax.named_scope("mlp_weights"):
        full_downward = lax.all_gather(frozen_downward, "dp", axis=0, tiled=True)
        full_gate = lax.all_gather(frozen_gate, "dp", axis=0, tiled=True)
        full_upward = lax.all_gather(frozen_upward, "dp", axis=0, tiled=True)
    with jax.named_scope("cot_ring"):
        cot_blocks = [cotangent]
        for _ in range(tensor_size - 1):
            cot_blocks.append(ring(cot_blocks[-1]))

    with jax.named_scope("lookup"):
        local_ids = packed_dp[:, :, :SUBWORD_SLOTS].reshape(-1) - dp_at * table_rows
        inside = (local_ids >= 0) & (local_ids < table_rows)
        served = jnp.take(
            subword_embedding_rows, jnp.clip(local_ids, 0, table_rows - 1), axis=0
        )
        served = jnp.where(inside[:, None], served, jnp.zeros((), bfloat))
        served = lax.all_to_all(
            served.reshape(dp_size, flat_rows, HYPER_WIDTH), "dp", 0, 0, tiled=True
        )
        rows_in = jnp.sum(served.astype(single), axis=0)

    with jax.named_scope("hyper_fwd"):
        valid = jnp.arange(SUBWORD_SLOTS)[None, :] < entry_lengths[:, None]
        normed_one, norm_back_one = jax.vjp(layer_norm, rows_in, normone_gain)
        first_in = normed_one.astype(bfloat)
        triple = matmul(first_in, encoder_triple).astype(bfloat)
        enc_queries = triple[:, :HYPER_WIDTH].reshape(entries, SUBWORD_SLOTS, EH, EHD)
        enc_keys = triple[:, HYPER_WIDTH : 2 * HYPER_WIDTH].reshape(
            entries, SUBWORD_SLOTS, EH, EHD
        )
        enc_values = triple[:, 2 * HYPER_WIDTH :].reshape(entries, SUBWORD_SLOTS, EH, EHD)
        enc_scale = EHD ** (-0.5)
        enc_scores = (
            jnp.einsum("nqhd,nkhd->nhqk", enc_queries, enc_keys, preferred_element_type=single)
            * enc_scale
        )
        enc_scores = jnp.where(valid[:, None, None, :], enc_scores, NEG)
        enc_probs = jax.nn.softmax(enc_scores, axis=-1)
        enc_probs_low = enc_probs.astype(bfloat)
        enc_mixed = jnp.einsum(
            "nhqk,nkhd->nqhd", enc_probs_low, enc_values, preferred_element_type=single
        )
        enc_mixed = enc_mixed.reshape(flat_rows, HYPER_WIDTH).astype(bfloat)
        resid_one = rows_in + matmul(enc_mixed, encoder_merge)
        normed_two, norm_back_two = jax.vjp(layer_norm, resid_one, normtwo_gain)
        second_in = normed_two.astype(bfloat)
        expanded = matmul(second_in, encoder_expand)
        activated, gelu_back = jax.vjp(partial(jax.nn.gelu, approximate=False), expanded)
        activated_low = activated.astype(bfloat)
        resid_two = resid_one + matmul(activated_low, encoder_reduce)
        slot_counts = entry_lengths.astype(single)[:, None]
        pooled = (
            jnp.sum(
                jnp.where(
                    valid[:, :, None],
                    resid_two.reshape(entries, SUBWORD_SLOTS, HYPER_WIDTH),
                    0.0,
                ),
                axis=1,
            )
            / slot_counts
        )
        pooled_low = pooled.astype(bfloat)
    with jax.named_scope("pooled_gather"):
        all_pooled = lax.all_gather(pooled_low, "tensor", axis=0, tiled=True)
        all_pooled = lax.all_gather(all_pooled, "dp", axis=0, tiled=True)

    with jax.named_scope("entry_vectors"):
        all_vectors = matmul(all_pooled, embed_project).astype(bfloat)
        vectors = lax.dynamic_slice_in_dim(all_vectors, device_at * entries, entries, 0)
        packed_ids = packed_all[:, : dp_size * entries * (SUBWORD_SLOTS + 1)].reshape(
            tensor_size, dp_size, entries, SUBWORD_SLOTS + 1
        )
        packed_ids = packed_ids.transpose(1, 0, 2, 3).reshape(entry_total, SUBWORD_SLOTS + 1)
        all_ids = packed_ids[:, :SUBWORD_SLOTS].reshape(-1)
        all_weights = (1.0 / jnp.log(1.0 + packed_ids[:, SUBWORD_SLOTS].astype(single))).astype(
            bfloat
        )
        seq_tokens = packed_all[:, dp_size * entries * (SUBWORD_SLOTS + 1) :].reshape(-1)
        length = seq_tokens.shape[0]
        rows_here = text_tokens.shape[0]
        seq_hot = (seq_tokens[:, None] == jnp.arange(entry_total)[None, :]).astype(bfloat)
        own_hot = (text_tokens[:, None] == jnp.arange(entry_total)[None, :]).astype(bfloat)
        seq_weight = matmul(seq_hot, all_weights[:, None])
        all_wide = all_vectors.astype(single)
        entry_normed, entry_norm_back = jax.vjp(
            lambda values: rms_norm(values, prenorm_gain), all_wide
        )
        entry_normed = entry_normed.astype(bfloat)
        entry_triple = matmul(entry_normed, full_triple)
        entry_high = entry_triple.astype(bfloat)
        entry_rest = (entry_triple - entry_high.astype(single)).astype(bfloat)
        seq_triple = matmul(seq_hot, entry_high) + matmul(seq_hot, entry_rest)
        resid_in = matmul(own_hot, all_vectors)

    heads_here = frozen_query.shape[1] // HD
    groups_here = frozen_key.shape[1] // HD
    query_width = frozen_query.shape[1]
    key_width = frozen_key.shape[1]
    share = heads_here // groups_here
    cosine, sine = rope_tables(length, HD)

    def to_heads(values, count):
        return values.reshape(length, count, HD).transpose(1, 0, 2)

    def from_heads(values):
        return values.transpose(1, 0, 2).reshape(length, values.shape[0] * HD)

    with jax.named_scope("attention_fwd"):
        lm_queries = rotate(
            to_heads(seq_triple[:, :query_width], heads_here), cosine, sine
        ).astype(bfloat)
        lm_keys = rotate(
            to_heads(seq_triple[:, query_width : query_width + key_width], groups_here),
            cosine,
            sine,
        ).astype(bfloat)
        lm_values = to_heads(seq_triple[:, query_width + key_width :], groups_here).astype(bfloat)
        block_rows = min(512, length)
        block_total = length // block_rows
        head_scale = HD ** (-0.5)

        def block_scores(block_idx):
            first = block_idx * block_rows
            key_end = first + block_rows
            query_block = lm_queries[:, first:key_end].reshape(groups_here, share, block_rows, HD)
            scores = (
                jnp.einsum(
                    "cgqd,ckd->cgqk",
                    query_block,
                    lm_keys[:, :key_end],
                    preferred_element_type=single,
                )
                * head_scale
            )
            causal = (first + jnp.arange(block_rows))[:, None] >= jnp.arange(key_end)[None, :]
            return (query_block, jnp.where(causal, scores, NEG))

        outputs = []
        lse_list = []
        for block_idx in range(block_total):
            key_end = (block_idx + 1) * block_rows
            query_block, scores = block_scores(block_idx)
            largest = jnp.max(scores, axis=-1, keepdims=True)
            expon = jnp.exp(scores - largest)
            total = jnp.sum(expon, axis=-1, keepdims=True)
            lse_list.append(largest + jnp.log(total))
            probs_low = (expon / total).astype(bfloat)
            block_out = jnp.einsum(
                "cgqk,ckd->cgqd", probs_low, lm_values[:, :key_end], preferred_element_type=single
            )
            outputs.append(block_out.reshape(heads_here, block_rows, HD))
        lm_mixed = from_heads(jnp.concatenate(outputs, axis=1)).astype(bfloat)
        own_mixed = lax.all_to_all(lm_mixed, "tensor", 0, 1, tiled=True)

    with jax.named_scope("attention_out"):
        resid_mid = resid_in + times_trans(own_mixed, full_output)
        pre_two, pre_back_two = jax.vjp(lambda values: rms_norm(values, midnorm_gain), resid_mid)

    with jax.named_scope("mlp_ring"):
        weight_blocks = seq_weight.reshape(tensor_size, rows_here, 1)
        block_at = [
            lax.rem(tensor_at - step + tensor_size, tensor_size) for step in range(tensor_size)
        ]
        out_cot = None
        seq_block = pre_two.astype(bfloat)
        carried = None
        own_part = None
        swiglu_blocks = []
        for step in range(tensor_size):
            now = seq_block
            if step < tensor_size - 1:
                seq_block = ring(seq_block)
            weight_block = lax.dynamic_index_in_dim(
                weight_blocks, block_at[step], 0, keepdims=False
            )
            cot_block = weight_block * cot_blocks[step].astype(single)
            if step == 0:
                out_cot = cot_block
            swiglu_grad = matmul(cot_block.astype(bfloat), full_downward)
            gate_raw = matmul(now, full_gate)
            upward_raw = matmul(now, full_upward)
            swiglu, swiglu_back = jax.vjp(
                lambda gate, upward: jax.nn.silu(gate) * upward, gate_raw, upward_raw
            )
            swiglu_blocks.append(swiglu.astype(bfloat))
            gate_grad, upward_grad = swiglu_back(swiglu_grad)
            part = times_trans(gate_grad.astype(bfloat), full_gate) + times_trans(
                upward_grad.astype(bfloat), full_upward
            )
            if step == 0:
                own_part = part
            else:
                if carried is not None:
                    part = part + carried.astype(single)
                carried = ring(part.astype(bfloat))
        norm_two_grad = own_part if carried is None else own_part + carried.astype(single)

    with jax.named_scope("layer_out"):
        swiglu_low = jnp.concatenate(in_order(swiglu_blocks, tensor_at), axis=0)
        layer_final = resid_mid + lax.psum_scatter(
            times_trans(swiglu_low, full_downward).astype(bfloat),
            "tensor",
            scatter_dimension=0,
            tiled=True,
        ).astype(single)

    with jax.named_scope("attention_bwd"):
        mid_grad = out_cot + pre_back_two(norm_two_grad)[0]
        mid_low = mid_grad.astype(bfloat)
        own_mixed_grad = matmul(mid_low, full_output).astype(bfloat)
        mixed_grad = to_heads(
            lax.all_to_all(own_mixed_grad, "tensor", 1, 0, tiled=True), heads_here
        )
        query_parts = []
        key_acc = jnp.zeros((groups_here, length, HD), single)
        value_acc = jnp.zeros((groups_here, length, HD), single)
        for block_idx in range(block_total):
            first = block_idx * block_rows
            key_end = first + block_rows
            query_block, scores = block_scores(block_idx)
            probs = jnp.exp(scores - lse_list[block_idx])
            grad_block = mixed_grad[:, first:key_end].reshape(groups_here, share, block_rows, HD)
            prob_grad = jnp.einsum(
                "cgqd,ckd->cgqk", grad_block, lm_values[:, :key_end], preferred_element_type=single
            )
            delta = jnp.sum(probs * prob_grad, axis=-1, keepdims=True)
            score_grad = (probs * (prob_grad - delta)).astype(bfloat)
            block_query = jnp.einsum(
                "cgqk,ckd->cgqd", score_grad, lm_keys[:, :key_end], preferred_element_type=single
            )
            query_parts.append(block_query.reshape(heads_here, block_rows, HD) * head_scale)
            key_part = (
                jnp.einsum("cgqk,cgqd->ckd", score_grad, query_block, preferred_element_type=single)
                * head_scale
            )
            key_acc = key_acc.at[:, :key_end].add(key_part)
            value_part = jnp.einsum(
                "cgqk,cgqd->ckd", probs.astype(bfloat), grad_block, preferred_element_type=single
            )
            value_acc = value_acc.at[:, :key_end].add(value_part)
        query_grad = from_heads(rotate(jnp.concatenate(query_parts, axis=1), cosine, -sine)).astype(
            bfloat
        )
        key_grad = from_heads(rotate(key_acc, cosine, -sine)).astype(bfloat)
        value_grad = from_heads(value_acc).astype(bfloat)
        triple_out = jnp.concatenate([query_grad, key_grad, value_grad], axis=1)

    with jax.named_scope("entry_bwd"):
        entry_out = trans_times(seq_hot, triple_out).astype(bfloat)
        entry_part = entry_norm_back(times_trans(entry_out, full_triple))[0]
        entry_part = (entry_part + trans_times(own_hot, mid_low)).astype(bfloat)
        project_part = trans_times(all_pooled, entry_part).astype(bfloat)
        pooled_part = times_trans(entry_part, embed_project)
        pooled_grad = lax.psum_scatter(pooled_part, "dp", scatter_dimension=0, tiled=True)
        pooled_grad = lax.psum_scatter(pooled_grad, "tensor", scatter_dimension=0, tiled=True)

    def summed(part):
        if part.ndim == 2:
            part = part.astype(bfloat)
        part = lax.psum_scatter(part, "dp", scatter_dimension=0, tiled=True)
        return lax.psum_scatter(part, "tensor", scatter_dimension=0, tiled=True).astype(single)

    with jax.named_scope("hyper_bwd"):
        project_grad = summed(project_part)
        pooled_grad = pooled_grad / slot_counts
        grid_grad = jnp.where(valid[:, :, None], pooled_grad[:, None, :], 0.0).reshape(
            flat_rows, HYPER_WIDTH
        )
        reduce_in = grid_grad.astype(bfloat)
        reduce_grad = trans_times(activated_low, reduce_in)
        expand_in = gelu_back(times_trans(reduce_in, encoder_reduce))[0].astype(bfloat)
        expand_grad = trans_times(second_in, expand_in)
        resid_part, normtwo_grad = norm_back_two(times_trans(expand_in, encoder_expand))
        resid_one_grad = grid_grad + resid_part
        merge_in = resid_one_grad.astype(bfloat)
        merge_grad = trans_times(enc_mixed, merge_in)
        enc_mixed_grad = (
            times_trans(merge_in, encoder_merge)
            .astype(bfloat)
            .reshape(entries, SUBWORD_SLOTS, EH, EHD)
        )
        enc_prob_grad = jnp.einsum(
            "nqhd,nkhd->nhqk", enc_mixed_grad, enc_values, preferred_element_type=single
        )
        enc_delta = jnp.sum(enc_probs * enc_prob_grad, axis=-1, keepdims=True)
        enc_score_grad = (enc_probs * (enc_prob_grad - enc_delta)).astype(bfloat)
        enc_query_grad = (
            jnp.einsum("nhqk,nkhd->nqhd", enc_score_grad, enc_keys, preferred_element_type=single)
            * enc_scale
        )
        enc_key_grad = (
            jnp.einsum(
                "nhqk,nqhd->nkhd", enc_score_grad, enc_queries, preferred_element_type=single
            )
            * enc_scale
        )
        enc_value_grad = jnp.einsum(
            "nhqk,nqhd->nkhd", enc_probs_low, enc_mixed_grad, preferred_element_type=single
        )
        triple_in = jnp.concatenate(
            [
                enc_query_grad.reshape(flat_rows, HYPER_WIDTH),
                enc_key_grad.reshape(flat_rows, HYPER_WIDTH),
                enc_value_grad.reshape(flat_rows, HYPER_WIDTH),
            ],
            axis=1,
        ).astype(bfloat)
        triple_grad = trans_times(first_in, triple_in)
        rows_part, normone_grad = norm_back_one(times_trans(triple_in, encoder_triple))
        rows_low = (resid_one_grad + rows_part).astype(bfloat)

    with jax.named_scope("grads_out"):
        all_rows = lax.all_gather(rows_low, "tensor", axis=0, tiled=True)
        all_rows = lax.all_gather(all_rows, "dp", axis=0, tiled=True)
        own_rows = table_rows // tensor_size
        row_hot = (
            (jnp.arange(own_rows) + device_at * own_rows)[:, None] == all_ids[None, :]
        ).astype(bfloat)
        subword_grad = matmul(row_hot, all_rows)
        reduce_grad = summed(reduce_grad)
        expand_grad = summed(expand_grad)
        merge_grad = summed(merge_grad)
        triple_grad = summed(triple_grad)
        gain_grads = summed(jnp.stack([normone_grad, normtwo_grad], axis=1).reshape(-1))
        gain_grads = gain_grads.reshape(-1, 2)
    return (
        layer_final.astype(bfloat),
        vectors,
        subword_grad,
        triple_grad,
        merge_grad,
        expand_grad,
        reduce_grad,
        project_grad,
        gain_grads[:, 0],
        gain_grads[:, 1],
    )


def solution(mesh):
    return jax.shard_map(
        per_device,
        mesh=mesh,
        in_specs=(
            P("dp", None),
            P(("dp", "tensor"), None),
            P(("dp", "tensor")),
            P(("dp", "tensor")),
            P(),
            P(),
            P(),
            P(),
            P(),
            P(),
            P(),
            P("dp", "tensor"),
            P("dp", "tensor"),
            P("dp", "tensor"),
            P("dp", "tensor"),
            P("dp", "tensor"),
            P("dp", "tensor"),
            P("dp", "tensor"),
            P(),
            P(),
            P(("dp", "tensor")),
            P(("dp", "tensor"), None),
        ),
        out_specs=(
            P(("dp", "tensor"), None),
            P(("dp", "tensor"), None),
            P(("dp", "tensor"), None),
            P(("dp", "tensor"), None),
            P(("dp", "tensor"), None),
            P(("dp", "tensor"), None),
            P(("dp", "tensor"), None),
            P(("dp", "tensor"), None),
            P(("dp", "tensor")),
            P(("dp", "tensor")),
        ),
        check_vma=False,
    )
```

```python
from functools import partial

import jax
import jax.numpy as jnp
from jax import lax
from jax.experimental import pallas as pl
from jax.experimental.pallas import tpu as pltpu
from jax.sharding import PartitionSpec as P

HD = 64
HYPER_WIDTH = 512
EH = 8
EHD = 64
SUBWORD_SLOTS = 8


NEG = -1000000000.0
EPS = 1e-05
THETA = 10000.0
VMEM_LIMIT = 62 * 1024 * 1024


def layer_norm(values, gain):
    center = values - jnp.mean(values, axis=-1, keepdims=True)
    spread = jnp.mean(center * center, axis=-1, keepdims=True)
    return center * lax.rsqrt(spread + EPS) * gain


def rms_norm(values, gain):
    return values * lax.rsqrt(jnp.mean(values * values, axis=-1, keepdims=True) + EPS) * gain


def rope_tables(length, width):
    half_width = width // 2
    inverse = THETA ** (-(2.0 * jnp.arange(half_width, dtype=jnp.float32)) / width)
    angles = jnp.arange(length, dtype=jnp.float32)[:, None] * inverse[None, :]
    return (jnp.cos(angles), jnp.sin(angles))


def rotate(values, cosine, sine):
    half_width = values.shape[-1] // 2
    former = values[..., :half_width]
    latter = values[..., half_width:]
    return jnp.concatenate(
        [former * cosine - latter * sine, latter * cosine + former * sine], axis=-1
    )


def matmul(left, right):
    return jnp.dot(left, right, preferred_element_type=jnp.float32)


def times_trans(left, right):
    return lax.dot_general(
        left, right, (((1,), (1,)), ((), ())), preferred_element_type=jnp.float32
    )


def trans_times(left, right):
    return lax.dot_general(
        left, right, (((0,), (0,)), ((), ())), preferred_element_type=jnp.float32
    )


def ring(values, shift=1):
    size = lax.axis_size("tensor")
    return lax.ppermute(values, "tensor", [(i, (i + shift) % size) for i in range(size)])


def tie(values, *others):
    return lax.optimization_barrier((values, *others))[0]


def tie_all(first, *values):
    return lax.optimization_barrier((*values, first))[:-1]


def in_order(blocks, first):
    size = len(blocks)
    stacked = jnp.stack(blocks)
    return [
        lax.dynamic_index_in_dim(stacked, lax.rem(first - at + size, size), 0, keepdims=False)
        for at in range(size)
    ]


def scatter_dp(values):
    size = lax.axis_size("dp")
    blocks = values.reshape(size, values.shape[0] // size, values.shape[1])
    blocks = lax.all_to_all(blocks, "dp", 0, 0, tiled=True)
    return jnp.sum(blocks.astype(jnp.float32), axis=0)


def from_all(values):
    return [values] + [ring(values, shift) for shift in range(1, lax.axis_size("tensor"))]


def rope_lanes(length):
    cosine, sine = rope_tables(length, HD)
    return (
        jnp.concatenate([cosine] * 4, axis=1),
        jnp.concatenate([-sine, sine, -sine, sine], axis=1),
    )


def swap(values):
    width = values.shape[1]
    lane = lax.broadcasted_iota(jnp.int32, values.shape, 1)
    ahead = pltpu.roll(values, width - HD // 2, 1)
    behind = pltpu.roll(values, HD // 2, 1)
    return jnp.where(lane % HD < HD // 2, ahead, behind)


def attention_operands(query_ref, pair_ref, cos_ref, sin_ref):
    bfloat = jnp.bfloat16
    cosine = cos_ref[...]
    sine = sin_ref[...]
    queries = query_ref[...]
    pair = pair_ref[...]
    queries = (queries * cosine + swap(queries) * sine).astype(bfloat)
    queries = queries * jnp.asarray(HD ** (-0.5), bfloat)
    keys = (pair * cosine + swap(pair) * sine).astype(bfloat)[:, :HD]
    return queries, keys, pair.astype(bfloat)[:, HD:]


def scores_by_key(keys, query_block, first):
    rows = query_block.shape[0]
    own = times_trans(keys[first : first + rows], query_block)
    key_at = lax.broadcasted_iota(jnp.int32, own.shape, 0)
    query_at = lax.broadcasted_iota(jnp.int32, own.shape, 1)
    parts = [jnp.where(query_at >= key_at, own, NEG)]
    if first > 0:
        parts.insert(0, times_trans(keys[:first], query_block))
    largest = parts[0].max(axis=0, keepdims=True)
    for part in parts[1:]:
        largest = jnp.maximum(largest, part.max(axis=0, keepdims=True))
    parts = [jnp.exp(part - largest) for part in parts]
    total = sum(part.sum(axis=0, keepdims=True) for part in parts)
    return parts, 1.0 / total


def attention_kernel(block_rows, query_ref, pair_ref, cos_ref, sin_ref, out_ref):
    queries, keys, values = attention_operands(query_ref, pair_ref, cos_ref, sin_ref)
    for first in range(0, queries.shape[0], block_rows):
        rows = slice(first, first + block_rows)
        heads = []
        for head in range(queries.shape[1] // HD):
            query_block = queries[rows, head * HD : (head + 1) * HD]
            parts, inverse = scores_by_key(keys, query_block, first)
            at = 0
            mixed = None
            for part in parts:
                here = trans_times(
                    values[at : at + part.shape[0]], (part * inverse).astype(jnp.bfloat16)
                )
                mixed = here if mixed is None else mixed + here
                at += part.shape[0]
            heads.append(mixed)
        out_ref[rows, :] = jnp.concatenate(heads, axis=0).T.astype(jnp.bfloat16)


def attention_back_kernel(
    block_rows, query_ref, pair_ref, cos_ref, sin_ref, grad_ref, query_out, pair_out, acc_ref
):
    bfloat = jnp.bfloat16
    queries, keys, values = attention_operands(query_ref, pair_ref, cos_ref, sin_ref)

    @pl.when(pl.program_id(0) == 0)
    def _():
        acc_ref[...] = jnp.zeros_like(acc_ref)

    for first in range(0, queries.shape[0], block_rows):
        rows = slice(first, first + block_rows)
        heads = []
        for head in range(queries.shape[1] // HD):
            lanes = slice(head * HD, (head + 1) * HD)
            query_block = queries[rows, lanes]
            grad_block = grad_ref[rows, lanes]
            parts, inverse = scores_by_key(keys, query_block, first)
            parts = [part * inverse for part in parts]
            at = 0
            prob_grads = []
            delta = 0.0
            for part in parts:
                prob_grad = times_trans(values[at : at + part.shape[0]], grad_block)
                delta = delta + (part * prob_grad).sum(axis=0, keepdims=True)
                prob_grads.append(prob_grad)
                at += part.shape[0]
            at = 0
            query_grad = None
            for part, prob_grad in zip(parts, prob_grads):
                here = slice(at, at + part.shape[0])
                score_grad = (part * (prob_grad - delta)).astype(bfloat)
                key_part = matmul(score_grad, query_block)
                value_part = matmul(part.astype(bfloat), grad_block)
                acc_ref[here, :] += jnp.concatenate([key_part, value_part], axis=1)
                query_part = trans_times(keys[here], score_grad)
                query_grad = query_part if query_grad is None else query_grad + query_part
                at += part.shape[0]
            heads.append(query_grad)
        grad = jnp.concatenate(heads, axis=0).T * HD ** (-0.5)
        grad = grad * cos_ref[rows, :] - swap(grad) * sin_ref[rows, :]
        query_out[rows, :] = grad.astype(bfloat)

    @pl.when(pl.program_id(0) == pl.num_programs(0) - 1)
    def _():
        total = acc_ref[...]
        turned = total * cos_ref[...] - swap(total) * sin_ref[...]
        lane = lax.broadcasted_iota(jnp.int32, total.shape, 1)
        pair_out[...] = jnp.where(lane < HD, turned, total).astype(bfloat)


def attention_specs(length, pairs):
    wide = 2 * HD
    return [
        pl.BlockSpec((length, wide), lambda at: (0, at)),
        pl.BlockSpec((length, wide), lambda at: (0, pairs)),
        pl.BlockSpec((length, wide), lambda at: (0, 0)),
        pl.BlockSpec((length, wide), lambda at: (0, 0)),
    ]


def attention(seq_triple, cosine, sine, query_width):
    length = seq_triple.shape[0]
    pairs = query_width // (2 * HD)
    return pl.pallas_call(
        partial(attention_kernel, min(256, length)),
        grid=(pairs,),
        in_specs=attention_specs(length, pairs),
        out_specs=pl.BlockSpec((length, 2 * HD), lambda at: (0, at)),
        out_shape=jax.ShapeDtypeStruct((length, query_width), jnp.bfloat16),
        compiler_params=pltpu.CompilerParams(vmem_limit_bytes=VMEM_LIMIT),
        name="attention",
    )(seq_triple, seq_triple, cosine, sine)


def attention_back(seq_triple, cosine, sine, mixed_grad):
    length, query_width = mixed_grad.shape
    pairs = query_width // (2 * HD)
    wide = 2 * HD
    return pl.pallas_call(
        partial(attention_back_kernel, min(256, length)),
        grid=(pairs,),
        in_specs=attention_specs(length, pairs)
        + [pl.BlockSpec((length, wide), lambda at: (0, at))],
        out_specs=[
            pl.BlockSpec((length, wide), lambda at: (0, at)),
            pl.BlockSpec((length, wide), lambda at: (0, 0)),
        ],
        out_shape=[
            jax.ShapeDtypeStruct((length, query_width), jnp.bfloat16),
            jax.ShapeDtypeStruct((length, wide), jnp.bfloat16),
        ],
        scratch_shapes=[pltpu.VMEM((length, wide), jnp.float32)],
        compiler_params=pltpu.CompilerParams(vmem_limit_bytes=VMEM_LIMIT),
        name="attention_back",
    )(seq_triple, seq_triple, cosine, sine, mixed_grad)


def mlp_kernel(
    query_width,
    unit_width,
    positions,
    resid_in_ref,
    swiglu_grad_ref,
    cot_ref,
    own_weight_ref,
    gain_ref,
    weights_ref,
    *refs,
):
    bfloat = jnp.bfloat16
    mixed_refs = refs[:positions]
    resid_ref, swiglu_ref, mid_ref, part_ref = refs[positions:]
    output_width = positions * query_width
    resid = resid_in_ref[...].astype(jnp.float32)
    for at, mixed_ref in enumerate(mixed_refs):
        columns = slice(at * query_width, (at + 1) * query_width)
        resid = resid + times_trans(mixed_ref[...], weights_ref[:, columns])
    resid_ref[...] = resid
    gain = gain_ref[...]
    spread = lax.rsqrt(jnp.mean(resid * resid, axis=1, keepdims=True) + EPS)
    normed = resid * spread
    seq_two = (normed * gain).astype(bfloat)
    gate_columns = slice(output_width, output_width + unit_width)
    upward_columns = slice(output_width + unit_width, output_width + 2 * unit_width)
    gate = matmul(seq_two, weights_ref[:, gate_columns])
    upward = matmul(seq_two, weights_ref[:, upward_columns])
    open_gate = jax.nn.sigmoid(gate)
    silu = gate * open_gate
    swiglu_ref[...] = (silu * upward).astype(bfloat)
    swiglu_grad = swiglu_grad_ref[...]
    slope = open_gate * (1.0 + gate * (1.0 - open_gate))
    gate_grad = (swiglu_grad * upward * slope).astype(bfloat)
    upward_grad = (swiglu_grad * silu).astype(bfloat)
    grad = times_trans(gate_grad, weights_ref[:, gate_columns])
    grad = grad + times_trans(upward_grad, weights_ref[:, upward_columns])
    grad = grad * gain
    grad = spread * (grad - normed * jnp.mean(grad * normed, axis=1, keepdims=True))
    grad = grad + own_weight_ref[...] * cot_ref[...].astype(jnp.float32)
    mid_low = grad.astype(bfloat)
    mid_ref[...] = mid_low
    part_ref[...] = matmul(mid_low, weights_ref[:, :output_width]).astype(bfloat)


def mlp(resid_in, swiglu_grad, cot, own_weight, gain, weights, mixed, rows_at, row_total):
    width = resid_in.shape[1]
    unit_width = swiglu_grad.shape[1]
    query_width = mixed[0].shape[1]
    block = min(256, row_total)
    offset = rows_at // block

    def rows_of(columns, shift):
        return pl.BlockSpec((block, columns), lambda at: (at + shift, 0))

    return pl.pallas_call(
        partial(mlp_kernel, query_width, unit_width, len(mixed)),
        grid=(row_total // block,),
        in_specs=[
            rows_of(width, offset),
            rows_of(unit_width, offset),
            rows_of(width, offset),
            rows_of(1, offset),
            pl.BlockSpec((1, width), lambda at: (0, 0)),
            pl.BlockSpec(weights.shape, lambda at: (0, 0), pipeline_mode=pl.Buffered(1)),
        ]
        + [rows_of(query_width, 0)] * len(mixed),
        out_specs=[
            rows_of(width, 0),
            rows_of(unit_width, 0),
            rows_of(width, 0),
            rows_of(query_width * len(mixed), 0),
        ],
        out_shape=[
            jax.ShapeDtypeStruct((row_total, width), jnp.float32),
            jax.ShapeDtypeStruct((row_total, unit_width), jnp.bfloat16),
            jax.ShapeDtypeStruct((row_total, width), jnp.bfloat16),
            jax.ShapeDtypeStruct((row_total, query_width * len(mixed)), jnp.bfloat16),
        ],
        compiler_params=pltpu.CompilerParams(vmem_limit_bytes=VMEM_LIMIT),
        name="mlp",
    )(resid_in, swiglu_grad, cot, own_weight, gain[None, :], weights, *mixed)


def hyper_heads(values):
    blocks = values.shape[0] // min(128, values.shape[0])
    return values.reshape(blocks, -1, EH, EHD).transpose(0, 2, 1, 3)


def hyper_rows(values):
    blocks, heads, rows, width = values.shape
    return values.transpose(0, 2, 1, 3).reshape(blocks * rows, heads * width)


def hyper_forward(rows_in, lengths, encoder_triple, encoder_merge, encoder_expand, encoder_reduce, gains):
    bfloat = jnp.bfloat16
    single = jnp.float32
    entries = lengths.shape[0]
    flat_rows = entries * SUBWORD_SLOTS
    valid = jnp.arange(SUBWORD_SLOTS)[None, :] < lengths[:, None]
    normed_one, norm_back_one = jax.vjp(layer_norm, rows_in, gains[0])
    first_in = normed_one.astype(bfloat)
    triple = matmul(first_in, encoder_triple).astype(bfloat)
    queries = hyper_heads(triple[:, :HYPER_WIDTH])
    keys = hyper_heads(triple[:, HYPER_WIDTH : 2 * HYPER_WIDTH])
    values = hyper_heads(triple[:, 2 * HYPER_WIDTH :])
    blocks, _, block_rows, _ = queries.shape
    scores = jnp.einsum("bhqd,bhkd->bhqk", queries, keys, preferred_element_type=single) * EHD ** (
        -0.5
    )
    at = jnp.arange(block_rows) // SUBWORD_SLOTS
    same = at[:, None] == at[None, :]
    open_slots = same[None] & valid.reshape(blocks, 1, block_rows)
    scores = jnp.where(open_slots[:, None], scores, NEG)
    probs = jax.nn.softmax(scores, axis=-1)
    probs_low = probs.astype(bfloat)
    mixed = jnp.einsum("bhqk,bhkd->bhqd", probs_low, values, preferred_element_type=single)
    mixed = hyper_rows(mixed.astype(bfloat))
    resid_one = rows_in + matmul(mixed, encoder_merge)
    normed_two, norm_back_two = jax.vjp(layer_norm, resid_one, gains[1])
    second_in = normed_two.astype(bfloat)
    expanded = matmul(second_in, encoder_expand)
    activated, gelu_back = jax.vjp(partial(jax.nn.gelu, approximate=False), expanded)
    activated_low = activated.astype(bfloat)

    def pool():
        resid_two = resid_one + matmul(activated_low, encoder_reduce)
        kept = jnp.where(
            valid[:, :, None], resid_two.reshape(entries, SUBWORD_SLOTS, HYPER_WIDTH), 0.0
        )
        return (jnp.sum(kept, axis=1) / lengths.astype(single)[:, None]).astype(bfloat)

    def backward(pooled_grad, share):
        pooled_grad = pooled_grad / lengths.astype(single)[:, None]
        grid_grad = jnp.where(valid[:, :, None], pooled_grad[:, None, :], 0.0).reshape(
            flat_rows, HYPER_WIDTH
        )
        reduce_in = grid_grad.astype(bfloat)
        reduce_grad = trans_times(share(activated_low), reduce_in)
        expand_in = gelu_back(times_trans(reduce_in, encoder_reduce))[0].astype(bfloat)
        expand_grad = trans_times(share(second_in), expand_in)
        resid_part, normtwo_grad = norm_back_two(times_trans(expand_in, encoder_expand))
        resid_one_grad = grid_grad + resid_part
        merge_in = resid_one_grad.astype(bfloat)
        merge_grad = trans_times(share(mixed), merge_in)
        mixed_grad = hyper_heads(times_trans(merge_in, encoder_merge).astype(bfloat))
        prob_grad = jnp.einsum("bhqd,bhkd->bhqk", mixed_grad, values, preferred_element_type=single)
        delta = jnp.sum(probs * prob_grad, axis=-1, keepdims=True)
        score_grad = (probs * (prob_grad - delta)).astype(bfloat)
        scale = EHD ** (-0.5)
        query_grad = (
            jnp.einsum("bhqk,bhkd->bhqd", score_grad, keys, preferred_element_type=single) * scale
        )
        key_grad = (
            jnp.einsum("bhqk,bhqd->bhkd", score_grad, queries, preferred_element_type=single)
            * scale
        )
        value_grad = jnp.einsum(
            "bhqk,bhqd->bhkd", probs_low, mixed_grad, preferred_element_type=single
        )
        triple_in = jnp.concatenate(
            [hyper_rows(grad.astype(bfloat)) for grad in (query_grad, key_grad, value_grad)], axis=1
        )
        triple_grad = trans_times(share(first_in), triple_in)
        rows_part, normone_grad = norm_back_one(times_trans(triple_in, encoder_triple))
        rows_low = (resid_one_grad + rows_part).astype(bfloat)
        return (
            rows_low,
            reduce_grad,
            expand_grad,
            merge_grad,
            triple_grad,
            normone_grad,
            normtwo_grad,
        )

    return pool, backward


def per_device(
    subword_embedding_rows,
    entry_subword_index,
    entry_lengths,
    entry_counts,
    encoder_triple,
    encoder_merge,
    encoder_expand,
    encoder_reduce,
    embed_project,
    normone_gain,
    normtwo_gain,
    frozen_query,
    frozen_key,
    frozen_value,
    frozen_output,
    frozen_gate,
    frozen_upward,
    frozen_downward,
    prenorm_gain,
    midnorm_gain,
    text_tokens,
    cotangent,
):
    bfloat = jnp.bfloat16
    single = jnp.float32
    dp_size = lax.axis_size("dp")
    tensor_size = lax.axis_size("tensor")
    dp_at = lax.axis_index("dp")
    tensor_at = lax.axis_index("tensor")
    device_at = dp_at * tensor_size + tensor_at
    entries = entry_subword_index.shape[0]
    entry_total = entries * dp_size * tensor_size
    flat_rows = entries * SUBWORD_SLOTS
    table_rows = subword_embedding_rows.shape[0]
    model_width = embed_project.shape[1]

    with jax.named_scope("ids"):
        packed = jnp.concatenate(
            [entry_subword_index, entry_counts[:, None], entry_lengths[:, None]], axis=1
        )
        packed_width = packed.shape[1]
        packed_dp = lax.all_gather(packed, "dp", axis=0, tiled=False)
    with jax.named_scope("first_weights"):
        first_weights = jnp.concatenate(
            [frozen_query, frozen_key, frozen_value, frozen_downward], axis=1
        )
        first_weights, cot_sent, output_sent = tie_all(
            packed_dp, first_weights, cotangent, frozen_output
        )
        first_weights = lax.all_gather(first_weights, "dp", axis=0, tiled=True)
        query_width = frozen_query.shape[1]
        key_width = frozen_key.shape[1]
        triple_width = query_width + 2 * key_width
        full_triple = first_weights[:, :triple_width]
        full_downward = first_weights[:, triple_width:]
    with jax.named_scope("output_weights"):
        output_blocks = from_all(output_sent)

    with jax.named_scope("lookup"):
        local_ids = packed_dp[:, :, :SUBWORD_SLOTS].reshape(-1) - dp_at * table_rows
        inside = (local_ids >= 0) & (local_ids < table_rows)
        served = jnp.take(subword_embedding_rows, jnp.clip(local_ids, 0, table_rows - 1), axis=0)
        served = jnp.where(inside[:, None], served, jnp.zeros((), bfloat))
        packed_all = from_all(
            tie(jnp.concatenate([packed_dp.reshape(-1), text_tokens]), served)
        )
        served_all = lax.all_to_all(
            served.reshape(dp_size, flat_rows, HYPER_WIDTH), "dp", 0, 0, tiled=True
        )
        rows_in = jnp.sum(served_all.astype(single), axis=0)
    with jax.named_scope("cot_ring"):
        cot_blocks = [cotangent]
        cot_blocks.append(ring(cot_sent))
        cot_blocks.append(ring(tie(cot_blocks[-1], served)))
    with jax.named_scope("second_weights"):
        second_weights = lax.all_gather(
            jnp.concatenate([*tie(output_blocks, served), frozen_gate, frozen_upward], axis=1),
            "dp",
            axis=0,
            tiled=True,
        )
    with jax.named_scope("hyper_wide"):
        rows_blocks = from_all(rows_in.astype(bfloat))

    encoders = (encoder_triple, encoder_merge, encoder_expand, encoder_reduce)
    gains = (normone_gain, normtwo_gain)
    with jax.named_scope("hyper_fwd"):
        pool, _ = hyper_forward(rows_in, entry_lengths, *encoders, gains)
        pooled_low = pool()
    with jax.named_scope("pooled_gather"):
        pooled_blocks = from_all(pooled_low)
        dp_pooled = jnp.concatenate(in_order(pooled_blocks, tensor_at), axis=0)
        all_pooled = lax.all_gather(dp_pooled, "dp", axis=0, tiled=True)
    with jax.named_scope("cot_ring"):
        cot_blocks.append(ring(tie(cot_blocks[-1], dp_pooled)))

    with jax.named_scope("entry_vectors"):
        all_vectors = matmul(all_pooled, embed_project).astype(bfloat)
        vectors = lax.dynamic_slice_in_dim(all_vectors, device_at * entries, entries, 0)
        packed_all = jnp.stack(in_order(packed_all, tensor_at))
        ids_size = dp_size * entries * packed_width
        packed_ids = packed_all[:, :ids_size].reshape(tensor_size, dp_size, entries, packed_width)
        lengths_wide = lax.dynamic_index_in_dim(packed_ids, dp_at, 1, keepdims=False)
        lengths_wide = lengths_wide[:, :, SUBWORD_SLOTS + 1].reshape(-1)
        packed_ids = packed_ids.transpose(1, 0, 2, 3).reshape(entry_total, packed_width)
        all_ids = packed_ids[:, :SUBWORD_SLOTS].reshape(-1)
        all_weights = (1.0 / jnp.log(1.0 + packed_ids[:, SUBWORD_SLOTS].astype(single))).astype(
            bfloat
        )
        seq_tokens = packed_all[:, ids_size:].reshape(-1)
        length = seq_tokens.shape[0]
        rows_here = text_tokens.shape[0]
        seq_hot = (seq_tokens[:, None] == jnp.arange(entry_total)[None, :]).astype(bfloat)
        seq_weight = matmul(seq_hot, all_weights[:, None])
        all_wide = all_vectors.astype(single)
        entry_normed, entry_norm_back = jax.vjp(
            lambda values: rms_norm(values, prenorm_gain), all_wide
        )
        entry_normed = entry_normed.astype(bfloat)
        entry_triple = matmul(entry_normed, full_triple)
        entry_high = entry_triple.astype(bfloat)
        entry_rest = (entry_triple - entry_high.astype(single)).astype(bfloat)
        seq_triple = matmul(seq_hot, entry_high) + matmul(seq_hot, entry_rest)

    cosine, sine = rope_lanes(length)
    with jax.named_scope("attention_fwd"):
        lm_mixed = attention(seq_triple, cosine, sine, query_width)
        block_rows = min(512, length)
        block_total = length // block_rows
        mixed_parts = [
            [lm_mixed[first : first + block_rows]] for first in range(0, length, block_rows)
        ]
    with jax.named_scope("mixed_ring"):
        mixed_parts[0][0] = tie(mixed_parts[0][0], cot_blocks[-1])
        late_hot, late_cot = tie_all(lm_mixed, seq_hot, cot_blocks)
        for parts in mixed_parts:
            for _ in range(tensor_size - 1):
                parts.append(ring(parts[-1]))
    with jax.named_scope("swiglu_grad"):
        seq_cot = jnp.concatenate(in_order(late_cot, tensor_at), axis=0)
        resid_in = matmul(late_hot, all_vectors).astype(bfloat)
        swiglu_grad = matmul((seq_weight * seq_cot.astype(single)).astype(bfloat), full_downward)
        own_rows_here = jnp.arange(length) // rows_here == tensor_at
        own_weight = jnp.where(own_rows_here[:, None], seq_weight, 0.0)

    with jax.named_scope("mlp"):
        resid_blocks = []
        swiglu_blocks = []
        mid_blocks = []
        mixed_grads = []
        for block_idx, parts in enumerate(mixed_parts):
            resid_mid, swiglu_low, mid_low, mixed_part = mlp(
                resid_in,
                swiglu_grad,
                seq_cot,
                own_weight,
                midnorm_gain,
                second_weights,
                parts,
                block_idx * block_rows,
                block_rows,
            )
            resid_blocks.append(resid_mid)
            swiglu_blocks.append(swiglu_low)
            mid_blocks.append(mid_low)
            carried = None
            for step in [*range(1, tensor_size), 0]:
                part = mixed_part[:, step * query_width : (step + 1) * query_width]
                if carried is not None:
                    part = (part.astype(single) + carried.astype(single)).astype(bfloat)
                if step > 0:
                    carried = ring(part)
            mixed_grads.append(part)

    with jax.named_scope("hyper_wide"):
        rows_wide = jnp.concatenate(in_order(rows_blocks, tensor_at), axis=0).astype(single)
        rows_wide = tie(rows_wide, mixed_parts[-1][0])
        _, hyper_backward = hyper_forward(rows_wide, lengths_wide, *encoders, gains)

    with jax.named_scope("layer_out"):
        layer_part = times_trans(jnp.concatenate(swiglu_blocks, axis=0), full_downward)
        layer_part, mixed_grads = lax.optimization_barrier((layer_part.astype(bfloat), mixed_grads))
        blocks_of = [
            lax.dynamic_slice_in_dim(
                block, lax.rem(tensor_at * rows_here, block_rows), rows_here, 0
            )
            for block in resid_blocks
        ]
        resid_own = blocks_of[0]
        for block_idx in range(1, block_total):
            resid_own = jnp.where(
                tensor_at * rows_here // block_rows == block_idx, blocks_of[block_idx], resid_own
            )
        layer_final = resid_own + lax.psum_scatter(
            layer_part, "tensor", scatter_dimension=0, tiled=True
        ).astype(single)
    with jax.named_scope("attention_bwd"):
        query_out, pair_out = attention_back(
            seq_triple, cosine, sine, jnp.concatenate(mixed_grads, axis=0)
        )
        triple_out = jnp.concatenate([query_out, pair_out], axis=1)

    with jax.named_scope("entry_bwd"):
        entry_out = trans_times(seq_hot, triple_out).astype(bfloat)
        entry_part = entry_norm_back(times_trans(entry_out, full_triple))[0]
        entry_part = entry_part + trans_times(seq_hot, jnp.concatenate(mid_blocks, axis=0))
        entry_part = entry_part.astype(bfloat)
        pooled_part = times_trans(entry_part, embed_project).astype(bfloat)
        pooled_part = tie(pooled_part, layer_final)
        pooled_part = scatter_dp(pooled_part).astype(bfloat)
        pooled_grad = sum(block.astype(single) for block in from_all(pooled_part))
        project_part = trans_times(all_pooled, tie(entry_part, pooled_part)).astype(bfloat)

    def share(values):
        rows, width = values.shape
        split = values.reshape(rows, dp_size, tensor_size, width // (dp_size * tensor_size))
        return lax.dynamic_index_in_dim(split, tensor_at, 2, keepdims=False).reshape(
            rows, width // tensor_size
        )

    with jax.named_scope("hyper_bwd"):
        project_grad = lax.psum_scatter(project_part, "dp", scatter_dimension=0, tiled=True)
        rows_low, reduce_grad, expand_grad, merge_grad, triple_grad, normone_grad, normtwo_grad = (
            hyper_backward(pooled_grad, share)
        )

    with jax.named_scope("grads_out"):
        all_rows = lax.all_gather(rows_low, "dp", axis=0, tiled=True)
        project_grad = tie(project_grad, rows_low)
        project_grad = project_grad.reshape(tensor_size, -1, model_width)
        project_grad = lax.all_to_all(project_grad, "tensor", 0, 0, tiled=True)
        project_grad = jnp.sum(project_grad.astype(single), axis=0)
        own_rows = table_rows // tensor_size
        row_hot = (
            (jnp.arange(own_rows) + device_at * own_rows)[:, None] == all_ids[None, :]
        ).astype(bfloat)
        subword_grad = matmul(row_hot, all_rows)

        depth = HYPER_WIDTH // (dp_size * tensor_size)
        deep = reduce_grad.shape[0] // dp_size // depth
        reduce_grad = reduce_grad.astype(bfloat).reshape(dp_size, deep, depth, HYPER_WIDTH)
        early = [reduce_grad[:, at] for at in range(deep)]
        early += [
            part.astype(bfloat).reshape(dp_size, depth, -1) for part in (expand_grad, merge_grad)
        ]
        early = jnp.concatenate(early, axis=2).reshape(dp_size * depth, -1)
        early = scatter_dp(early)
        gain_grads = share(jnp.stack([normone_grad, normtwo_grad])).transpose(1, 0)
        late = jnp.concatenate([triple_grad, jnp.pad(gain_grads, ((0, 0), (0, 126)))], axis=1)
        late = scatter_dp(late.astype(bfloat))
        reduce_width = deep * HYPER_WIDTH
        expand_width = expand_grad.shape[1]
        reduce_grad = early[:, :reduce_width].reshape(depth, deep, HYPER_WIDTH)
        reduce_grad = reduce_grad.transpose(1, 0, 2).reshape(deep * depth, HYPER_WIDTH)
        expand_grad = early[:, reduce_width : reduce_width + expand_width]
        merge_grad = early[:, reduce_width + expand_width :]
        grad_width = triple_grad.shape[1]
    return (
        layer_final.astype(bfloat),
        vectors,
        subword_grad,
        late[:, :grad_width],
        merge_grad,
        expand_grad,
        reduce_grad,
        project_grad,
        late[:, grad_width],
        late[:, grad_width + 1],
    )


def solution(mesh):
    return jax.shard_map(
        per_device,
        mesh=mesh,
        in_specs=(
            P("dp", None),
            P(("dp", "tensor"), None),
            P(("dp", "tensor")),
            P(("dp", "tensor")),
            P(),
            P(),
            P(),
            P(),
            P(),
            P(),
            P(),
            P("dp", "tensor"),
            P("dp", "tensor"),
            P("dp", "tensor"),
            P("dp", "tensor"),
            P("dp", "tensor"),
            P("dp", "tensor"),
            P("dp", "tensor"),
            P(),
            P(),
            P(("dp", "tensor")),
            P(("dp", "tensor"), None),
        ),
        out_specs=(
            P(("dp", "tensor"), None),
            P(("dp", "tensor"), None),
            P(("dp", "tensor"), None),
            P(("dp", "tensor"), None),
            P(("dp", "tensor"), None),
            P(("dp", "tensor"), None),
            P(("dp", "tensor"), None),
            P(("dp", "tensor"), None),
            P(("dp", "tensor")),
            P(("dp", "tensor")),
        ),
        check_vma=False,
    )
```

```python
import math
from functools import partial

import jax
import jax.numpy as jnp
from jax import lax
from jax.experimental import pallas as pl
from jax.experimental.pallas import tpu as pltpu
from jax.sharding import PartitionSpec as P

HD = 64
HYPER_WIDTH = 512
EH = 8
EHD = 64
SUBWORD_SLOTS = 8


NEG = -1000000000.0
EPS = 1e-05
THETA = 10000.0
VMEM_LIMIT = 62 * 1024 * 1024


def layer_norm(values, gain):
    center = values - jnp.mean(values, axis=-1, keepdims=True)
    spread = jnp.mean(center * center, axis=-1, keepdims=True)
    return center * lax.rsqrt(spread + EPS) * gain


def rms_norm(values, gain):
    return values * lax.rsqrt(jnp.mean(values * values, axis=-1, keepdims=True) + EPS) * gain


def rope_tables(length, width):
    half_width = width // 2
    inverse = THETA ** (-(2.0 * jnp.arange(half_width, dtype=jnp.float32)) / width)
    angles = jnp.arange(length, dtype=jnp.float32)[:, None] * inverse[None, :]
    return (jnp.cos(angles), jnp.sin(angles))


def rotate(values, cosine, sine):
    half_width = values.shape[-1] // 2
    former = values[..., :half_width]
    latter = values[..., half_width:]
    return jnp.concatenate(
        [former * cosine - latter * sine, latter * cosine + former * sine], axis=-1
    )


def matmul(left, right):
    return jnp.dot(left, right, preferred_element_type=jnp.float32)


def times_trans(left, right):
    return lax.dot_general(
        left, right, (((1,), (1,)), ((), ())), preferred_element_type=jnp.float32
    )


def trans_times(left, right):
    return lax.dot_general(
        left, right, (((0,), (0,)), ((), ())), preferred_element_type=jnp.float32
    )


def ring(values, shift=1):
    size = lax.axis_size("tensor")
    return lax.ppermute(values, "tensor", [(i, (i + shift) % size) for i in range(size)])


def tie(values, *others):
    return lax.optimization_barrier((values, *others))[0]


def tie_all(first, *values):
    return lax.optimization_barrier((*values, first))[:-1]


def in_order(blocks, first):
    size = len(blocks)
    stacked = jnp.stack(blocks)
    return [
        lax.dynamic_index_in_dim(stacked, lax.rem(first - at + size, size), 0, keepdims=False)
        for at in range(size)
    ]


def scatter_dp(values):
    size = lax.axis_size("dp")
    blocks = values.reshape(size, values.shape[0] // size, values.shape[1])
    blocks = lax.all_to_all(blocks, "dp", 0, 0, tiled=True)
    return jnp.sum(blocks.astype(jnp.float32), axis=0)


def from_all(values):
    return [values] + [ring(values, shift) for shift in range(1, lax.axis_size("tensor"))]


def cost(multiplies, values, transcendentals=0):
    return pl.CostEstimate(
        flops=2 * multiplies, bytes_accessed=values, transcendentals=transcendentals
    )


def rope_lanes(length):
    cosine, sine = rope_tables(length, HD)
    return (
        jnp.concatenate([cosine] * 4, axis=1),
        jnp.concatenate([-sine, sine, -sine, sine], axis=1),
    )


def swap(values):
    width = values.shape[1]
    lane = lax.broadcasted_iota(jnp.int32, values.shape, 1)
    ahead = pltpu.roll(values, width - HD // 2, 1)
    behind = pltpu.roll(values, HD // 2, 1)
    return jnp.where(lane % HD < HD // 2, ahead, behind)


def attention_operands(query_ref, pair_ref, cos_ref, sin_ref):
    bfloat = jnp.bfloat16
    cosine = cos_ref[...]
    sine = sin_ref[...]
    queries = query_ref[...]
    pair = pair_ref[...]
    queries = (queries * cosine + swap(queries) * sine).astype(bfloat)
    queries = queries * jnp.asarray(HD ** (-0.5), bfloat)
    keys = (pair * cosine + swap(pair) * sine).astype(bfloat)[:, :HD]
    return queries, keys, pair.astype(bfloat)[:, HD:]


def scores_by_key(keys, query_block, first):
    rows = query_block.shape[0]
    own = times_trans(keys[first : first + rows], query_block)
    key_at = lax.broadcasted_iota(jnp.int32, own.shape, 0)
    query_at = lax.broadcasted_iota(jnp.int32, own.shape, 1)
    parts = [jnp.where(query_at >= key_at, own, NEG)]
    if first > 0:
        parts.insert(0, times_trans(keys[:first], query_block))
    largest = parts[0].max(axis=0, keepdims=True)
    for part in parts[1:]:
        largest = jnp.maximum(largest, part.max(axis=0, keepdims=True))
    parts = [jnp.exp(part - largest) for part in parts]
    total = sum(part.sum(axis=0, keepdims=True) for part in parts)
    return parts, 1.0 / total


def attention_kernel(block_rows, base, query_ref, pair_ref, cos_ref, sin_ref, out_ref):
    queries, keys, values = attention_operands(query_ref, pair_ref, cos_ref, sin_ref)
    for first in range(base, queries.shape[0], block_rows):
        rows = slice(first, first + block_rows)
        heads = []
        for head in range(queries.shape[1] // HD):
            query_block = queries[rows, head * HD : (head + 1) * HD]
            parts, inverse = scores_by_key(keys, query_block, first)
            at = 0
            mixed = None
            for part in parts:
                here = trans_times(
                    values[at : at + part.shape[0]], (part * inverse).astype(jnp.bfloat16)
                )
                mixed = here if mixed is None else mixed + here
                at += part.shape[0]
            heads.append(mixed)
        out_rows = slice(first - base, first - base + block_rows)
        out_ref[out_rows, :] = jnp.concatenate(heads, axis=0).T.astype(jnp.bfloat16)


def attention_back_kernel(
    block_rows, base, query_ref, pair_ref, cos_ref, sin_ref, grad_ref, add_ref, query_out, pair_out, acc_ref
):
    bfloat = jnp.bfloat16
    queries, keys, values = attention_operands(query_ref, pair_ref, cos_ref, sin_ref)

    @pl.when(pl.program_id(0) == 0)
    def _():
        acc_ref[...] = jnp.zeros_like(acc_ref) if add_ref is None else add_ref[...]

    for first in range(base, queries.shape[0], block_rows):
        rows = slice(first, first + block_rows)
        out_rows = slice(first - base, first - base + block_rows)
        heads = []
        for head in range(queries.shape[1] // HD):
            lanes = slice(head * HD, (head + 1) * HD)
            query_block = queries[rows, lanes]
            grad_block = grad_ref[out_rows, lanes]
            parts, inverse = scores_by_key(keys, query_block, first)
            parts = [part * inverse for part in parts]
            at = 0
            prob_grads = []
            delta = 0.0
            for part in parts:
                prob_grad = times_trans(values[at : at + part.shape[0]], grad_block)
                delta = delta + (part * prob_grad).sum(axis=0, keepdims=True)
                prob_grads.append(prob_grad)
                at += part.shape[0]
            at = 0
            query_grad = None
            for part, prob_grad in zip(parts, prob_grads):
                here = slice(at, at + part.shape[0])
                score_grad = (part * (prob_grad - delta)).astype(bfloat)
                key_part = matmul(score_grad, query_block)
                value_part = matmul(part.astype(bfloat), grad_block)
                acc_ref[here, :] += jnp.concatenate([key_part, value_part], axis=1)
                query_part = trans_times(keys[here], score_grad)
                query_grad = query_part if query_grad is None else query_grad + query_part
                at += part.shape[0]
            heads.append(query_grad)
        grad = jnp.concatenate(heads, axis=0).T * HD ** (-0.5)
        grad = grad * cos_ref[rows, :] - swap(grad) * sin_ref[rows, :]
        query_out[out_rows, :] = grad.astype(bfloat)

    @pl.when(pl.program_id(0) == pl.num_programs(0) - 1)
    def _():
        total = acc_ref[...]
        if pair_out.dtype == jnp.float32:
            pair_out[...] = jnp.zeros_like(pair_out)
            pair_out[: total.shape[0], :] = total
            return
        turned = total * cos_ref[...] - swap(total) * sin_ref[...]
        lane = lax.broadcasted_iota(jnp.int32, total.shape, 1)
        pair_out[...] = jnp.where(lane < HD, turned, total).astype(bfloat)


def attention(seq_triple, cosine, sine, query_width, base, rows):
    pairs = query_width // (2 * HD)
    wide = 2 * HD
    keys = base + rows
    return pl.pallas_call(
        partial(attention_kernel, min(256, rows), base),
        grid=(pairs,),
        in_specs=[
            pl.BlockSpec((keys, wide), lambda at: (0, at)),
            pl.BlockSpec((keys, wide), lambda at: (0, pairs)),
            pl.BlockSpec((keys, wide), lambda at: (0, 0)),
            pl.BlockSpec((keys, wide), lambda at: (0, 0)),
        ],
        out_specs=pl.BlockSpec((rows, wide), lambda at: (0, at)),
        out_shape=jax.ShapeDtypeStruct((rows, query_width), jnp.bfloat16),
        cost_estimate=cost(
            8 * query_width * rows * keys, 6 * query_width * keys, query_width * keys * 10
        ),
        compiler_params=pltpu.CompilerParams(vmem_limit_bytes=VMEM_LIMIT),
        name="attention",
    )(seq_triple, seq_triple, cosine, sine)


def attention_back(seq_triple, cosine, sine, mixed_grad, base, before):
    length = seq_triple.shape[0]
    rows, query_width = mixed_grad.shape
    pairs = query_width // (2 * HD)
    wide = 2 * HD
    keys = base + rows
    last = keys == length
    specs = [
        pl.BlockSpec((keys, wide), lambda at: (0, at)),
        pl.BlockSpec((keys, wide), lambda at: (0, pairs)),
        pl.BlockSpec((keys, wide), lambda at: (0, 0)),
        pl.BlockSpec((keys, wide), lambda at: (0, 0)),
        pl.BlockSpec((rows, wide), lambda at: (0, at)),
    ]
    operands = [seq_triple, seq_triple, cosine, sine, mixed_grad]
    if before is not None:
        specs.append(pl.BlockSpec((keys, wide), lambda at: (0, 0)))
        operands.append(before)

    def kernel(*refs):
        given = refs[: len(operands)]
        add_ref = None if before is None else given[-1]
        attention_back_kernel(
            min(256, rows), base, *given[:5], add_ref, *refs[len(operands) :]
        )

    return pl.pallas_call(
        kernel,
        grid=(pairs,),
        in_specs=specs,
        out_specs=[
            pl.BlockSpec((rows, wide), lambda at: (0, at)),
            pl.BlockSpec((length, wide), lambda at: (0, 0)),
        ],
        out_shape=[
            jax.ShapeDtypeStruct((rows, query_width), jnp.bfloat16),
            jax.ShapeDtypeStruct((length, wide), jnp.bfloat16 if last else jnp.float32),
        ],
        cost_estimate=cost(
            20 * query_width * rows * keys, 8 * query_width * length, query_width * keys * 10
        ),
        scratch_shapes=[pltpu.VMEM((keys, wide), jnp.float32)],
        compiler_params=pltpu.CompilerParams(vmem_limit_bytes=VMEM_LIMIT),
        name="attention_back",
    )(*operands)


def unit_scale(values):
    spread = lax.rsqrt(jnp.mean(values * values, axis=1, keepdims=True) + EPS)
    return values * spread, spread


def one_hot(places, first, shape, axis):
    at = lax.broadcasted_iota(jnp.int32, shape, axis) + first
    return jnp.where(places == at, 1.0, 0.0).astype(jnp.bfloat16)


def entry_kernel(
    tokens_ref, pooled_ref, project_ref, gain_ref, triple_w_ref, vectors_ref, seq_ref
):
    bfloat = jnp.bfloat16
    step = pl.program_id(0)
    vectors = matmul(pooled_ref[...], project_ref[...]).astype(bfloat)
    vectors_ref[...] = vectors
    normed, _ = unit_scale(vectors.astype(jnp.float32))
    triple = matmul((normed * gain_ref[...]).astype(bfloat), triple_w_ref[...])
    high = triple.astype(bfloat)
    rest = (triple - high.astype(jnp.float32)).astype(bfloat)
    count = vectors.shape[0]
    hot = one_hot(tokens_ref[...], step * count, (seq_ref.shape[0], count), 1)
    picked = matmul(hot, high) + matmul(hot, rest)

    @pl.when(step == 0)
    def _():
        seq_ref[...] = picked

    @pl.when(step > 0)
    def _():
        seq_ref[...] += picked


def entry(tokens, pooled, project, gain, weights, triple_width):
    total, inner = pooled.shape
    length = tokens.shape[0]
    width = project.shape[1]
    block = min(512, total)

    def whole(shape):
        return pl.BlockSpec(shape, lambda at: (0, 0), pipeline_mode=pl.Buffered(1))

    return pl.pallas_call(
        entry_kernel,
        grid=(total // block,),
        in_specs=[
            whole((length, 1)),
            pl.BlockSpec((block, inner), lambda at: (at, 0)),
            whole(project.shape),
            whole((1, width)),
            whole((width, triple_width)),
        ],
        out_specs=[
            pl.BlockSpec((block, width), lambda at: (at, 0)),
            pl.BlockSpec((length, triple_width), lambda at: (0, 0)),
        ],
        out_shape=[
            jax.ShapeDtypeStruct((total, width), jnp.bfloat16),
            jax.ShapeDtypeStruct((length, triple_width), jnp.float32),
        ],
        cost_estimate=cost(
            total * width * (inner + triple_width) + 2 * length * total * triple_width,
            4 * width * (inner + triple_width),
        ),
        compiler_params=pltpu.CompilerParams(vmem_limit_bytes=VMEM_LIMIT),
        name="entry",
    )(tokens[:, None], pooled, project, gain[None, :], weights)


def entry_back_kernel(
    tokens_ref,
    vectors_ref,
    gain_ref,
    triple_w_ref,
    mid_ref,
    project_ref,
    pair_ref,
    *refs,
):
    bfloat = jnp.bfloat16
    query_refs = refs[:-2]
    entry_ref, pooled_ref = refs[-2:]
    count = vectors_ref.shape[0]
    length = tokens_ref.shape[1]
    hot = one_hot(tokens_ref[...], pl.program_id(0) * count, (count, length), 0)
    at = 0
    query_out = None
    for ref in query_refs:
        here = matmul(hot[:, at : at + ref.shape[0]], ref[...])
        query_out = here if query_out is None else query_out + here
        at += ref.shape[0]
    pair_out = matmul(hot, pair_ref[...])
    query_width = query_out.shape[1]
    grad = times_trans(query_out.astype(bfloat), triple_w_ref[:, :query_width])
    grad = grad + times_trans(pair_out.astype(bfloat), triple_w_ref[:, query_width:])
    grad = grad * gain_ref[...]
    normed, spread = unit_scale(vectors_ref[...].astype(jnp.float32))
    grad = spread * (grad - normed * jnp.mean(grad * normed, axis=1, keepdims=True))
    entry_grad = (grad + mid_ref[...]).astype(bfloat)
    entry_ref[...] = entry_grad
    pooled_ref[...] = times_trans(entry_grad, project_ref[...]).astype(bfloat)


def entry_back(tokens, vectors, gain, weights, mid_entries, project, pair_out, query_parts):
    total, width = vectors.shape
    length = tokens.shape[0]
    block = min(256, total)
    triple_width = query_parts[0].shape[1] + pair_out.shape[1]
    inner = project.shape[0]

    def whole(shape):
        return pl.BlockSpec(shape, lambda at: (0, 0), pipeline_mode=pl.Buffered(1))

    def rows_of(columns):
        return pl.BlockSpec((block, columns), lambda at: (at, 0))

    return pl.pallas_call(
        entry_back_kernel,
        grid=(total // block,),
        in_specs=[
            whole((1, length)),
            rows_of(width),
            whole((1, width)),
            whole((width, triple_width)),
            rows_of(width),
            whole(project.shape),
            whole(pair_out.shape),
        ]
        + [whole(part.shape) for part in query_parts],
        out_specs=[rows_of(width), rows_of(inner)],
        out_shape=[
            jax.ShapeDtypeStruct((total, width), jnp.bfloat16),
            jax.ShapeDtypeStruct((total, inner), jnp.bfloat16),
        ],
        cost_estimate=cost(
            total * (length * triple_width + width * (inner + triple_width)),
            4 * width * (inner + triple_width) + 8 * total * width,
        ),
        compiler_params=pltpu.CompilerParams(vmem_limit_bytes=VMEM_LIMIT),
        name="entry_back",
    )(tokens[None, :], vectors, gain[None, :], weights, mid_entries, project, pair_out, *query_parts)


def mlp_kernel(
    query_width,
    unit_width,
    positions,
    places_ref,
    resid_in_ref,
    swiglu_grad_ref,
    cot_ref,
    own_weight_ref,
    gain_ref,
    output_from,
    units_from,
    *refs,
):
    bfloat = jnp.bfloat16
    mixed_refs = refs[:positions]
    resid_ref, swiglu_ref, mid_ref, part_ref, output_ref, units_ref, arrived = refs[positions:]
    gate_columns = pl.ds(0, unit_width)
    upward_columns = pl.ds(unit_width, unit_width)
    copies = [
        pltpu.make_async_copy(output_from, output_ref, arrived.at[0]),
        pltpu.make_async_copy(
            units_from.at[:, gate_columns], units_ref.at[:, gate_columns], arrived.at[1]
        ),
        pltpu.make_async_copy(
            units_from.at[:, upward_columns], units_ref.at[:, upward_columns], arrived.at[2]
        ),
    ]

    def on_first(act):
        pl.when(pl.program_id(0) == 0)(act)

    @on_first
    def _():
        for copy in copies:
            copy.start()
        copies[0].wait()

    resid = resid_in_ref[...].astype(jnp.float32)
    for at, mixed_ref in enumerate(mixed_refs):
        columns = slice(at * query_width, (at + 1) * query_width)
        resid = resid + times_trans(mixed_ref[...], output_ref[:, columns])
    resid_ref[...] = resid
    gain = gain_ref[...]
    spread = lax.rsqrt(jnp.mean(resid * resid, axis=1, keepdims=True) + EPS)
    normed = resid * spread
    seq_two = (normed * gain).astype(bfloat)
    on_first(copies[1].wait)
    gate = matmul(seq_two, units_ref[:, gate_columns])
    on_first(copies[2].wait)
    upward = matmul(seq_two, units_ref[:, upward_columns])
    open_gate = jax.nn.sigmoid(gate)
    silu = gate * open_gate
    swiglu_ref[...] = (silu * upward).astype(bfloat)
    swiglu_grad = swiglu_grad_ref[...]
    slope = open_gate * (1.0 + gate * (1.0 - open_gate))
    gate_grad = (swiglu_grad * upward * slope).astype(bfloat)
    upward_grad = (swiglu_grad * silu).astype(bfloat)
    grad = times_trans(gate_grad, units_ref[:, gate_columns])
    grad = grad + times_trans(upward_grad, units_ref[:, upward_columns])
    grad = grad * gain
    grad = spread * (grad - normed * jnp.mean(grad * normed, axis=1, keepdims=True))
    grad = grad + own_weight_ref[...] * cot_ref[...].astype(jnp.float32)
    mid_low = grad.astype(bfloat)
    mid_ref[...] = mid_low
    for at in range(positions):
        columns = slice(at * query_width, (at + 1) * query_width)
        part_ref[places_ref[at]] = matmul(mid_low, output_ref[:, columns]).astype(bfloat)


def mlp(
    places, resid_in, swiglu_grad, cot, own_weight, gain, output_w, units_w, mixed, rows_at, row_total
):
    width = resid_in.shape[1]
    unit_width = swiglu_grad.shape[1]
    query_width = mixed[0].shape[1]
    block = min(256, row_total)
    offset = rows_at // block

    def rows_of(columns, shift):
        return pl.BlockSpec((block, columns), lambda at: (at + shift, 0))

    return pl.pallas_call(
        partial(mlp_kernel, query_width, unit_width, len(mixed)),
        grid=(row_total // block,),
        in_specs=[
            pl.BlockSpec(memory_space=pltpu.SMEM),
            rows_of(width, offset),
            rows_of(unit_width, offset),
            rows_of(width, offset),
            rows_of(1, offset),
            pl.BlockSpec((1, width), lambda at: (0, 0)),
            pl.BlockSpec(memory_space=pl.ANY),
            pl.BlockSpec(memory_space=pl.ANY),
        ]
        + [rows_of(query_width, 0)] * len(mixed),
        out_specs=[
            rows_of(width, 0),
            rows_of(unit_width, 0),
            rows_of(width, 0),
            pl.BlockSpec((len(mixed), block, query_width), lambda at: (0, at, 0)),
        ],
        out_shape=[
            jax.ShapeDtypeStruct((row_total, width), jnp.float32),
            jax.ShapeDtypeStruct((row_total, unit_width), jnp.bfloat16),
            jax.ShapeDtypeStruct((row_total, width), jnp.bfloat16),
            jax.ShapeDtypeStruct((len(mixed), row_total, query_width), jnp.bfloat16),
        ],
        cost_estimate=cost(
            2 * row_total * (output_w.size + units_w.size),
            2 * (output_w.size + units_w.size) + 16 * row_total * width,
        ),
        scratch_shapes=[
            pltpu.VMEM(output_w.shape, output_w.dtype),
            pltpu.VMEM(units_w.shape, units_w.dtype),
            pltpu.SemaphoreType.DMA((3,)),
        ],
        compiler_params=pltpu.CompilerParams(vmem_limit_bytes=VMEM_LIMIT),
        name="mlp",
    )(places, resid_in, swiglu_grad, cot, own_weight, gain[None, :], output_w, units_w, *mixed)


def centred(values):
    center = values - jnp.mean(values, axis=1, keepdims=True)
    spread = lax.rsqrt(jnp.mean(center * center, axis=1, keepdims=True) + EPS)
    return center * spread, spread


def centred_back(grad, normed, spread):
    return spread * (
        grad
        - jnp.mean(grad, axis=1, keepdims=True)
        - normed * jnp.mean(grad * normed, axis=1, keepdims=True)
    )


def slot_probs(triple_ref, rows, head, shut):
    wide = HYPER_WIDTH
    at = head * EHD
    queries = triple_ref[rows, at : at + EHD]
    keys = triple_ref[rows, wide + at : wide + at + EHD]
    values = triple_ref[rows, 2 * wide + at : 2 * wide + at + EHD]
    scores = jnp.where(shut, NEG, times_trans(keys, queries) * EHD ** (-0.5))
    parts = jnp.exp(scores - scores.max(axis=0, keepdims=True))
    return queries, keys, values, parts * (1.0 / parts.sum(axis=0, keepdims=True))


def slot_shut(open_ref, rows, count):
    key_entry = lax.broadcasted_iota(jnp.int32, (count, count), 0) // SUBWORD_SLOTS
    query_entry = lax.broadcasted_iota(jnp.int32, (count, count), 1) // SUBWORD_SLOTS
    return (key_entry != query_entry) | (open_ref[rows, :] == 0.0)


def hyper_wide_kernel(
    rows_ref,
    open_ref,
    gains_ref,
    triple_w_ref,
    merge_w_ref,
    expand_w_ref,
    reduce_w_ref,
    length_ref,
    first_ref,
    triple_ref,
    mixed_ref,
    resid_ref,
    second_ref,
    active_ref,
    slope_ref,
    pooled_ref,
):
    bfloat = jnp.bfloat16
    rows_in = rows_ref[...].astype(jnp.float32)
    first_in = (centred(rows_in)[0] * gains_ref[0:1, :]).astype(bfloat)
    first_ref[...] = first_in
    triple_ref[...] = matmul(first_in, triple_w_ref[...]).astype(bfloat)
    total = rows_in.shape[0]
    count = min(128, total)
    for first in range(0, total, count):
        rows = slice(first, first + count)
        shut = slot_shut(open_ref, rows, count)
        heads = []
        for head in range(EH):
            _, _, values, probs = slot_probs(triple_ref, rows, head, shut)
            heads.append(trans_times(values, probs.astype(bfloat)))
        mixed_ref[rows, :] = jnp.concatenate(heads, axis=0).T.astype(bfloat)
    resid_one = rows_in + matmul(mixed_ref[...], merge_w_ref[...])
    resid_ref[...] = resid_one
    second_in = (centred(resid_one)[0] * gains_ref[1:2, :]).astype(bfloat)
    second_ref[...] = second_in
    expanded = matmul(second_in, expand_w_ref[...])
    below = 0.5 * (1.0 + lax.erf(expanded * 0.5**0.5))
    active = (expanded * below).astype(bfloat)
    active_ref[...] = active
    resid_two = resid_one + matmul(active, reduce_w_ref[...])
    kept = jnp.where(open_ref[...] == 0.0, 0.0, resid_two)
    pooled = kept.reshape(total // SUBWORD_SLOTS, SUBWORD_SLOTS, kept.shape[1]).sum(axis=1)
    pooled_ref[...] = (pooled / length_ref[...]).astype(bfloat)
    bell = jnp.exp(-0.5 * expanded * expanded) * (2.0 * math.pi) ** (-0.5)
    slope_ref[...] = below + expanded * bell


def hyper_wide(rows_in, open_rows, gains, triple_w, merge_w, expand_w, reduce_w, lengths):
    total, width = rows_in.shape
    block = min(256, total)
    units = expand_w.shape[1]
    bfloat = jnp.bfloat16
    single = jnp.float32

    def rows_of(columns):
        return pl.BlockSpec((block, columns), lambda at: (at, 0))

    def whole(array):
        return pl.BlockSpec(array.shape, lambda at: (0, 0), pipeline_mode=pl.Buffered(1))

    outs = [
        (width, bfloat),
        (3 * width, bfloat),
        (width, bfloat),
        (width, single),
        (width, bfloat),
        (units, bfloat),
        (units, single),
    ]
    return pl.pallas_call(
        hyper_wide_kernel,
        grid=(total // block,),
        in_specs=[rows_of(width), rows_of(1)]
        + [whole(array) for array in (gains, triple_w, merge_w, expand_w, reduce_w)]
        + [pl.BlockSpec((block // SUBWORD_SLOTS, 1), lambda at: (at, 0))],
        out_specs=[rows_of(columns) for columns, _ in outs]
        + [pl.BlockSpec((block // SUBWORD_SLOTS, width), lambda at: (at, 0))],
        out_shape=[jax.ShapeDtypeStruct((total, columns), kind) for columns, kind in outs]
        + [jax.ShapeDtypeStruct((total // SUBWORD_SLOTS, width), bfloat)],
        cost_estimate=cost(16 * total * width * units, 12 * total * units),
        compiler_params=pltpu.CompilerParams(vmem_limit_bytes=VMEM_LIMIT),
        name="hyper_wide",
    )(rows_in, open_rows, gains, triple_w, merge_w, expand_w, reduce_w, lengths)


def hyper_back_units_kernel(
    dp_size,
    pooled_refs,
    scale_ref,
    gains_ref,
    resid_ref,
    slope_ref,
    mixed_share_ref,
    second_share_ref,
    active_share_ref,
    merge_w_ref,
    expand_w_ref,
    reduce_w_ref,
    resid_out,
    mixed_out,
    early_out,
    gains_out,
    reduce_acc,
    expand_acc,
    merge_acc,
):
    bfloat = jnp.bfloat16
    step = pl.program_id(0)
    total, width = resid_ref.shape
    pooled_grad = sum(ref[...].astype(jnp.float32) for ref in pooled_refs)
    grid_grad = jnp.broadcast_to(
        pooled_grad[:, None, :], (total // SUBWORD_SLOTS, SUBWORD_SLOTS, width)
    ).reshape(total, width)
    grid_grad = grid_grad * scale_ref[...]
    reduce_in = grid_grad.astype(bfloat)
    expand_in = times_trans(reduce_in, reduce_w_ref[...]) * slope_ref[...]
    expand_in = expand_in.astype(bfloat)
    second_grad = times_trans(expand_in, expand_w_ref[...])
    normed, spread = centred(resid_ref[...])
    gain_two = (second_grad * normed).sum(axis=0, keepdims=True)
    resid_grad = grid_grad + centred_back(second_grad * gains_ref[1:2, :], normed, spread)
    resid_out[...] = resid_grad
    merge_in = resid_grad.astype(bfloat)
    mixed_out[...] = times_trans(merge_in, merge_w_ref[...]).astype(bfloat)

    @pl.when(step == 0)
    def _():
        for ref in (reduce_acc, expand_acc, merge_acc, gains_out):
            ref[...] = jnp.zeros_like(ref)

    gains_out[0:1, :] += gain_two
    reduce_acc[...] += trans_times(active_share_ref[...], reduce_in)
    expand_acc[...] += trans_times(second_share_ref[...], expand_in)
    merge_acc[...] += trans_times(mixed_share_ref[...], merge_in)

    @pl.when(step == pl.num_programs(0) - 1)
    def _():
        depth = expand_acc.shape[0] // dp_size
        deep = reduce_acc.shape[0] // expand_acc.shape[0]
        reduced = reduce_acc[...].astype(bfloat).reshape(dp_size, deep, depth, width)
        for at in range(deep):
            early_out[:, at * width : (at + 1) * width] = reduced[:, at].reshape(
                dp_size * depth, width
            )
        units = expand_acc.shape[1]
        early_out[:, deep * width : deep * width + units] = expand_acc[...].astype(bfloat)
        early_out[:, deep * width + units :] = merge_acc[...].astype(bfloat)


def hyper_back_slots_kernel(
    resid_grad_ref,
    mixed_grad_ref,
    rows_ref,
    open_ref,
    gains_ref,
    triple_ref,
    first_share_ref,
    triple_w_ref,
    rows_out,
    late_out,
    gains_out,
    triple_acc,
    triple_in,
):
    bfloat = jnp.bfloat16
    step = pl.program_id(0)
    total, width = rows_ref.shape
    count = min(128, total)
    for first in range(0, total, count):
        rows = slice(first, first + count)
        shut = slot_shut(open_ref, rows, count)
        query_grads = []
        for head in range(EH):
            queries, keys, values, probs = slot_probs(triple_ref, rows, head, shut)
            at = head * EHD
            grad = mixed_grad_ref[rows, at : at + EHD]
            prob_grad = times_trans(values, grad)
            delta = (probs * prob_grad).sum(axis=0, keepdims=True)
            score_grad = (probs * (prob_grad - delta)).astype(bfloat)
            query_grads.append(trans_times(keys, score_grad))
            key_grad = matmul(score_grad, queries) * EHD ** (-0.5)
            value_grad = matmul(probs.astype(bfloat), grad)
            triple_in[rows, width + at : width + at + EHD] = key_grad.astype(bfloat)
            triple_in[rows, 2 * width + at : 2 * width + at + EHD] = value_grad.astype(bfloat)
        query_grad = jnp.concatenate(query_grads, axis=0).T * EHD ** (-0.5)
        triple_in[rows, :width] = query_grad.astype(bfloat)
    triple_grad = triple_in[...]
    first_grad = times_trans(triple_grad, triple_w_ref[...])
    normed, spread = centred(rows_ref[...].astype(jnp.float32))
    gain_one = (first_grad * normed).sum(axis=0, keepdims=True)
    rows_grad = resid_grad_ref[...] + centred_back(first_grad * gains_ref[0:1, :], normed, spread)
    rows_out[...] = rows_grad.astype(bfloat)

    @pl.when(step == 0)
    def _():
        triple_acc[...] = jnp.zeros_like(triple_acc)
        gains_out[...] = jnp.zeros_like(gains_out)

    gains_out[0:1, :] += gain_one
    triple_acc[...] += trans_times(first_share_ref[...], triple_grad)

    @pl.when(step == pl.num_programs(0) - 1)
    def _():
        late_out[...] = triple_acc[...].astype(bfloat)


def row_block(columns, rows):
    return pl.BlockSpec((rows, columns), lambda at: (at, 0))


def whole_block(shape):
    return pl.BlockSpec(shape, lambda at: (0, 0), pipeline_mode=pl.Buffered(1))


def hyper_back_units(dp_size, pooled, scale, gains, resid, slope, shares, weights):
    total, width = resid.shape
    block = min(256, total)
    units = slope.shape[1]
    share_width = shares[0].shape[1]
    deep = shares[2].shape[1] // share_width
    bfloat = jnp.bfloat16
    single = jnp.float32

    def kernel(*refs):
        hyper_back_units_kernel(dp_size, refs[: len(pooled)], *refs[len(pooled) :])

    early_width = deep * width + units + width
    return pl.pallas_call(
        kernel,
        grid=(total // block,),
        in_specs=[row_block(width, block // SUBWORD_SLOTS)] * len(pooled)
        + [row_block(1, block), whole_block(gains.shape)]
        + [row_block(width, block), row_block(units, block)]
        + [row_block(array.shape[1], block) for array in shares]
        + [whole_block(array.shape) for array in weights],
        out_specs=[
            row_block(width, block),
            row_block(width, block),
            pl.BlockSpec((share_width, early_width), lambda at: (0, 0)),
            pl.BlockSpec((8, width), lambda at: (0, 0)),
        ],
        out_shape=[
            jax.ShapeDtypeStruct((total, width), single),
            jax.ShapeDtypeStruct((total, width), bfloat),
            jax.ShapeDtypeStruct((share_width, early_width), bfloat),
            jax.ShapeDtypeStruct((8, width), single),
        ],
        scratch_shapes=[
            pltpu.VMEM((deep * share_width, width), single),
            pltpu.VMEM((share_width, units), single),
            pltpu.VMEM((share_width, width), single),
        ],
        cost_estimate=cost(12 * total * width * units, 6 * total * units),
        compiler_params=pltpu.CompilerParams(vmem_limit_bytes=VMEM_LIMIT),
        name="hyper_back_units",
    )(*pooled, scale, gains, resid, slope, *shares, *weights)


def hyper_back_slots(resid_grad, mixed_grad, rows_in, open_rows, gains, triple, first_share, weight):
    total, width = rows_in.shape
    block = min(256, total)
    share_width = first_share.shape[1]
    bfloat = jnp.bfloat16
    single = jnp.float32
    return pl.pallas_call(
        hyper_back_slots_kernel,
        grid=(total // block,),
        in_specs=[row_block(width, block)] * 3
        + [row_block(1, block), whole_block(gains.shape), row_block(3 * width, block)]
        + [row_block(share_width, block), whole_block(weight.shape)],
        out_specs=[
            row_block(width, block),
            pl.BlockSpec((share_width, 3 * width), lambda at: (0, 0)),
            pl.BlockSpec((8, width), lambda at: (0, 0)),
        ],
        out_shape=[
            jax.ShapeDtypeStruct((total, width), bfloat),
            jax.ShapeDtypeStruct((share_width, 3 * width), bfloat),
            jax.ShapeDtypeStruct((8, width), single),
        ],
        scratch_shapes=[
            pltpu.VMEM((share_width, 3 * width), single),
            pltpu.VMEM((block, 3 * width), bfloat),
        ],
        cost_estimate=cost(40 * total * width * width, 8 * total * width),
        compiler_params=pltpu.CompilerParams(vmem_limit_bytes=VMEM_LIMIT),
        name="hyper_back_slots",
    )(resid_grad, mixed_grad, rows_in, open_rows, gains, triple, first_share, weight)


def per_device(
    subword_embedding_rows,
    entry_subword_index,
    entry_lengths,
    entry_counts,
    encoder_triple,
    encoder_merge,
    encoder_expand,
    encoder_reduce,
    embed_project,
    normone_gain,
    normtwo_gain,
    frozen_query,
    frozen_key,
    frozen_value,
    frozen_output,
    frozen_gate,
    frozen_upward,
    frozen_downward,
    prenorm_gain,
    midnorm_gain,
    text_tokens,
    cotangent,
):
    bfloat = jnp.bfloat16
    single = jnp.float32
    dp_size = lax.axis_size("dp")
    tensor_size = lax.axis_size("tensor")
    dp_at = lax.axis_index("dp")
    tensor_at = lax.axis_index("tensor")
    device_at = dp_at * tensor_size + tensor_at
    entries = entry_subword_index.shape[0]
    entry_total = entries * dp_size * tensor_size
    flat_rows = entries * SUBWORD_SLOTS
    table_rows = subword_embedding_rows.shape[0]
    model_width = embed_project.shape[1]

    with jax.named_scope("ids"):
        packed = jnp.concatenate(
            [entry_subword_index, entry_counts[:, None], entry_lengths[:, None]], axis=1
        )
        packed_width = packed.shape[1]
        first_weights = jnp.concatenate(
            [frozen_query, frozen_key, frozen_value, frozen_downward], axis=1
        )
        packed_dp = lax.all_gather(tie(packed, first_weights), "dp", axis=0, tiled=False)
    with jax.named_scope("first_weights"):
        first_weights = lax.all_gather(first_weights, "dp", axis=0, tiled=True)
        query_width = frozen_query.shape[1]
        key_width = frozen_key.shape[1]
        triple_width = query_width + 2 * key_width
        full_triple = first_weights[:, :triple_width]
        full_downward = first_weights[:, triple_width:]
    with jax.named_scope("lookup"):
        local_ids = packed_dp[:, :, :SUBWORD_SLOTS].reshape(-1) - dp_at * table_rows
        inside = (local_ids >= 0) & (local_ids < table_rows)
        served = jnp.take(subword_embedding_rows, jnp.clip(local_ids, 0, table_rows - 1), axis=0)
        served = jnp.where(inside[:, None], served, jnp.zeros((), bfloat))
        served_all = lax.all_to_all(
            served.reshape(dp_size, flat_rows, HYPER_WIDTH), "dp", 0, 0, tiled=True
        )
        rows_in = jnp.sum(served_all.astype(single), axis=0)
    with jax.named_scope("cot_ring"):
        cot_blocks = [cotangent, ring(cotangent)]
        length = text_tokens.shape[0] * tensor_size
        cosine, sine = rope_lanes(length)
        rows_in = lax.optimization_barrier((rows_in, cot_blocks[-1], cosine, sine))
        rows_in, _, cosine, sine = rows_in
        cot_blocks.append(ring(cot_blocks[-1]))
        packed_all = from_all(
            tie(jnp.concatenate([packed_dp.reshape(-1), text_tokens]), cot_blocks[1])
        )
    with jax.named_scope("hyper_wide"):
        rows_blocks = from_all(rows_in.astype(bfloat))
    with jax.named_scope("second_weights"):
        second_weights = jnp.concatenate([frozen_gate, frozen_upward], axis=1)
        second_weights = lax.all_gather(
            tie(second_weights, served), "dp", axis=0, tiled=True
        )
    with jax.named_scope("hyper_wide"):
        rows_wide = jnp.concatenate(in_order(rows_blocks, tensor_at), axis=0)
        rows_wide, cot_blocks[2] = lax.optimization_barrier((rows_wide, cot_blocks[2]))
        packed_all = jnp.stack(in_order(packed_all, tensor_at))
        ids_size = dp_size * entries * packed_width
        packed_ids = packed_all[:, :ids_size].reshape(tensor_size, dp_size, entries, packed_width)
        lengths_wide = lax.dynamic_index_in_dim(packed_ids, dp_at, 1, keepdims=False)
        lengths_wide = lengths_wide[:, :, SUBWORD_SLOTS + 1].reshape(-1)
        valid_wide = jnp.arange(SUBWORD_SLOTS)[None, :] < lengths_wide[:, None]
        valid_wide = valid_wide.astype(single)
        counts_wide = lengths_wide.astype(single)[:, None]
        open_wide = valid_wide.reshape(-1, 1)
        scale_wide = (valid_wide / counts_wide).reshape(-1, 1)
        gain_pair = jnp.stack([normone_gain, normtwo_gain])
        encoders = (encoder_triple, encoder_merge, encoder_expand, encoder_reduce)
        first_in, triple, mixed, resid_one, second_in, activated, slope, dp_pooled = hyper_wide(
            rows_wide, open_wide, gain_pair, *encoders, counts_wide
        )
    with jax.named_scope("cot_ring"):
        cot_blocks.append(ring(cot_blocks[-1]))
        dp_pooled = tie(dp_pooled, cot_blocks[-1])
    with jax.named_scope("output_weights"):
        output_blocks = from_all(tie(frozen_output, dp_pooled))
    with jax.named_scope("pooled_gather"):
        all_pooled = lax.all_gather(dp_pooled, "dp", axis=0, tiled=True)
    with jax.named_scope("entry_vectors"):
        seq_tokens = packed_all[:, ids_size:].reshape(-1)
        all_vectors, seq_triple = entry(
            seq_tokens, all_pooled, embed_project, prenorm_gain, first_weights, triple_width
        )
    with jax.named_scope("output_weights"):
        output_weights = jnp.concatenate(tie(output_blocks, seq_triple), axis=1)
        output_weights = lax.all_gather(
            tie(output_weights, first_weights), "dp", axis=0, tiled=True
        )

    with jax.named_scope("attention_fwd"):
        block_rows = min(512, length)
        block_total = length // block_rows
        mixed_parts = []
        for first in range(0, length, block_rows):
            lm_mixed = attention(seq_triple, cosine, sine, query_width, first, block_rows)
            mixed_parts.append([lm_mixed])
            seq_triple = tie(seq_triple, lm_mixed)
    with jax.named_scope("mixed_ring"):
        late_ids, late_tokens, late_cot = tie_all(lm_mixed, packed_ids, seq_tokens, cot_blocks)
        for parts in mixed_parts:
            for _ in range(tensor_size - 1):
                parts.append(ring(parts[-1]))
    with jax.named_scope("swiglu_grad"):
        vectors = lax.dynamic_slice_in_dim(all_vectors, device_at * entries, entries, 0)
        late_ids = late_ids.transpose(1, 0, 2, 3).reshape(entry_total, packed_width)
        all_ids = late_ids[:, :SUBWORD_SLOTS].reshape(-1)
        all_weights = (1.0 / jnp.log(1.0 + late_ids[:, SUBWORD_SLOTS].astype(single))).astype(
            bfloat
        )
        rows_here = text_tokens.shape[0]
        seq_hot = (late_tokens[:, None] == jnp.arange(entry_total)[None, :]).astype(bfloat)
        seq_weight = matmul(seq_hot, all_weights[:, None])
        seq_cot = jnp.concatenate(in_order(late_cot, tensor_at), axis=0)
        resid_in = matmul(seq_hot, all_vectors).astype(bfloat)
        swiglu_grad = matmul((seq_weight * seq_cot.astype(single)).astype(bfloat), full_downward)
        own_rows_here = jnp.arange(length) // rows_here == tensor_at
        own_weight = jnp.where(own_rows_here[:, None], seq_weight, 0.0)

    def share(values):
        rows, width = values.shape
        split = values.reshape(rows, dp_size, tensor_size, width // (dp_size * tensor_size))
        return lax.dynamic_index_in_dim(split, tensor_at, 2, keepdims=False).reshape(
            rows, width // tensor_size
        )

    shares = [share(array) for array in tie((first_in, mixed, second_in, activated), lm_mixed)]

    with jax.named_scope("mlp"):
        places = lax.rem(tensor_at + tensor_size - jnp.arange(tensor_size), tensor_size)
        resid_blocks = []
        swiglu_blocks = []
        mid_blocks = []
        mixed_grads = []
        for block_idx, parts in enumerate(mixed_parts):
            last = block_idx == block_total - 1
            if block_idx == 0:
                mixed_parts = lax.optimization_barrier(mixed_parts)
                parts = mixed_parts[0]
            else:
                parts = mixed_parts[block_idx]
            if block_idx > 0:
                parts = tie(parts, mixed_part)
            resid_mid, swiglu_low, mid_low, mixed_part = mlp(
                jnp.arange(tensor_size) if last else places,
                resid_in,
                swiglu_grad,
                seq_cot,
                own_weight,
                midnorm_gain,
                output_weights,
                second_weights,
                parts,
                block_idx * block_rows,
                block_rows,
            )
            resid_blocks.append(resid_mid)
            swiglu_blocks.append(swiglu_low)
            mid_blocks.append(mid_low)
            if not last:
                mixed_grads.append(
                    lax.psum_scatter(
                        mixed_part.reshape(-1, query_width),
                        "tensor",
                        scatter_dimension=0,
                        tiled=True,
                    )
                )
                continue
            carried = None
            for step in [*range(1, tensor_size), 0]:
                part = mixed_part[step]
                if carried is not None:
                    part = (part.astype(single) + carried.astype(single)).astype(bfloat)
                if step == 2:
                    mid_entries = trans_times(seq_hot, jnp.concatenate(mid_blocks, axis=0))
                    part, mid_entries = lax.optimization_barrier((part, mid_entries))
                if step == 3:
                    layer_part = times_trans(jnp.concatenate(swiglu_blocks, axis=0), full_downward)
                    part, layer_part = lax.optimization_barrier((part, layer_part.astype(bfloat)))
                if step == 0:
                    pair_out = None
                    query_parts = []
                    for at, mixed_grad in enumerate(mixed_grads):
                        query_part, pair_out = attention_back(
                            seq_triple, cosine, sine, mixed_grad, at * block_rows, pair_out
                        )
                        query_parts.append(query_part)
                    part, pair_out = lax.optimization_barrier((part, pair_out))
                if step > 0:
                    carried = ring(part)
            last_grad = part

    with jax.named_scope("layer_out"):
        layer_part = tie(layer_part, last_grad)
        blocks_of = [
            lax.dynamic_slice_in_dim(
                block, lax.rem(tensor_at * rows_here, block_rows), rows_here, 0
            )
            for block in resid_blocks
        ]
        resid_own = blocks_of[0]
        for block_idx in range(1, block_total):
            resid_own = jnp.where(
                tensor_at * rows_here // block_rows == block_idx, blocks_of[block_idx], resid_own
            )
        layer_final = resid_own + lax.psum_scatter(
            layer_part, "tensor", scatter_dimension=0, tiled=True
        ).astype(single)
    with jax.named_scope("attention_bwd"):
        query_part, pair_out = attention_back(
            seq_triple, cosine, sine, last_grad, length - block_rows, pair_out
        )
        query_parts.append(query_part)

    with jax.named_scope("entry_bwd"):
        entry_part, pooled_part = entry_back(
            seq_tokens,
            all_vectors,
            prenorm_gain,
            first_weights,
            mid_entries,
            embed_project,
            pair_out,
            query_parts,
        )
        pooled_part = scatter_dp(pooled_part).astype(bfloat)
        pooled_grads = from_all(pooled_part)
        project_part = trans_times(all_pooled, entry_part).astype(bfloat)
        project_part = tie(project_part, pooled_part)

    with jax.named_scope("hyper_bwd"):
        project_grad = scatter_dp(project_part).astype(bfloat)
        resid_grad, mixed_grad, early, gain_two = hyper_back_units(
            dp_size,
            pooled_grads,
            scale_wide,
            gain_pair,
            resid_one,
            slope,
            shares[1:],
            encoders[1:],
        )
        resid_grad, early, project_grad = lax.optimization_barrier(
            (resid_grad, early, project_grad)
        )
        early = scatter_dp(early)
        rows_low, late, gain_one = hyper_back_slots(
            resid_grad,
            mixed_grad,
            rows_wide,
            open_wide,
            gain_pair,
            triple,
            shares[0],
            encoder_triple,
        )

    with jax.named_scope("grads_out"):
        rows_low, early = lax.optimization_barrier((rows_low, early))
        all_rows = lax.all_gather(rows_low, "dp", axis=0, tiled=True)
        late, project_grad = tie_all(rows_low, late, project_grad)
        project_grad = project_grad.reshape(tensor_size, -1, model_width)
        project_grad = lax.all_to_all(project_grad, "tensor", 0, 0, tiled=True)
        project_grad = jnp.sum(project_grad.astype(single), axis=0)
        own_rows = table_rows // tensor_size
        row_hot = (
            (jnp.arange(own_rows) + device_at * own_rows)[:, None] == all_ids[None, :]
        ).astype(bfloat)
        subword_grad = matmul(row_hot, all_rows)

        gain_grads = share(jnp.concatenate([gain_one[:1], gain_two[:1]], axis=0)).transpose(1, 0).astype(bfloat)
        late = jnp.concatenate([late, jnp.pad(gain_grads, ((0, 0), (0, 126)))], axis=1)
        late = scatter_dp(late)
        depth = early.shape[0]
        deep = encoder_reduce.shape[0] // HYPER_WIDTH
        reduce_width = deep * HYPER_WIDTH
        expand_width = encoder_expand.shape[1]
        reduce_grad = early[:, :reduce_width].reshape(depth, deep, HYPER_WIDTH)
        reduce_grad = reduce_grad.transpose(1, 0, 2).reshape(deep * depth, HYPER_WIDTH)
        expand_grad = early[:, reduce_width : reduce_width + expand_width]
        merge_grad = early[:, reduce_width + expand_width :]
        grad_width = encoder_triple.shape[1]
    return (
        layer_final.astype(bfloat),
        vectors,
        subword_grad,
        late[:, :grad_width],
        merge_grad,
        expand_grad,
        reduce_grad,
        project_grad,
        late[:, grad_width],
        late[:, grad_width + 1],
    )


def solution(mesh):
    return jax.shard_map(
        per_device,
        mesh=mesh,
        in_specs=(
            P("dp", None),
            P(("dp", "tensor"), None),
            P(("dp", "tensor")),
            P(("dp", "tensor")),
            P(),
            P(),
            P(),
            P(),
            P(),
            P(),
            P(),
            P("dp", "tensor"),
            P("dp", "tensor"),
            P("dp", "tensor"),
            P("dp", "tensor"),
            P("dp", "tensor"),
            P("dp", "tensor"),
            P("dp", "tensor"),
            P(),
            P(),
            P(("dp", "tensor")),
            P(("dp", "tensor"), None),
        ),
        out_specs=(
            P(("dp", "tensor"), None),
            P(("dp", "tensor"), None),
            P(("dp", "tensor"), None),
            P(("dp", "tensor"), None),
            P(("dp", "tensor"), None),
            P(("dp", "tensor"), None),
            P(("dp", "tensor"), None),
            P(("dp", "tensor"), None),
            P(("dp", "tensor")),
            P(("dp", "tensor")),
        ),
        check_vma=False,
    )
```

```python
import math
from functools import partial

import jax
import jax.numpy as jnp
from jax import lax
from jax.experimental import pallas as pl
from jax.experimental.pallas import tpu as pltpu
from jax.sharding import PartitionSpec as P

HD = 64
HYPER_WIDTH = 512
EH = 8
EHD = 64
SUBWORD_SLOTS = 8


NEG = -1000000000.0
EPS = 1e-05
THETA = 10000.0
VMEM_LIMIT = 62 * 1024 * 1024


def layer_norm(values, gain):
    center = values - jnp.mean(values, axis=-1, keepdims=True)
    spread = jnp.mean(center * center, axis=-1, keepdims=True)
    return center * lax.rsqrt(spread + EPS) * gain


def rms_norm(values, gain):
    return values * lax.rsqrt(jnp.mean(values * values, axis=-1, keepdims=True) + EPS) * gain


def rope_tables(length, width):
    half_width = width // 2
    inverse = THETA ** (-(2.0 * jnp.arange(half_width, dtype=jnp.float32)) / width)
    angles = jnp.arange(length, dtype=jnp.float32)[:, None] * inverse[None, :]
    return (jnp.cos(angles), jnp.sin(angles))


def rotate(values, cosine, sine):
    half_width = values.shape[-1] // 2
    former = values[..., :half_width]
    latter = values[..., half_width:]
    return jnp.concatenate(
        [former * cosine - latter * sine, latter * cosine + former * sine], axis=-1
    )


def matmul(left, right):
    return jnp.dot(left, right, preferred_element_type=jnp.float32)


def times_trans(left, right):
    return lax.dot_general(
        left, right, (((1,), (1,)), ((), ())), preferred_element_type=jnp.float32
    )


def trans_times(left, right):
    return lax.dot_general(
        left, right, (((0,), (0,)), ((), ())), preferred_element_type=jnp.float32
    )


def ring(values, shift=1):
    size = lax.axis_size("tensor")
    return lax.ppermute(values, "tensor", [(i, (i + shift) % size) for i in range(size)])


def tie(values, *others):
    return lax.optimization_barrier((values, *others))[0]


def tie_all(first, *values):
    return lax.optimization_barrier((*values, first))[:-1]


def in_order(blocks, first):
    size = len(blocks)
    stacked = jnp.stack(blocks)
    return [
        lax.dynamic_index_in_dim(stacked, lax.rem(first - at + size, size), 0, keepdims=False)
        for at in range(size)
    ]


def to_owners(values):
    size = lax.axis_size("dp")
    blocks = values.reshape(size, values.shape[0] // size, values.shape[1])
    return lax.all_to_all(blocks, "dp", 0, 0, tiled=True)


def scatter_dp(values):
    return jnp.sum(to_owners(values).astype(jnp.float32), axis=0)


def from_all(values):
    return [values] + [ring(values, shift) for shift in range(1, lax.axis_size("tensor"))]


def cost(multiplies, values, transcendentals=0):
    return pl.CostEstimate(
        flops=2 * multiplies, bytes_accessed=values, transcendentals=transcendentals
    )


def rope_lanes(length):
    cosine, sine = rope_tables(length, HD)
    return (
        jnp.concatenate([cosine] * 4, axis=1),
        jnp.concatenate([-sine, sine, -sine, sine], axis=1),
    )


def swap(values):
    width = values.shape[1]
    lane = lax.broadcasted_iota(jnp.int32, values.shape, 1)
    ahead = pltpu.roll(values, width - HD // 2, 1)
    behind = pltpu.roll(values, HD // 2, 1)
    return jnp.where(lane % HD < HD // 2, ahead, behind)


def attention_operands(query_ref, pair_ref, cos_ref, sin_ref):
    bfloat = jnp.bfloat16
    cosine = cos_ref[...]
    sine = sin_ref[...]
    queries = query_ref[...]
    pair = pair_ref[...]
    queries = (queries * cosine + swap(queries) * sine).astype(bfloat)
    queries = queries * jnp.asarray(HD ** (-0.5), bfloat)
    keys = (pair * cosine + swap(pair) * sine).astype(bfloat)[:, :HD]
    return queries, keys, pair.astype(bfloat)[:, HD:]


def scores_by_key(keys, query_block, first):
    rows = query_block.shape[0]
    own = times_trans(keys[first : first + rows], query_block)
    key_at = lax.broadcasted_iota(jnp.int32, own.shape, 0)
    query_at = lax.broadcasted_iota(jnp.int32, own.shape, 1)
    parts = [jnp.where(query_at >= key_at, own, NEG)]
    if first > 0:
        parts.insert(0, times_trans(keys[:first], query_block))
    largest = parts[0].max(axis=0, keepdims=True)
    for part in parts[1:]:
        largest = jnp.maximum(largest, part.max(axis=0, keepdims=True))
    parts = [jnp.exp(part - largest) for part in parts]
    total = sum(part.sum(axis=0, keepdims=True) for part in parts)
    return parts, 1.0 / total


def attention_kernel(block_rows, base, query_ref, pair_ref, cos_ref, sin_ref, out_ref):
    queries, keys, values = attention_operands(query_ref, pair_ref, cos_ref, sin_ref)
    for first in range(base, queries.shape[0], block_rows):
        rows = slice(first, first + block_rows)
        heads = []
        for head in range(queries.shape[1] // HD):
            query_block = queries[rows, head * HD : (head + 1) * HD]
            parts, inverse = scores_by_key(keys, query_block, first)
            at = 0
            mixed = None
            for part in parts:
                here = trans_times(
                    values[at : at + part.shape[0]], (part * inverse).astype(jnp.bfloat16)
                )
                mixed = here if mixed is None else mixed + here
                at += part.shape[0]
            heads.append(mixed)
        out_rows = slice(first - base, first - base + block_rows)
        out_ref[out_rows, :] = jnp.concatenate(heads, axis=0).T.astype(jnp.bfloat16)


def attention_back_kernel(
    block_rows, base, query_ref, pair_ref, cos_ref, sin_ref, grad_ref, add_ref, query_out, pair_out, acc_ref
):
    bfloat = jnp.bfloat16
    queries, keys, values = attention_operands(query_ref, pair_ref, cos_ref, sin_ref)

    @pl.when(pl.program_id(0) == 0)
    def _():
        acc_ref[...] = jnp.zeros_like(acc_ref) if add_ref is None else add_ref[...]

    for first in range(base, queries.shape[0], block_rows):
        rows = slice(first, first + block_rows)
        out_rows = slice(first - base, first - base + block_rows)
        heads = []
        for head in range(queries.shape[1] // HD):
            lanes = slice(head * HD, (head + 1) * HD)
            query_block = queries[rows, lanes]
            grad_block = grad_ref[out_rows, lanes]
            parts, inverse = scores_by_key(keys, query_block, first)
            parts = [part * inverse for part in parts]
            at = 0
            prob_grads = []
            delta = 0.0
            for part in parts:
                prob_grad = times_trans(values[at : at + part.shape[0]], grad_block)
                delta = delta + (part * prob_grad).sum(axis=0, keepdims=True)
                prob_grads.append(prob_grad)
                at += part.shape[0]
            at = 0
            query_grad = None
            for part, prob_grad in zip(parts, prob_grads):
                here = slice(at, at + part.shape[0])
                score_grad = (part * (prob_grad - delta)).astype(bfloat)
                key_part = matmul(score_grad, query_block)
                value_part = matmul(part.astype(bfloat), grad_block)
                acc_ref[here, :] += jnp.concatenate([key_part, value_part], axis=1)
                query_part = trans_times(keys[here], score_grad)
                query_grad = query_part if query_grad is None else query_grad + query_part
                at += part.shape[0]
            heads.append(query_grad)
        grad = jnp.concatenate(heads, axis=0).T * HD ** (-0.5)
        grad = grad * cos_ref[rows, :] - swap(grad) * sin_ref[rows, :]
        query_out[out_rows, :] = grad.astype(bfloat)

    @pl.when(pl.program_id(0) == pl.num_programs(0) - 1)
    def _():
        total = acc_ref[...]
        if pair_out.dtype == jnp.float32:
            pair_out[...] = jnp.zeros_like(pair_out)
            pair_out[: total.shape[0], :] = total
            return
        turned = total * cos_ref[...] - swap(total) * sin_ref[...]
        lane = lax.broadcasted_iota(jnp.int32, total.shape, 1)
        pair_out[...] = jnp.where(lane < HD, turned, total).astype(bfloat)


def attention(seq_triple, cosine, sine, query_width, base, rows):
    pairs = query_width // (2 * HD)
    wide = 2 * HD
    keys = base + rows
    return pl.pallas_call(
        partial(attention_kernel, min(256, rows), base),
        grid=(pairs,),
        in_specs=[
            pl.BlockSpec((keys, wide), lambda at: (0, at)),
            pl.BlockSpec((keys, wide), lambda at: (0, pairs)),
            pl.BlockSpec((keys, wide), lambda at: (0, 0)),
            pl.BlockSpec((keys, wide), lambda at: (0, 0)),
        ],
        out_specs=pl.BlockSpec((rows, wide), lambda at: (0, at)),
        out_shape=jax.ShapeDtypeStruct((rows, query_width), jnp.bfloat16),
        cost_estimate=cost(
            8 * query_width * rows * keys, 6 * query_width * keys, query_width * keys * 10
        ),
        compiler_params=pltpu.CompilerParams(vmem_limit_bytes=VMEM_LIMIT),
        name="attention",
    )(seq_triple, seq_triple, cosine, sine)


def attention_back(seq_triple, cosine, sine, mixed_grad, base, before):
    length = seq_triple.shape[0]
    rows, query_width = mixed_grad.shape
    pairs = query_width // (2 * HD)
    wide = 2 * HD
    keys = base + rows
    last = keys == length
    specs = [
        pl.BlockSpec((keys, wide), lambda at: (0, at)),
        pl.BlockSpec((keys, wide), lambda at: (0, pairs)),
        pl.BlockSpec((keys, wide), lambda at: (0, 0)),
        pl.BlockSpec((keys, wide), lambda at: (0, 0)),
        pl.BlockSpec((rows, wide), lambda at: (0, at)),
    ]
    operands = [seq_triple, seq_triple, cosine, sine, mixed_grad]
    if before is not None:
        specs.append(pl.BlockSpec((keys, wide), lambda at: (0, 0)))
        operands.append(before)

    def kernel(*refs):
        given = refs[: len(operands)]
        add_ref = None if before is None else given[-1]
        attention_back_kernel(
            min(256, rows), base, *given[:5], add_ref, *refs[len(operands) :]
        )

    return pl.pallas_call(
        kernel,
        grid=(pairs,),
        in_specs=specs,
        out_specs=[
            pl.BlockSpec((rows, wide), lambda at: (0, at)),
            pl.BlockSpec((length, wide), lambda at: (0, 0)),
        ],
        out_shape=[
            jax.ShapeDtypeStruct((rows, query_width), jnp.bfloat16),
            jax.ShapeDtypeStruct((length, wide), jnp.bfloat16 if last else jnp.float32),
        ],
        cost_estimate=cost(
            20 * query_width * rows * keys, 8 * query_width * length, query_width * keys * 10
        ),
        scratch_shapes=[pltpu.VMEM((keys, wide), jnp.float32)],
        compiler_params=pltpu.CompilerParams(vmem_limit_bytes=VMEM_LIMIT),
        name="attention_back",
    )(*operands)


def unit_scale(values):
    spread = lax.rsqrt(jnp.mean(values * values, axis=1, keepdims=True) + EPS)
    return values * spread, spread


def one_hot(places, first, shape, axis):
    at = lax.broadcasted_iota(jnp.int32, shape, axis) + first
    return jnp.where(places == at, 1.0, 0.0).astype(jnp.bfloat16)


def entry_kernel(
    tokens_ref, pooled_ref, project_ref, gain_ref, triple_w_ref, vectors_ref, seq_ref
):
    bfloat = jnp.bfloat16
    step = pl.program_id(0)
    vectors = matmul(pooled_ref[...], project_ref[...]).astype(bfloat)
    vectors_ref[...] = vectors
    normed, _ = unit_scale(vectors.astype(jnp.float32))
    triple = matmul((normed * gain_ref[...]).astype(bfloat), triple_w_ref[...])
    high = triple.astype(bfloat)
    rest = (triple - high.astype(jnp.float32)).astype(bfloat)
    count = vectors.shape[0]
    hot = one_hot(tokens_ref[...], step * count, (seq_ref.shape[0], count), 1)
    picked = matmul(hot, high) + matmul(hot, rest)

    @pl.when(step == 0)
    def _():
        seq_ref[...] = picked

    @pl.when(step > 0)
    def _():
        seq_ref[...] += picked


def entry(tokens, pooled, project, gain, weights, triple_width):
    total, inner = pooled.shape
    length = tokens.shape[0]
    width = project.shape[1]
    block = min(512, total)

    def whole(shape):
        return pl.BlockSpec(shape, lambda at: (0, 0), pipeline_mode=pl.Buffered(1))

    return pl.pallas_call(
        entry_kernel,
        grid=(total // block,),
        in_specs=[
            whole((length, 1)),
            pl.BlockSpec((block, inner), lambda at: (at, 0)),
            whole(project.shape),
            whole((1, width)),
            whole((width, triple_width)),
        ],
        out_specs=[
            pl.BlockSpec((block, width), lambda at: (at, 0)),
            pl.BlockSpec((length, triple_width), lambda at: (0, 0)),
        ],
        out_shape=[
            jax.ShapeDtypeStruct((total, width), jnp.bfloat16),
            jax.ShapeDtypeStruct((length, triple_width), jnp.float32),
        ],
        cost_estimate=cost(
            total * width * (inner + triple_width) + 2 * length * total * triple_width,
            4 * width * (inner + triple_width),
        ),
        compiler_params=pltpu.CompilerParams(vmem_limit_bytes=VMEM_LIMIT),
        name="entry",
    )(tokens[:, None], pooled, project, gain[None, :], weights)


def entry_back_kernel(
    tokens_ref,
    vectors_ref,
    gain_ref,
    triple_w_ref,
    project_ref,
    pair_ref,
    *refs,
):
    bfloat = jnp.bfloat16
    half = (len(refs) - 2) // 2
    mid_refs, query_refs = refs[:half], refs[half:-2]
    entry_ref, pooled_ref = refs[-2:]
    count = vectors_ref.shape[0]
    length = tokens_ref.shape[1]
    hot = one_hot(tokens_ref[...], pl.program_id(0) * count, (count, length), 0)
    at = 0
    query_out = None
    for ref in query_refs:
        here = matmul(hot[:, at : at + ref.shape[0]], ref[...])
        query_out = here if query_out is None else query_out + here
        at += ref.shape[0]
    pair_out = matmul(hot, pair_ref[...])
    query_width = query_out.shape[1]
    grad = times_trans(query_out.astype(bfloat), triple_w_ref[:, :query_width])
    grad = grad + times_trans(pair_out.astype(bfloat), triple_w_ref[:, query_width:])
    grad = grad * gain_ref[...]
    normed, spread = unit_scale(vectors_ref[...].astype(jnp.float32))
    grad = spread * (grad - normed * jnp.mean(grad * normed, axis=1, keepdims=True))
    entry_grad = (grad + sum(ref[...] for ref in mid_refs)).astype(bfloat)
    entry_ref[...] = entry_grad
    pooled_ref[...] = times_trans(entry_grad, project_ref[...]).astype(bfloat)


def entry_back(tokens, vectors, gain, weights, project, pair_out, mid_parts, query_parts):
    total, width = vectors.shape
    length = tokens.shape[0]
    block = min(256, total)
    triple_width = query_parts[0].shape[1] + pair_out.shape[1]
    inner = project.shape[0]

    def whole(shape):
        return pl.BlockSpec(shape, lambda at: (0, 0), pipeline_mode=pl.Buffered(1))

    def rows_of(columns):
        return pl.BlockSpec((block, columns), lambda at: (at, 0))

    return pl.pallas_call(
        entry_back_kernel,
        grid=(total // block,),
        in_specs=[
            whole((1, length)),
            rows_of(width),
            whole((1, width)),
            whole((width, triple_width)),
            whole(project.shape),
            whole(pair_out.shape),
        ]
        + [rows_of(width)] * len(mid_parts)
        + [whole(part.shape) for part in query_parts],
        out_specs=[rows_of(width), rows_of(inner)],
        out_shape=[
            jax.ShapeDtypeStruct((total, width), jnp.bfloat16),
            jax.ShapeDtypeStruct((total, inner), jnp.bfloat16),
        ],
        cost_estimate=cost(
            total * (length * triple_width + width * (inner + triple_width)),
            4 * width * (inner + triple_width) + 8 * total * width,
        ),
        compiler_params=pltpu.CompilerParams(vmem_limit_bytes=VMEM_LIMIT),
        name="entry_back",
    )(tokens[None, :], vectors, gain[None, :], weights, project, pair_out, *mid_parts, *query_parts)


def mlp_kernel(
    query_width,
    unit_width,
    positions,
    stacked,
    plan_ref,
    resid_in_ref,
    weight_ref,
    own_weight_ref,
    own_cot_ref,
    gain_ref,
    output_from,
    units_from,
    *refs,
):
    bfloat = jnp.bfloat16
    grads_from, mixed_refs, refs = refs[:positions], refs[positions : 2 * positions], refs[2 * positions :]
    resid_ref, swiglu_ref, mid_ref, *refs = refs
    part_refs, refs = refs[:-5], refs[-5:]
    output_ref, units_ref, swiglu_grad_ref, arrived, grad_arrived = refs
    grad_place = plan_ref[positions + pl.program_id(0)]
    for at, grad_from in enumerate(grads_from):
        copy = pltpu.make_async_copy(grad_from, swiglu_grad_ref, grad_arrived)
        pl.when(grad_place == at)(copy.start)
    gate_columns, upward_columns = [pl.ds(at * unit_width, unit_width) for at in range(2)]
    output_columns = [pl.ds(at * query_width, query_width) for at in range(positions)]
    copies = [
        pltpu.make_async_copy(
            output_from.at[:, columns], output_ref.at[:, columns], arrived.at[at]
        )
        for at, columns in enumerate(output_columns)
    ] + [
        pltpu.make_async_copy(
            units_from.at[:, columns], units_ref.at[:, columns], arrived.at[positions + at]
        )
        for at, columns in enumerate((gate_columns, upward_columns))
    ]

    def on_first(act):
        pl.when(pl.program_id(0) == 0)(act)

    @on_first
    def _():
        for copy in copies:
            copy.start()

    resid = resid_in_ref[...].astype(jnp.float32)
    for at, mixed_ref in enumerate(mixed_refs):
        on_first(copies[at].wait)
        columns = output_columns[at]
        resid = resid + times_trans(mixed_ref[...], output_ref[:, columns])
    resid_ref[...] = resid
    gain = gain_ref[...]
    spread = lax.rsqrt(jnp.mean(resid * resid, axis=1, keepdims=True) + EPS)
    normed = resid * spread
    seq_two = (normed * gain).astype(bfloat)
    on_first(copies[positions].wait)
    gate = matmul(seq_two, units_ref[:, gate_columns])
    on_first(copies[positions + 1].wait)
    upward = matmul(seq_two, units_ref[:, upward_columns])
    open_gate = jax.nn.sigmoid(gate)
    silu = gate * open_gate
    swiglu_ref[...] = (silu * upward).astype(bfloat)
    pltpu.make_async_copy(grads_from[0], swiglu_grad_ref, grad_arrived).wait()
    swiglu_grad = weight_ref[...] * swiglu_grad_ref[...]
    slope = open_gate * (1.0 + gate * (1.0 - open_gate))
    gate_grad = (swiglu_grad * upward * slope).astype(bfloat)
    upward_grad = (swiglu_grad * silu).astype(bfloat)
    grad = times_trans(gate_grad, units_ref[:, gate_columns])
    grad = grad + times_trans(upward_grad, units_ref[:, upward_columns])
    grad = grad * gain
    grad = spread * (grad - normed * jnp.mean(grad * normed, axis=1, keepdims=True))
    grad = grad + own_weight_ref[...] * own_cot_ref[...].astype(jnp.float32)
    mid_low = grad.astype(bfloat)
    mid_ref[...] = mid_low
    for at in range(positions):
        columns = output_columns[at]
        part = matmul(mid_low, output_ref[:, columns]).astype(bfloat)
        if stacked:
            part_refs[0][plan_ref[at]] = part
        else:
            part_refs[at][...] = part


def mlp(
    plan,
    block_idx,
    row_total,
    resid_in,
    weight,
    own_weight,
    own_cot,
    swiglu_grads,
    gain,
    output_w,
    units_w,
    mixed,
    stacked,
):
    width = resid_in.shape[1]
    unit_width = units_w.shape[1] // 2
    query_width = mixed[0].shape[1]
    positions = len(mixed)
    block = own_cot.shape[0]

    def rows_of(columns, first=0):
        return pl.BlockSpec((block, columns), lambda at, plan: (at + first, 0))

    first = block_idx * row_total // block
    part_shape = jax.ShapeDtypeStruct((row_total, query_width), jnp.bfloat16)
    part_specs = [rows_of(query_width)] * positions
    part_shapes = [part_shape] * positions
    if stacked:
        part_specs = [pl.BlockSpec((positions, block, query_width), lambda at, plan: (0, at, 0))]
        part_shapes = [
            jax.ShapeDtypeStruct((positions, row_total, query_width), jnp.bfloat16)
        ]

    def whole(shape):
        return pl.BlockSpec(shape, lambda at, plan: (0, 0), pipeline_mode=pl.Buffered(1))

    return pl.pallas_call(
        partial(mlp_kernel, query_width, unit_width, positions, stacked),
        grid_spec=pltpu.PrefetchScalarGridSpec(
            num_scalar_prefetch=1,
            grid=(row_total // block,),
            in_specs=[
                rows_of(width, first),
                rows_of(1, first),
                rows_of(1, first),
                whole((block, width)),
                whole((1, width)),
            ]
            + [pl.BlockSpec(memory_space=pl.ANY)] * (2 + positions)
            + [rows_of(query_width)] * positions,
            out_specs=[
                rows_of(width),
                rows_of(unit_width),
                rows_of(width),
            ]
            + part_specs,
            scratch_shapes=[
                pltpu.VMEM(output_w.shape, output_w.dtype),
                pltpu.VMEM(units_w.shape, units_w.dtype),
                pltpu.VMEM((block, unit_width), jnp.float32),
                pltpu.SemaphoreType.DMA((positions + 2,)),
                pltpu.SemaphoreType.DMA,
            ],
        ),
        out_shape=[
            jax.ShapeDtypeStruct((row_total, width), jnp.float32),
            jax.ShapeDtypeStruct((row_total, unit_width), jnp.bfloat16),
            jax.ShapeDtypeStruct((row_total, width), jnp.bfloat16),
        ]
        + part_shapes,
        cost_estimate=cost(
            row_total * width * (2 * width + 4 * unit_width),
            2 * width * (width + 2 * unit_width) + 16 * row_total * width,
        ),
        compiler_params=pltpu.CompilerParams(vmem_limit_bytes=VMEM_LIMIT),
        name="mlp",
    )(
        plan,
        resid_in,
        weight,
        own_weight,
        own_cot,
        gain[None, :],
        output_w,
        units_w,
        *swiglu_grads,
        *mixed,
    )


def centred(values):
    center = values - jnp.mean(values, axis=1, keepdims=True)
    spread = lax.rsqrt(jnp.mean(center * center, axis=1, keepdims=True) + EPS)
    return center * spread, spread


def centred_back(grad, normed, spread):
    return spread * (
        grad
        - jnp.mean(grad, axis=1, keepdims=True)
        - normed * jnp.mean(grad * normed, axis=1, keepdims=True)
    )


def slot_probs(triple_ref, rows, head, shut):
    wide = HYPER_WIDTH
    at = head * EHD
    queries = triple_ref[rows, at : at + EHD]
    keys = triple_ref[rows, wide + at : wide + at + EHD]
    values = triple_ref[rows, 2 * wide + at : 2 * wide + at + EHD]
    scores = jnp.where(shut, NEG, times_trans(keys, queries) * EHD ** (-0.5))
    parts = jnp.exp(scores - scores.max(axis=0, keepdims=True))
    return queries, keys, values, parts * (1.0 / parts.sum(axis=0, keepdims=True))


def slot_shut(open_ref, rows, count):
    key_entry = lax.broadcasted_iota(jnp.int32, (count, count), 0) // SUBWORD_SLOTS
    query_entry = lax.broadcasted_iota(jnp.int32, (count, count), 1) // SUBWORD_SLOTS
    return (key_entry != query_entry) | (open_ref[rows, :] == 0.0)


def hyper_wide_kernel(
    rows_ref,
    open_ref,
    gains_ref,
    triple_w_ref,
    merge_w_ref,
    expand_w_ref,
    reduce_w_ref,
    length_ref,
    first_ref,
    triple_ref,
    mixed_ref,
    resid_ref,
    second_ref,
    active_ref,
    slope_ref,
    pooled_ref,
):
    bfloat = jnp.bfloat16
    rows_in = rows_ref[...].astype(jnp.float32)
    first_in = (centred(rows_in)[0] * gains_ref[0:1, :]).astype(bfloat)
    first_ref[...] = first_in
    triple_ref[...] = matmul(first_in, triple_w_ref[...]).astype(bfloat)
    total = rows_in.shape[0]
    count = min(128, total)
    for first in range(0, total, count):
        rows = slice(first, first + count)
        shut = slot_shut(open_ref, rows, count)
        heads = []
        for head in range(EH):
            _, _, values, probs = slot_probs(triple_ref, rows, head, shut)
            heads.append(trans_times(values, probs.astype(bfloat)))
        mixed_ref[rows, :] = jnp.concatenate(heads, axis=0).T.astype(bfloat)
    resid_one = rows_in + matmul(mixed_ref[...], merge_w_ref[...])
    resid_ref[...] = resid_one
    second_in = (centred(resid_one)[0] * gains_ref[1:2, :]).astype(bfloat)
    second_ref[...] = second_in
    expanded = matmul(second_in, expand_w_ref[...])
    below = 0.5 * (1.0 + lax.erf(expanded * 0.5**0.5))
    active = (expanded * below).astype(bfloat)
    active_ref[...] = active
    resid_two = resid_one + matmul(active, reduce_w_ref[...])
    kept = jnp.where(open_ref[...] == 0.0, 0.0, resid_two)
    pooled = kept.reshape(total // SUBWORD_SLOTS, SUBWORD_SLOTS, kept.shape[1]).sum(axis=1)
    pooled_ref[...] = (pooled / length_ref[...]).astype(bfloat)
    bell = jnp.exp(-0.5 * expanded * expanded) * (2.0 * math.pi) ** (-0.5)
    slope_ref[...] = below + expanded * bell


def hyper_wide(rows_in, open_rows, gains, triple_w, merge_w, expand_w, reduce_w, lengths):
    total, width = rows_in.shape
    block = min(256, total)
    units = expand_w.shape[1]
    bfloat = jnp.bfloat16
    single = jnp.float32

    def rows_of(columns):
        return pl.BlockSpec((block, columns), lambda at: (at, 0))

    def whole(array):
        return pl.BlockSpec(array.shape, lambda at: (0, 0), pipeline_mode=pl.Buffered(1))

    outs = [
        (width, bfloat),
        (3 * width, bfloat),
        (width, bfloat),
        (width, single),
        (width, bfloat),
        (units, bfloat),
        (units, single),
    ]
    return pl.pallas_call(
        hyper_wide_kernel,
        grid=(total // block,),
        in_specs=[rows_of(width), rows_of(1)]
        + [whole(array) for array in (gains, triple_w, merge_w, expand_w, reduce_w)]
        + [pl.BlockSpec((block // SUBWORD_SLOTS, 1), lambda at: (at, 0))],
        out_specs=[rows_of(columns) for columns, _ in outs]
        + [pl.BlockSpec((block // SUBWORD_SLOTS, width), lambda at: (at, 0))],
        out_shape=[jax.ShapeDtypeStruct((total, columns), kind) for columns, kind in outs]
        + [jax.ShapeDtypeStruct((total // SUBWORD_SLOTS, width), bfloat)],
        cost_estimate=cost(16 * total * width * units, 12 * total * units),
        compiler_params=pltpu.CompilerParams(vmem_limit_bytes=VMEM_LIMIT),
        name="hyper_wide",
    )(rows_in, open_rows, gains, triple_w, merge_w, expand_w, reduce_w, lengths)


def hyper_back_units_kernel(
    dp_size,
    pooled_refs,
    scale_ref,
    gains_ref,
    resid_ref,
    slope_ref,
    mixed_share_ref,
    second_share_ref,
    active_share_ref,
    merge_w_ref,
    expand_w_ref,
    reduce_w_ref,
    resid_out,
    mixed_out,
    early_out,
    gains_out,
    reduce_acc,
    expand_acc,
    merge_acc,
):
    bfloat = jnp.bfloat16
    step = pl.program_id(0)
    total, width = resid_ref.shape
    pooled_grad = sum(ref[...].astype(jnp.float32) for ref in pooled_refs)
    grid_grad = jnp.broadcast_to(
        pooled_grad[:, None, :], (total // SUBWORD_SLOTS, SUBWORD_SLOTS, width)
    ).reshape(total, width)
    grid_grad = grid_grad * scale_ref[...]
    reduce_in = grid_grad.astype(bfloat)
    expand_in = times_trans(reduce_in, reduce_w_ref[...]) * slope_ref[...]
    expand_in = expand_in.astype(bfloat)
    second_grad = times_trans(expand_in, expand_w_ref[...])
    normed, spread = centred(resid_ref[...])
    gain_two = (second_grad * normed).sum(axis=0, keepdims=True)
    resid_grad = grid_grad + centred_back(second_grad * gains_ref[1:2, :], normed, spread)
    resid_out[...] = resid_grad
    merge_in = resid_grad.astype(bfloat)
    mixed_out[...] = times_trans(merge_in, merge_w_ref[...]).astype(bfloat)

    @pl.when(step == 0)
    def _():
        for ref in (reduce_acc, expand_acc, merge_acc, gains_out):
            ref[...] = jnp.zeros_like(ref)

    gains_out[0:1, :] += gain_two
    reduce_acc[...] += trans_times(active_share_ref[...], reduce_in)
    expand_acc[...] += trans_times(second_share_ref[...], expand_in)
    merge_acc[...] += trans_times(mixed_share_ref[...], merge_in)

    @pl.when(step == pl.num_programs(0) - 1)
    def _():
        depth = expand_acc.shape[0] // dp_size
        deep = reduce_acc.shape[0] // expand_acc.shape[0]
        reduced = reduce_acc[...].astype(bfloat).reshape(dp_size, deep, depth, width)
        for at in range(deep):
            early_out[:, at * width : (at + 1) * width] = reduced[:, at].reshape(
                dp_size * depth, width
            )
        units = expand_acc.shape[1]
        early_out[:, deep * width : deep * width + units] = expand_acc[...].astype(bfloat)
        early_out[:, deep * width + units :] = merge_acc[...].astype(bfloat)


def hyper_back_slots_kernel(
    resid_grad_ref,
    mixed_grad_ref,
    rows_ref,
    open_ref,
    gains_ref,
    triple_ref,
    first_share_ref,
    triple_w_ref,
    rows_out,
    late_out,
    gains_out,
    triple_acc,
    triple_in,
):
    bfloat = jnp.bfloat16
    step = pl.program_id(0)
    total, width = rows_ref.shape
    count = min(128, total)
    for first in range(0, total, count):
        rows = slice(first, first + count)
        shut = slot_shut(open_ref, rows, count)
        query_grads = []
        for head in range(EH):
            queries, keys, values, probs = slot_probs(triple_ref, rows, head, shut)
            at = head * EHD
            grad = mixed_grad_ref[rows, at : at + EHD]
            prob_grad = times_trans(values, grad)
            delta = (probs * prob_grad).sum(axis=0, keepdims=True)
            score_grad = (probs * (prob_grad - delta)).astype(bfloat)
            query_grads.append(trans_times(keys, score_grad))
            key_grad = matmul(score_grad, queries) * EHD ** (-0.5)
            value_grad = matmul(probs.astype(bfloat), grad)
            triple_in[rows, width + at : width + at + EHD] = key_grad.astype(bfloat)
            triple_in[rows, 2 * width + at : 2 * width + at + EHD] = value_grad.astype(bfloat)
        query_grad = jnp.concatenate(query_grads, axis=0).T * EHD ** (-0.5)
        triple_in[rows, :width] = query_grad.astype(bfloat)
    triple_grad = triple_in[...]
    first_grad = times_trans(triple_grad, triple_w_ref[...])
    normed, spread = centred(rows_ref[...].astype(jnp.float32))
    gain_one = (first_grad * normed).sum(axis=0, keepdims=True)
    rows_grad = resid_grad_ref[...] + centred_back(first_grad * gains_ref[0:1, :], normed, spread)
    rows_out[...] = rows_grad.astype(bfloat)

    @pl.when(step == 0)
    def _():
        triple_acc[...] = jnp.zeros_like(triple_acc)
        gains_out[...] = jnp.zeros_like(gains_out)

    gains_out[0:1, :] += gain_one
    triple_acc[...] += trans_times(first_share_ref[...], triple_grad)

    @pl.when(step == pl.num_programs(0) - 1)
    def _():
        late_out[...] = triple_acc[...].astype(bfloat)


def row_block(columns, rows):
    return pl.BlockSpec((rows, columns), lambda at: (at, 0))


def whole_block(shape):
    return pl.BlockSpec(shape, lambda at: (0, 0), pipeline_mode=pl.Buffered(1))


def hyper_back_units(dp_size, pooled, scale, gains, resid, slope, shares, weights):
    total, width = resid.shape
    block = min(256, total)
    units = slope.shape[1]
    share_width = shares[0].shape[1]
    deep = shares[2].shape[1] // share_width
    bfloat = jnp.bfloat16
    single = jnp.float32

    def kernel(*refs):
        hyper_back_units_kernel(dp_size, refs[: len(pooled)], *refs[len(pooled) :])

    early_width = deep * width + units + width
    return pl.pallas_call(
        kernel,
        grid=(total // block,),
        in_specs=[row_block(width, block // SUBWORD_SLOTS)] * len(pooled)
        + [row_block(1, block), whole_block(gains.shape)]
        + [row_block(width, block), row_block(units, block)]
        + [row_block(array.shape[1], block) for array in shares]
        + [whole_block(array.shape) for array in weights],
        out_specs=[
            row_block(width, block),
            row_block(width, block),
            pl.BlockSpec((share_width, early_width), lambda at: (0, 0)),
            pl.BlockSpec((8, width), lambda at: (0, 0)),
        ],
        out_shape=[
            jax.ShapeDtypeStruct((total, width), single),
            jax.ShapeDtypeStruct((total, width), bfloat),
            jax.ShapeDtypeStruct((share_width, early_width), bfloat),
            jax.ShapeDtypeStruct((8, width), single),
        ],
        scratch_shapes=[
            pltpu.VMEM((deep * share_width, width), single),
            pltpu.VMEM((share_width, units), single),
            pltpu.VMEM((share_width, width), single),
        ],
        cost_estimate=cost(12 * total * width * units, 6 * total * units),
        compiler_params=pltpu.CompilerParams(vmem_limit_bytes=VMEM_LIMIT),
        name="hyper_back_units",
    )(*pooled, scale, gains, resid, slope, *shares, *weights)


def hyper_back_slots(resid_grad, mixed_grad, rows_in, open_rows, gains, triple, first_share, weight):
    total, width = rows_in.shape
    block = min(256, total)
    share_width = first_share.shape[1]
    bfloat = jnp.bfloat16
    single = jnp.float32
    return pl.pallas_call(
        hyper_back_slots_kernel,
        grid=(total // block,),
        in_specs=[row_block(width, block)] * 3
        + [row_block(1, block), whole_block(gains.shape), row_block(3 * width, block)]
        + [row_block(share_width, block), whole_block(weight.shape)],
        out_specs=[
            row_block(width, block),
            pl.BlockSpec((share_width, 3 * width), lambda at: (0, 0)),
            pl.BlockSpec((8, width), lambda at: (0, 0)),
        ],
        out_shape=[
            jax.ShapeDtypeStruct((total, width), bfloat),
            jax.ShapeDtypeStruct((share_width, 3 * width), bfloat),
            jax.ShapeDtypeStruct((8, width), single),
        ],
        scratch_shapes=[
            pltpu.VMEM((share_width, 3 * width), single),
            pltpu.VMEM((block, 3 * width), bfloat),
        ],
        cost_estimate=cost(40 * total * width * width, 8 * total * width),
        compiler_params=pltpu.CompilerParams(vmem_limit_bytes=VMEM_LIMIT),
        name="hyper_back_slots",
    )(resid_grad, mixed_grad, rows_in, open_rows, gains, triple, first_share, weight)


def per_device(
    subword_embedding_rows,
    entry_subword_index,
    entry_lengths,
    entry_counts,
    encoder_triple,
    encoder_merge,
    encoder_expand,
    encoder_reduce,
    embed_project,
    normone_gain,
    normtwo_gain,
    frozen_query,
    frozen_key,
    frozen_value,
    frozen_output,
    frozen_gate,
    frozen_upward,
    frozen_downward,
    prenorm_gain,
    midnorm_gain,
    text_tokens,
    cotangent,
):
    bfloat = jnp.bfloat16
    single = jnp.float32
    dp_size = lax.axis_size("dp")
    tensor_size = lax.axis_size("tensor")
    dp_at = lax.axis_index("dp")
    tensor_at = lax.axis_index("tensor")
    device_at = dp_at * tensor_size + tensor_at
    entries = entry_subword_index.shape[0]
    entry_total = entries * dp_size * tensor_size
    flat_rows = entries * SUBWORD_SLOTS
    table_rows = subword_embedding_rows.shape[0]
    model_width = embed_project.shape[1]

    with jax.named_scope("ids"):
        packed = jnp.concatenate(
            [entry_subword_index, entry_counts[:, None], entry_lengths[:, None]], axis=1
        )
        packed_width = packed.shape[1]
        first_weights = jnp.concatenate(
            [frozen_query, frozen_key, frozen_value, frozen_downward], axis=1
        )
        packed_dp = lax.all_gather(tie(packed, first_weights), "dp", axis=0, tiled=False)
    with jax.named_scope("first_weights"):
        first_weights = lax.all_gather(first_weights, "dp", axis=0, tiled=True)
        query_width = frozen_query.shape[1]
        key_width = frozen_key.shape[1]
        triple_width = query_width + 2 * key_width
        unit_width = frozen_gate.shape[1]
        full_downward = first_weights[:, triple_width:]
        second_weights = jnp.concatenate([frozen_gate, frozen_upward], axis=1)
    with jax.named_scope("lookup"):
        local_ids = packed_dp[:, :, :SUBWORD_SLOTS].reshape(-1) - dp_at * table_rows
        inside = (local_ids >= 0) & (local_ids < table_rows)
        served = jnp.take(subword_embedding_rows, jnp.clip(local_ids, 0, table_rows - 1), axis=0)
        served = jnp.where(inside[:, None], served, jnp.zeros((), bfloat))
        served_all = lax.all_to_all(
            served.reshape(dp_size, flat_rows, HYPER_WIDTH), "dp", 0, 0, tiled=True
        )
        rows_in = jnp.sum(served_all.astype(single), axis=0)
    with jax.named_scope("cot_ring"):
        cot_blocks = [cotangent, ring(cotangent)]
        length = text_tokens.shape[0] * tensor_size
        cosine, sine = rope_lanes(length)
        cot_blocks.append(ring(cot_blocks[-1]))
        rows_in, cosine, sine, second_weights, *cot_blocks = lax.optimization_barrier(
            (rows_in, cosine, sine, second_weights, *cot_blocks)
        )
        second_weights = lax.all_gather(second_weights, "dp", axis=0, tiled=True)
        packed_all = from_all(
            tie(jnp.concatenate([packed_dp.reshape(-1), text_tokens]), cot_blocks[1])
        )
    with jax.named_scope("hyper_wide"):
        rows_blocks = from_all(rows_in.astype(bfloat))
    with jax.named_scope("hyper_wide"):
        rows_wide = jnp.concatenate(in_order(rows_blocks, tensor_at), axis=0)
        packed_all = jnp.stack(in_order(packed_all, tensor_at))
        ids_size = dp_size * entries * packed_width
        packed_ids = packed_all[:, :ids_size].reshape(tensor_size, dp_size, entries, packed_width)
        lengths_wide = lax.dynamic_index_in_dim(packed_ids, dp_at, 1, keepdims=False)
        lengths_wide = lengths_wide[:, :, SUBWORD_SLOTS + 1].reshape(-1)
        valid_wide = jnp.arange(SUBWORD_SLOTS)[None, :] < lengths_wide[:, None]
        valid_wide = valid_wide.astype(single)
        counts_wide = lengths_wide.astype(single)[:, None]
        open_wide = valid_wide.reshape(-1, 1)
        scale_wide = (valid_wide / counts_wide).reshape(-1, 1)
        gain_pair = jnp.stack([normone_gain, normtwo_gain])
        encoders = (encoder_triple, encoder_merge, encoder_expand, encoder_reduce)
        first_in, triple, mixed, resid_one, second_in, activated, slope, dp_pooled = hyper_wide(
            rows_wide, open_wide, gain_pair, *encoders, counts_wide
        )
    with jax.named_scope("output_weights"):
        output_blocks = from_all(tie(frozen_output, dp_pooled))
    with jax.named_scope("pooled_gather"):
        all_pooled = lax.all_gather(dp_pooled, "dp", axis=0, tiled=True)
    with jax.named_scope("output_weights"):
        output_weights = jnp.concatenate(output_blocks, axis=1)
        output_weights, all_pooled = lax.optimization_barrier((output_weights, all_pooled))
        output_weights = lax.all_gather(
            tie(output_weights, first_weights), "dp", axis=0, tiled=True
        )
    with jax.named_scope("cot_ring"):
        cot_blocks.append(ring(tie(cot_blocks[-1], all_pooled)))
    with jax.named_scope("entry_vectors"):
        seq_tokens = packed_all[:, ids_size:].reshape(-1)
        all_vectors, seq_triple = entry(
            seq_tokens, all_pooled, embed_project, prenorm_gain, first_weights, triple_width
        )

    with jax.named_scope("attention_fwd"):
        block_rows = min(512, length)
        block_total = length // block_rows
        first_mixed = attention(seq_triple, cosine, sine, query_width, 0, block_rows)

    with jax.named_scope("mlp_rows"):
        late_ids, late_tokens = tie_all(first_mixed, packed_ids, seq_tokens)
        late_ids = late_ids.transpose(1, 0, 2, 3).reshape(entry_total, packed_width)
        all_ids = late_ids[:, :SUBWORD_SLOTS].reshape(-1)
        all_weights = (1.0 / jnp.log(1.0 + late_ids[:, SUBWORD_SLOTS].astype(single))).astype(
            bfloat
        )
        rows_here = text_tokens.shape[0]
        seq_hot = (late_tokens[:, None] == jnp.arange(entry_total)[None, :]).astype(bfloat)
        seq_weight = matmul(seq_hot, all_weights[:, None])
        own_rows_here = jnp.arange(length) // rows_here == tensor_at
        own_weight = jnp.where(own_rows_here[:, None], seq_weight, 0.0)
        resid_in = matmul(seq_hot, all_vectors).astype(bfloat)
        per_block = block_rows // rows_here
        vectors = lax.dynamic_slice_in_dim(all_vectors, device_at * entries, entries, 0)

    with jax.named_scope("attention_fwd"):
        seq_triple = tie(seq_triple, resid_in)
        mixed_parts = [[first_mixed]]
        for first in range(block_rows, length, block_rows):
            lm_mixed = attention(seq_triple, cosine, sine, query_width, first, block_rows)
            mixed_parts.append([lm_mixed])
    with jax.named_scope("mixed_ring"):
        for block_idx, parts in enumerate(mixed_parts):
            last_part = ring(parts[0], tensor_size - 1)
            parts.append(ring(parts[0]))
            for step in range(2, tensor_size - 1):
                parts.append(ring(parts[-1]))
            parts.append(last_part)

    def share(values):
        rows, width = values.shape
        split = values.reshape(rows, dp_size, tensor_size, width // (dp_size * tensor_size))
        return lax.dynamic_index_in_dim(split, tensor_at, 2, keepdims=False).reshape(
            rows, width // tensor_size
        )

    shares = [share(array) for array in (first_in, mixed, second_in, activated)]

    with jax.named_scope("swiglu_grad"):
        late_cots = tie(cot_blocks, lm_mixed)
        swiglu_grads = [matmul(cot, full_downward) for cot in late_cots]

    with jax.named_scope("mlp"):
        places = lax.rem(tensor_at + tensor_size - jnp.arange(tensor_size), tensor_size)
        resid_blocks = []
        layer_parts = []
        mid_parts = []
        mixed_grads = []
        for block_idx, parts in enumerate(mixed_parts):
            last = block_idx == block_total - 1
            rows = slice(block_idx * block_rows, (block_idx + 1) * block_rows)
            if block_idx == 0:
                near = [[later[1], later[-1]] for later in mixed_parts[1:]]
                parts, near = lax.optimization_barrier((parts, near))
                for later, (below, above) in zip(mixed_parts[1:], near):
                    later[1], later[-1] = below, above
                    for step in range(2, tensor_size - 1):
                        later[step] = ring(later[step - 1])
            else:
                parts, layer_parts, mid_parts = lax.optimization_barrier(
                    (parts, layer_parts, mid_parts)
                )
            block_places = block_idx * per_block + jnp.arange(per_block)
            block_places = lax.rem(tensor_at + tensor_size - block_places, tensor_size)
            resid_mid, swiglu_low, mid_low, *mixed_part = mlp(
                jnp.concatenate([places, block_places]),
                block_idx,
                block_rows,
                resid_in,
                seq_weight,
                own_weight,
                cotangent,
                swiglu_grads,
                midnorm_gain,
                output_weights,
                second_weights,
                parts,
                not last,
            )
            resid_blocks.append(resid_mid)
            if not last:
                mixed_grads.append(
                    lax.psum_scatter(
                        mixed_part[0].reshape(-1, query_width),
                        "tensor",
                        scatter_dimension=0,
                        tiled=True,
                    )
                )
                layer_parts.append(times_trans(swiglu_low, full_downward).astype(bfloat))
                mid_parts.append(trans_times(seq_hot[rows], mid_low))
                continue
            carried = None
            for step in [*range(1, tensor_size), 0]:
                part = mixed_part[step]
                if step == 2:
                    mid_parts.append(trans_times(seq_hot[rows], mid_low))
                    carried, mid_parts = lax.optimization_barrier((carried, mid_parts))
                if step == 3:
                    layer_parts.append(times_trans(swiglu_low, full_downward).astype(bfloat))
                    layer_cut = model_width * 5 // 8
                    layer_halves = [
                        jnp.concatenate([part[:, columns] for part in layer_parts], axis=0)
                        for columns in (slice(None, layer_cut), slice(layer_cut, None))
                    ]
                    carried, layer_halves, shares = lax.optimization_barrier(
                        (carried, layer_halves, shares)
                    )
                if step == 0:
                    pair_out = None
                    query_parts = []
                    for at, mixed_grad in enumerate(mixed_grads):
                        query_part, pair_out = attention_back(
                            seq_triple, cosine, sine, mixed_grad, at * block_rows, pair_out
                        )
                        query_parts.append(query_part)
                    carried, pair_out = lax.optimization_barrier((carried, pair_out))
                if carried is not None:
                    part = (part.astype(single) + carried.astype(single)).astype(bfloat)
                if step > 0:
                    carried = ring(part)
            last_grad = part

    with jax.named_scope("layer_out"):
        layer_near, layer_far = layer_halves
        layer_near = lax.psum_scatter(
            tie(layer_near, last_grad), "tensor", scatter_dimension=0, tiled=True
        )
        blocks_of = [
            lax.dynamic_slice_in_dim(
                block, lax.rem(tensor_at * rows_here, block_rows), rows_here, 0
            )
            for block in resid_blocks
        ]
        resid_own = blocks_of[0]
        for block_idx in range(1, block_total):
            resid_own = jnp.where(
                tensor_at * rows_here // block_rows == block_idx, blocks_of[block_idx], resid_own
            )
    with jax.named_scope("attention_bwd"):
        query_part, pair_out = attention_back(
            seq_triple, cosine, sine, last_grad, length - block_rows, pair_out
        )
        query_parts.append(query_part)

    with jax.named_scope("entry_bwd"):
        entry_part, pooled_part = entry_back(
            seq_tokens,
            all_vectors,
            prenorm_gain,
            first_weights,
            embed_project,
            pair_out,
            mid_parts,
            query_parts,
        )
        project_part = trans_times(all_pooled, entry_part).astype(bfloat)
        pooled_shares, project_part = lax.optimization_barrier(
            (to_owners(pooled_part), project_part)
        )
        pooled_part = jnp.sum(pooled_shares.astype(single), axis=0).astype(bfloat)
        pooled_grads = from_all(pooled_part)

    with jax.named_scope("hyper_bwd"):
        project_shares = to_owners(tie(project_part, pooled_grads[1]))
    with jax.named_scope("layer_out"):
        layer_far = lax.psum_scatter(
            tie(layer_far, pooled_grads, layer_near), "tensor", scatter_dimension=0, tiled=True
        )
        layer_final = resid_own + jnp.concatenate([layer_near, layer_far], axis=1).astype(single)
    with jax.named_scope("hyper_bwd"):
        resid_grad, mixed_grad, early, gain_two = hyper_back_units(
            dp_size,
            pooled_grads,
            scale_wide,
            gain_pair,
            resid_one,
            slope,
            shares[1:],
            encoders[1:],
        )
        resid_grad, early, project_shares = lax.optimization_barrier(
            (resid_grad, early, project_shares)
        )
        early = to_owners(early)
        rows_low, late, gain_one = hyper_back_slots(
            resid_grad,
            mixed_grad,
            rows_wide,
            open_wide,
            gain_pair,
            triple,
            shares[0],
            encoder_triple,
        )

    with jax.named_scope("grads_out"):
        rows_low, early, project_shares = lax.optimization_barrier(
            (rows_low, early, project_shares)
        )
        early = jnp.sum(early.astype(single), axis=0)
        project_grad = jnp.sum(project_shares.astype(single), axis=0).astype(bfloat)
        all_rows = lax.all_gather(rows_low, "dp", axis=0, tiled=True)
        late, project_grad = tie_all(rows_low, late, project_grad)
        project_grad = project_grad.reshape(tensor_size, -1, model_width)
        project_grad = lax.all_to_all(project_grad, "tensor", 0, 0, tiled=True)
        project_grad = jnp.sum(project_grad.astype(single), axis=0)
        own_rows = table_rows // tensor_size
        row_hot = (
            (jnp.arange(own_rows) + device_at * own_rows)[:, None] == all_ids[None, :]
        ).astype(bfloat)
        subword_grad = matmul(row_hot, all_rows)

        gain_grads = share(jnp.concatenate([gain_one[:1], gain_two[:1]], axis=0)).transpose(1, 0).astype(bfloat)
        late = jnp.concatenate([late, jnp.pad(gain_grads, ((0, 0), (0, 126)))], axis=1)
        late = scatter_dp(late)
        depth = early.shape[0]
        deep = encoder_reduce.shape[0] // HYPER_WIDTH
        reduce_width = deep * HYPER_WIDTH
        expand_width = encoder_expand.shape[1]
        reduce_grad = early[:, :reduce_width].reshape(depth, deep, HYPER_WIDTH)
        reduce_grad = reduce_grad.transpose(1, 0, 2).reshape(deep * depth, HYPER_WIDTH)
        expand_grad = early[:, reduce_width : reduce_width + expand_width]
        merge_grad = early[:, reduce_width + expand_width :]
        grad_width = encoder_triple.shape[1]
    return (
        layer_final.astype(bfloat),
        vectors,
        subword_grad,
        late[:, :grad_width],
        merge_grad,
        expand_grad,
        reduce_grad,
        project_grad,
        late[:, grad_width],
        late[:, grad_width + 1],
    )


def solution(mesh):
    return jax.shard_map(
        per_device,
        mesh=mesh,
        in_specs=(
            P("dp", None),
            P(("dp", "tensor"), None),
            P(("dp", "tensor")),
            P(("dp", "tensor")),
            P(),
            P(),
            P(),
            P(),
            P(),
            P(),
            P(),
            P("dp", "tensor"),
            P("dp", "tensor"),
            P("dp", "tensor"),
            P("dp", "tensor"),
            P("dp", "tensor"),
            P("dp", "tensor"),
            P("dp", "tensor"),
            P(),
            P(),
            P(("dp", "tensor")),
            P(("dp", "tensor"), None),
        ),
        out_specs=(
            P(("dp", "tensor"), None),
            P(("dp", "tensor"), None),
            P(("dp", "tensor"), None),
            P(("dp", "tensor"), None),
            P(("dp", "tensor"), None),
            P(("dp", "tensor"), None),
            P(("dp", "tensor"), None),
            P(("dp", "tensor"), None),
            P(("dp", "tensor")),
            P(("dp", "tensor")),
        ),
        check_vma=False,
    )
```

```python
import math
from functools import partial

import jax
import jax.numpy as jnp
from jax import lax
from jax.experimental import pallas as pl
from jax.experimental.pallas import tpu as pltpu
from jax.sharding import PartitionSpec as P

HD = 64
HYPER_WIDTH = 512
EH = 8
EHD = 64
SUBWORD_SLOTS = 8


NEG = -1000000000.0
EPS = 1e-05
THETA = 10000.0
VMEM_LIMIT = 62 * 1024 * 1024


def layer_norm(values, gain):
    center = values - jnp.mean(values, axis=-1, keepdims=True)
    spread = jnp.mean(center * center, axis=-1, keepdims=True)
    return center * lax.rsqrt(spread + EPS) * gain


def rms_norm(values, gain):
    return values * lax.rsqrt(jnp.mean(values * values, axis=-1, keepdims=True) + EPS) * gain


def rope_tables(length, width):
    half_width = width // 2
    inverse = THETA ** (-(2.0 * jnp.arange(half_width, dtype=jnp.float32)) / width)
    angles = jnp.arange(length, dtype=jnp.float32)[:, None] * inverse[None, :]
    return (jnp.cos(angles), jnp.sin(angles))


def rotate(values, cosine, sine):
    half_width = values.shape[-1] // 2
    former = values[..., :half_width]
    latter = values[..., half_width:]
    return jnp.concatenate(
        [former * cosine - latter * sine, latter * cosine + former * sine], axis=-1
    )


def matmul(left, right):
    return jnp.dot(left, right, preferred_element_type=jnp.float32)


def times_trans(left, right):
    return lax.dot_general(
        left, right, (((1,), (1,)), ((), ())), preferred_element_type=jnp.float32
    )


def trans_times(left, right):
    return lax.dot_general(
        left, right, (((0,), (0,)), ((), ())), preferred_element_type=jnp.float32
    )


def ring(values, shift=1):
    size = lax.axis_size("tensor")
    return lax.ppermute(values, "tensor", [(i, (i + shift) % size) for i in range(size)])


def tie(values, *others):
    return lax.optimization_barrier((values, *others))[0]


def tie_all(first, *values):
    return lax.optimization_barrier((*values, first))[:-1]


def in_order(blocks, first):
    size = len(blocks)
    stacked = jnp.stack(blocks)
    return [
        lax.dynamic_index_in_dim(stacked, lax.rem(first - at + size, size), 0, keepdims=False)
        for at in range(size)
    ]


def to_owners(values):
    size = lax.axis_size("dp")
    blocks = values.reshape(size, values.shape[0] // size, values.shape[1])
    return lax.all_to_all(blocks, "dp", 0, 0, tiled=True)


def scatter_dp(values):
    return jnp.sum(to_owners(values).astype(jnp.float32), axis=0)


def from_all(values):
    return [values] + [ring(values, shift) for shift in range(1, lax.axis_size("tensor"))]


def cost(multiplies, values, transcendentals=0):
    return pl.CostEstimate(
        flops=2 * multiplies, bytes_accessed=values, transcendentals=transcendentals
    )


def rope_lanes(length):
    cosine, sine = rope_tables(length, HD)
    return (
        jnp.concatenate([cosine] * 4, axis=1),
        jnp.concatenate([-sine, sine, -sine, sine], axis=1),
    )


def swap(values):
    width = values.shape[1]
    lane = lax.broadcasted_iota(jnp.int32, values.shape, 1)
    ahead = pltpu.roll(values, width - HD // 2, 1)
    behind = pltpu.roll(values, HD // 2, 1)
    return jnp.where(lane % HD < HD // 2, ahead, behind)


def attention_operands(query_ref, pair_ref, cos_ref, sin_ref):
    bfloat = jnp.bfloat16
    cosine = cos_ref[...]
    sine = sin_ref[...]
    queries = query_ref[...]
    pair = pair_ref[...]
    queries = (queries * cosine + swap(queries) * sine).astype(bfloat)
    queries = queries * jnp.asarray(HD ** (-0.5), bfloat)
    keys = (pair * cosine + swap(pair) * sine).astype(bfloat)[:, :HD]
    return queries, keys, pair.astype(bfloat)[:, HD:]


def scores_by_key(keys, query_block, first):
    rows = query_block.shape[0]
    own = times_trans(keys[first : first + rows], query_block)
    key_at = lax.broadcasted_iota(jnp.int32, own.shape, 0)
    query_at = lax.broadcasted_iota(jnp.int32, own.shape, 1)
    parts = [jnp.where(query_at >= key_at, own, NEG)]
    if first > 0:
        parts.insert(0, times_trans(keys[:first], query_block))
    return parts


def attention_kernel(
    block_rows, base, query_ref, pair_ref, cos_ref, sin_ref, out_ref, total_ref
):
    queries, keys, values = attention_operands(query_ref, pair_ref, cos_ref, sin_ref)
    for first in range(base, queries.shape[0], block_rows):
        rows = slice(first, first + block_rows)
        heads = []
        for head in range(queries.shape[1] // HD):
            query_block = queries[rows, head * HD : (head + 1) * HD]
            parts = scores_by_key(keys, query_block, first)
            largest = parts[0].max(axis=0, keepdims=True)
            for part in parts[1:]:
                largest = jnp.maximum(largest, part.max(axis=0, keepdims=True))
            parts = [jnp.exp(part - largest) for part in parts]
            total = sum(part.sum(axis=0, keepdims=True) for part in parts)
            at = 0
            mixed = None
            for part in parts:
                here = trans_times(values[at : at + part.shape[0]], part.astype(jnp.bfloat16))
                mixed = here if mixed is None else mixed + here
                at += part.shape[0]
            mixed = mixed * (1.0 / total)
            out_rows = slice(first - base, first - base + block_rows)
            total_ref[0, head : head + 1, out_rows] = largest + jnp.log(total)
            heads.append(mixed)
        out_ref[out_rows, :] = jnp.concatenate(heads, axis=0).T.astype(jnp.bfloat16)


def attention_back_kernel(
    block_rows, base, query_ref, pair_ref, cos_ref, sin_ref, grad_ref, mixed_ref, total_ref, add_ref, query_out, pair_out, acc_ref
):
    bfloat = jnp.bfloat16
    queries, keys, values = attention_operands(query_ref, pair_ref, cos_ref, sin_ref)

    @pl.when(pl.program_id(0) == 0)
    def _():
        acc_ref[...] = jnp.zeros_like(acc_ref) if add_ref is None else add_ref[...]

    for first in range(base, queries.shape[0], block_rows):
        rows = slice(first, first + block_rows)
        out_rows = slice(first - base, first - base + block_rows)
        deltas = mixed_ref[out_rows, :].astype(jnp.float32) * grad_ref[out_rows, :].astype(
            jnp.float32
        )
        deltas = deltas.T
        heads = []
        for head in range(queries.shape[1] // HD):
            lanes = slice(head * HD, (head + 1) * HD)
            query_block = queries[rows, lanes]
            grad_block = grad_ref[out_rows, lanes]
            parts = scores_by_key(keys, query_block, first)
            row_total = total_ref[0, head : head + 1, out_rows]
            parts = [jnp.exp(part - row_total) for part in parts]
            delta = deltas[head * HD : (head + 1) * HD].sum(axis=0, keepdims=True)
            at = 0
            prob_grads = []
            for part in parts:
                prob_grads.append(times_trans(values[at : at + part.shape[0]], grad_block))
                at += part.shape[0]
            at = 0
            query_grad = None
            for part, prob_grad in zip(parts, prob_grads):
                here = slice(at, at + part.shape[0])
                score_grad = (part * (prob_grad - delta)).astype(bfloat)
                key_part = matmul(score_grad, query_block)
                value_part = matmul(part.astype(bfloat), grad_block)
                acc_ref[here, :] += jnp.concatenate([key_part, value_part], axis=1)
                query_part = trans_times(keys[here], score_grad)
                query_grad = query_part if query_grad is None else query_grad + query_part
                at += part.shape[0]
            heads.append(query_grad)
        grad = jnp.concatenate(heads, axis=0).T * HD ** (-0.5)
        grad = grad * cos_ref[rows, :] - swap(grad) * sin_ref[rows, :]
        query_out[out_rows, :] = grad.astype(bfloat)

    @pl.when(pl.program_id(0) == pl.num_programs(0) - 1)
    def _():
        total = acc_ref[...]
        if pair_out.dtype == jnp.float32:
            pair_out[...] = jnp.zeros_like(pair_out)
            pair_out[: total.shape[0], :] = total
            return
        turned = total * cos_ref[...] - swap(total) * sin_ref[...]
        lane = lax.broadcasted_iota(jnp.int32, total.shape, 1)
        pair_out[...] = jnp.where(lane < HD, turned, total).astype(bfloat)


def attention(seq_triple, cosine, sine, query_width, base, rows):
    pairs = query_width // (2 * HD)
    wide = 2 * HD
    keys = base + rows
    return pl.pallas_call(
        partial(attention_kernel, min(256, rows), base),
        grid=(pairs,),
        in_specs=[
            pl.BlockSpec((keys, wide), lambda at: (0, at)),
            pl.BlockSpec((keys, wide), lambda at: (0, pairs)),
            pl.BlockSpec((keys, wide), lambda at: (0, 0)),
            pl.BlockSpec((keys, wide), lambda at: (0, 0)),
        ],
        out_specs=[
            pl.BlockSpec((rows, wide), lambda at: (0, at)),
            pl.BlockSpec((1, 8, rows), lambda at: (at, 0, 0)),
        ],
        out_shape=[
            jax.ShapeDtypeStruct((rows, query_width), jnp.bfloat16),
            jax.ShapeDtypeStruct((pairs, 8, rows), jnp.float32),
        ],
        cost_estimate=cost(
            8 * query_width * rows * keys, 6 * query_width * keys, query_width * keys * 10
        ),
        compiler_params=pltpu.CompilerParams(vmem_limit_bytes=VMEM_LIMIT),
        name="attention",
    )(seq_triple, seq_triple, cosine, sine)


def attention_back(seq_triple, cosine, sine, mixed_grad, mixed, totals, base, before):
    length = seq_triple.shape[0]
    rows, query_width = mixed_grad.shape
    pairs = query_width // (2 * HD)
    wide = 2 * HD
    keys = base + rows
    last = keys == length
    specs = [
        pl.BlockSpec((keys, wide), lambda at: (0, at)),
        pl.BlockSpec((keys, wide), lambda at: (0, pairs)),
        pl.BlockSpec((keys, wide), lambda at: (0, 0)),
        pl.BlockSpec((keys, wide), lambda at: (0, 0)),
        pl.BlockSpec((rows, wide), lambda at: (0, at)),
        pl.BlockSpec((rows, wide), lambda at: (0, at)),
        pl.BlockSpec((1, 8, rows), lambda at: (at, 0, 0)),
    ]
    operands = [seq_triple, seq_triple, cosine, sine, mixed_grad, mixed, totals]
    if before is not None:
        specs.append(pl.BlockSpec((keys, wide), lambda at: (0, 0)))
        operands.append(before)

    def kernel(*refs):
        given = refs[: len(operands)]
        add_ref = None if before is None else given[-1]
        attention_back_kernel(
            min(256, rows), base, *given[:7], add_ref, *refs[len(operands) :]
        )

    return pl.pallas_call(
        kernel,
        grid=(pairs,),
        in_specs=specs,
        out_specs=[
            pl.BlockSpec((rows, wide), lambda at: (0, at)),
            pl.BlockSpec((length, wide), lambda at: (0, 0)),
        ],
        out_shape=[
            jax.ShapeDtypeStruct((rows, query_width), jnp.bfloat16),
            jax.ShapeDtypeStruct((length, wide), jnp.bfloat16 if last else jnp.float32),
        ],
        cost_estimate=cost(
            20 * query_width * rows * keys, 8 * query_width * length, query_width * keys * 10
        ),
        scratch_shapes=[pltpu.VMEM((keys, wide), jnp.float32)],
        compiler_params=pltpu.CompilerParams(vmem_limit_bytes=VMEM_LIMIT),
        name="attention_back",
    )(*operands)


def unit_scale(values):
    spread = lax.rsqrt(jnp.mean(values * values, axis=1, keepdims=True) + EPS)
    return values * spread, spread


def one_hot(places, first, shape, axis):
    at = lax.broadcasted_iota(jnp.int32, shape, axis) + first
    return jnp.where(places == at, 1.0, 0.0).astype(jnp.bfloat16)


def entry_kernel(
    tokens_ref, pooled_ref, project_ref, gain_ref, triple_w_ref, vectors_ref, seq_ref
):
    bfloat = jnp.bfloat16
    step = pl.program_id(0)
    vectors = matmul(pooled_ref[...], project_ref[...]).astype(bfloat)
    vectors_ref[...] = vectors
    normed, _ = unit_scale(vectors.astype(jnp.float32))
    triple = matmul((normed * gain_ref[...]).astype(bfloat), triple_w_ref[...])
    high = triple.astype(bfloat)
    rest = (triple - high.astype(jnp.float32)).astype(bfloat)
    count = vectors.shape[0]
    hot = one_hot(tokens_ref[...], step * count, (seq_ref.shape[0], count), 1)
    picked = matmul(hot, high) + matmul(hot, rest)

    @pl.when(step == 0)
    def _():
        seq_ref[...] = picked

    @pl.when(step > 0)
    def _():
        seq_ref[...] += picked


def entry(tokens, pooled, project, gain, weights, triple_width):
    total, inner = pooled.shape
    length = tokens.shape[0]
    width = project.shape[1]
    block = min(512, total)

    def whole(shape):
        return pl.BlockSpec(shape, lambda at: (0, 0), pipeline_mode=pl.Buffered(1))

    return pl.pallas_call(
        entry_kernel,
        grid=(total // block,),
        in_specs=[
            whole((length, 1)),
            pl.BlockSpec((block, inner), lambda at: (at, 0)),
            whole(project.shape),
            whole((1, width)),
            whole((width, triple_width)),
        ],
        out_specs=[
            pl.BlockSpec((block, width), lambda at: (at, 0)),
            pl.BlockSpec((length, triple_width), lambda at: (0, 0)),
        ],
        out_shape=[
            jax.ShapeDtypeStruct((total, width), jnp.bfloat16),
            jax.ShapeDtypeStruct((length, triple_width), jnp.float32),
        ],
        cost_estimate=cost(
            total * width * (inner + triple_width) + 2 * length * total * triple_width,
            4 * width * (inner + triple_width),
        ),
        compiler_params=pltpu.CompilerParams(vmem_limit_bytes=VMEM_LIMIT),
        name="entry",
    )(tokens[:, None], pooled, project, gain[None, :], weights)


def entry_back_kernel(
    tokens_ref,
    vectors_ref,
    gain_ref,
    triple_w_ref,
    project_ref,
    pair_ref,
    *refs,
):
    bfloat = jnp.bfloat16
    half = (len(refs) - 2) // 2
    mid_refs, query_refs = refs[:half], refs[half:-2]
    entry_ref, pooled_ref = refs[-2:]
    count = vectors_ref.shape[0]
    length = tokens_ref.shape[1]
    hot = one_hot(tokens_ref[...], pl.program_id(0) * count, (count, length), 0)
    at = 0
    query_out = None
    for ref in query_refs:
        here = matmul(hot[:, at : at + ref.shape[0]], ref[...])
        query_out = here if query_out is None else query_out + here
        at += ref.shape[0]
    pair_out = matmul(hot, pair_ref[...])
    query_width = query_out.shape[1]
    grad = times_trans(query_out.astype(bfloat), triple_w_ref[:, :query_width])
    grad = grad + times_trans(pair_out.astype(bfloat), triple_w_ref[:, query_width:])
    grad = grad * gain_ref[...]
    normed, spread = unit_scale(vectors_ref[...].astype(jnp.float32))
    grad = spread * (grad - normed * jnp.mean(grad * normed, axis=1, keepdims=True))
    entry_grad = (grad + sum(ref[...] for ref in mid_refs)).astype(bfloat)
    entry_ref[...] = entry_grad
    pooled_ref[...] = times_trans(entry_grad, project_ref[...]).astype(bfloat)


def entry_back(tokens, vectors, gain, weights, project, pair_out, mid_parts, query_parts):
    total, width = vectors.shape
    length = tokens.shape[0]
    block = min(256, total)
    triple_width = query_parts[0].shape[1] + pair_out.shape[1]
    inner = project.shape[0]

    def whole(shape):
        return pl.BlockSpec(shape, lambda at: (0, 0), pipeline_mode=pl.Buffered(1))

    def rows_of(columns):
        return pl.BlockSpec((block, columns), lambda at: (at, 0))

    return pl.pallas_call(
        entry_back_kernel,
        grid=(total // block,),
        in_specs=[
            whole((1, length)),
            rows_of(width),
            whole((1, width)),
            whole((width, triple_width)),
            whole(project.shape),
            whole(pair_out.shape),
        ]
        + [rows_of(width)] * len(mid_parts)
        + [whole(part.shape) for part in query_parts],
        out_specs=[rows_of(width), rows_of(inner)],
        out_shape=[
            jax.ShapeDtypeStruct((total, width), jnp.bfloat16),
            jax.ShapeDtypeStruct((total, inner), jnp.bfloat16),
        ],
        cost_estimate=cost(
            total * (length * triple_width + width * (inner + triple_width)),
            4 * width * (inner + triple_width) + 8 * total * width,
        ),
        compiler_params=pltpu.CompilerParams(vmem_limit_bytes=VMEM_LIMIT),
        name="entry_back",
    )(tokens[None, :], vectors, gain[None, :], weights, project, pair_out, *mid_parts, *query_parts)


def swiglu_grad_kernel(first, *refs):
    positions = (len(refs) - 3) // 3
    grads_from, weights_from = refs[:positions], refs[positions]
    outs = refs[positions + 1 : 2 * positions + 1]
    weights_ref, cots, arrived = refs[-positions - 2], refs[-positions - 1 : -1], refs[-1]
    unit_width = weights_ref.shape[1]
    copies = [
        pltpu.make_async_copy(
            weights_from.at[:, pl.ds(first, unit_width)], weights_ref, arrived.at[positions]
        )
    ]
    for at in range(positions):
        copies.append(pltpu.make_async_copy(grads_from[at], cots[at], arrived.at[at]))
    for copy in copies:
        copy.start()
    copies[0].wait()
    for at in range(positions):
        copies[at + 1].wait()
        outs[at][...] = matmul(cots[at][...], weights_ref[...])


def swiglu_products(cots, weights, first, unit_width):
    rows, width = cots[0].shape
    return pl.pallas_call(
        partial(swiglu_grad_kernel, first),
        in_specs=[pl.BlockSpec(memory_space=pl.ANY)] * (len(cots) + 1),
        out_specs=[pl.BlockSpec(memory_space=pltpu.VMEM)] * len(cots),
        out_shape=[jax.ShapeDtypeStruct((rows, unit_width), jnp.float32)] * len(cots),
        scratch_shapes=[pltpu.VMEM((width, unit_width), weights.dtype)]
        + [pltpu.VMEM((rows, width), cots[0].dtype)] * len(cots)
        + [pltpu.SemaphoreType.DMA((len(cots) + 1,))],
        cost_estimate=cost(len(cots) * rows * width * unit_width, 4 * width * unit_width),
        compiler_params=pltpu.CompilerParams(vmem_limit_bytes=VMEM_LIMIT),
        name="swiglu_products",
    )(*cots, weights)


def mlp_kernel(
    query_width,
    unit_width,
    positions,
    stacked,
    plan_ref,
    resid_in_ref,
    weight_ref,
    own_weight_ref,
    own_cot_ref,
    gain_ref,
    output_from,
    units_from,
    *refs,
):
    bfloat = jnp.bfloat16
    grads_from, mixed_refs, refs = refs[:positions], refs[positions : 2 * positions], refs[2 * positions :]
    resid_ref, swiglu_ref, mid_ref, *refs = refs
    part_refs, refs = refs[:-5], refs[-5:]
    output_ref, units_ref, swiglu_grad_ref, arrived, grad_arrived = refs
    grad_place = plan_ref[positions + pl.program_id(0)]
    for at, grad_from in enumerate(grads_from):
        copy = pltpu.make_async_copy(grad_from, swiglu_grad_ref, grad_arrived)
        pl.when(grad_place == at)(copy.start)
    gate_columns, upward_columns = [pl.ds(at * unit_width, unit_width) for at in range(2)]
    output_columns = [pl.ds(at * query_width, query_width) for at in range(positions)]
    copies = [
        pltpu.make_async_copy(
            output_from.at[:, columns], output_ref.at[:, columns], arrived.at[at]
        )
        for at, columns in enumerate(output_columns)
    ] + [
        pltpu.make_async_copy(
            units_from.at[:, columns], units_ref.at[:, columns], arrived.at[positions + at]
        )
        for at, columns in enumerate((gate_columns, upward_columns))
    ]

    def on_first(act):
        pl.when(pl.program_id(0) == 0)(act)

    @on_first
    def _():
        for copy in copies:
            copy.start()

    resid = resid_in_ref[...].astype(jnp.float32)
    for at, mixed_ref in enumerate(mixed_refs):
        on_first(copies[at].wait)
        columns = output_columns[at]
        resid = resid + times_trans(mixed_ref[...], output_ref[:, columns])
    resid_ref[...] = resid
    gain = gain_ref[...]
    spread = lax.rsqrt(jnp.mean(resid * resid, axis=1, keepdims=True) + EPS)
    normed = resid * spread
    seq_two = (normed * gain).astype(bfloat)
    on_first(copies[positions].wait)
    gate = matmul(seq_two, units_ref[:, gate_columns])
    on_first(copies[positions + 1].wait)
    upward = matmul(seq_two, units_ref[:, upward_columns])
    open_gate = jax.nn.sigmoid(gate)
    silu = gate * open_gate
    swiglu_ref[...] = (silu * upward).astype(bfloat)
    pltpu.make_async_copy(grads_from[0], swiglu_grad_ref, grad_arrived).wait()
    swiglu_grad = weight_ref[...] * swiglu_grad_ref[...]
    slope = open_gate * (1.0 + gate * (1.0 - open_gate))
    gate_grad = (swiglu_grad * upward * slope).astype(bfloat)
    upward_grad = (swiglu_grad * silu).astype(bfloat)
    grad = times_trans(gate_grad, units_ref[:, gate_columns])
    grad = grad + times_trans(upward_grad, units_ref[:, upward_columns])
    grad = grad * gain
    grad = spread * (grad - normed * jnp.mean(grad * normed, axis=1, keepdims=True))
    grad = grad + own_weight_ref[...] * own_cot_ref[...].astype(jnp.float32)
    mid_low = grad.astype(bfloat)
    mid_ref[...] = mid_low
    for at in range(positions):
        columns = output_columns[at]
        part = matmul(mid_low, output_ref[:, columns]).astype(bfloat)
        if stacked:
            part_refs[0][plan_ref[at]] = part
        else:
            part_refs[at][...] = part


def mlp(
    plan,
    block_idx,
    row_total,
    resid_in,
    weight,
    own_weight,
    own_cot,
    swiglu_grads,
    gain,
    output_w,
    units_w,
    mixed,
    stacked,
):
    width = resid_in.shape[1]
    unit_width = units_w.shape[1] // 2
    query_width = mixed[0].shape[1]
    positions = len(mixed)
    block = own_cot.shape[0]

    def rows_of(columns, first=0):
        return pl.BlockSpec((block, columns), lambda at, plan: (at + first, 0))

    first = block_idx * row_total // block
    part_shape = jax.ShapeDtypeStruct((row_total, query_width), jnp.bfloat16)
    part_specs = [rows_of(query_width)] * positions
    part_shapes = [part_shape] * positions
    if stacked:
        part_specs = [pl.BlockSpec((positions, block, query_width), lambda at, plan: (0, at, 0))]
        part_shapes = [
            jax.ShapeDtypeStruct((positions, row_total, query_width), jnp.bfloat16)
        ]

    def whole(shape):
        return pl.BlockSpec(shape, lambda at, plan: (0, 0), pipeline_mode=pl.Buffered(1))

    return pl.pallas_call(
        partial(mlp_kernel, query_width, unit_width, positions, stacked),
        grid_spec=pltpu.PrefetchScalarGridSpec(
            num_scalar_prefetch=1,
            grid=(row_total // block,),
            in_specs=[
                rows_of(width, first),
                rows_of(1, first),
                rows_of(1, first),
                whole((block, width)),
                whole((1, width)),
            ]
            + [pl.BlockSpec(memory_space=pl.ANY)] * (2 + positions)
            + [rows_of(query_width)] * positions,
            out_specs=[
                rows_of(width),
                rows_of(unit_width),
                rows_of(width),
            ]
            + part_specs,
            scratch_shapes=[
                pltpu.VMEM(output_w.shape, output_w.dtype),
                pltpu.VMEM(units_w.shape, units_w.dtype),
                pltpu.VMEM((block, unit_width), jnp.float32),
                pltpu.SemaphoreType.DMA((positions + 2,)),
                pltpu.SemaphoreType.DMA,
            ],
        ),
        out_shape=[
            jax.ShapeDtypeStruct((row_total, width), jnp.float32),
            jax.ShapeDtypeStruct((row_total, unit_width), jnp.bfloat16),
            jax.ShapeDtypeStruct((row_total, width), jnp.bfloat16),
        ]
        + part_shapes,
        cost_estimate=cost(
            row_total * width * (2 * width + 4 * unit_width),
            2 * width * (width + 2 * unit_width) + 16 * row_total * width,
        ),
        compiler_params=pltpu.CompilerParams(vmem_limit_bytes=VMEM_LIMIT),
        name="mlp",
    )(
        plan,
        resid_in,
        weight,
        own_weight,
        own_cot,
        gain[None, :],
        output_w,
        units_w,
        *swiglu_grads,
        *mixed,
    )


def centred(values):
    center = values - jnp.mean(values, axis=1, keepdims=True)
    spread = lax.rsqrt(jnp.mean(center * center, axis=1, keepdims=True) + EPS)
    return center * spread, spread


def centred_back(grad, normed, spread):
    return spread * (
        grad
        - jnp.mean(grad, axis=1, keepdims=True)
        - normed * jnp.mean(grad * normed, axis=1, keepdims=True)
    )


def slot_probs(triple_ref, rows, head, shut):
    wide = HYPER_WIDTH
    at = head * EHD
    queries = triple_ref[rows, at : at + EHD]
    keys = triple_ref[rows, wide + at : wide + at + EHD]
    values = triple_ref[rows, 2 * wide + at : 2 * wide + at + EHD]
    scores = jnp.where(shut, NEG, times_trans(keys, queries) * EHD ** (-0.5))
    parts = jnp.exp(scores - scores.max(axis=0, keepdims=True))
    return queries, keys, values, parts * (1.0 / parts.sum(axis=0, keepdims=True))


def slot_shut(open_ref, rows, count):
    key_entry = lax.broadcasted_iota(jnp.int32, (count, count), 0) // SUBWORD_SLOTS
    query_entry = lax.broadcasted_iota(jnp.int32, (count, count), 1) // SUBWORD_SLOTS
    return (key_entry != query_entry) | (open_ref[rows, :] == 0.0)


def hyper_wide_kernel(
    rows_ref,
    open_ref,
    gains_ref,
    triple_w_ref,
    merge_w_ref,
    expand_w_ref,
    reduce_w_ref,
    length_ref,
    first_ref,
    triple_ref,
    mixed_ref,
    resid_ref,
    second_ref,
    active_ref,
    slope_ref,
    pooled_ref,
):
    bfloat = jnp.bfloat16
    rows_in = rows_ref[...].astype(jnp.float32)
    first_in = (centred(rows_in)[0] * gains_ref[0:1, :]).astype(bfloat)
    first_ref[...] = first_in
    triple_ref[...] = matmul(first_in, triple_w_ref[...]).astype(bfloat)
    total = rows_in.shape[0]
    count = min(128, total)
    for first in range(0, total, count):
        rows = slice(first, first + count)
        shut = slot_shut(open_ref, rows, count)
        heads = []
        for head in range(EH):
            _, _, values, probs = slot_probs(triple_ref, rows, head, shut)
            heads.append(trans_times(values, probs.astype(bfloat)))
        mixed_ref[rows, :] = jnp.concatenate(heads, axis=0).T.astype(bfloat)
    resid_one = rows_in + matmul(mixed_ref[...], merge_w_ref[...])
    resid_ref[...] = resid_one
    second_in = (centred(resid_one)[0] * gains_ref[1:2, :]).astype(bfloat)
    second_ref[...] = second_in
    expanded = matmul(second_in, expand_w_ref[...])
    below = 0.5 * (1.0 + lax.erf(expanded * 0.5**0.5))
    active = (expanded * below).astype(bfloat)
    active_ref[...] = active
    resid_two = resid_one + matmul(active, reduce_w_ref[...])
    kept = jnp.where(open_ref[...] == 0.0, 0.0, resid_two)
    pooled = kept.reshape(total // SUBWORD_SLOTS, SUBWORD_SLOTS, kept.shape[1]).sum(axis=1)
    pooled_ref[...] = (pooled / length_ref[...]).astype(bfloat)
    bell = jnp.exp(-0.5 * expanded * expanded) * (2.0 * math.pi) ** (-0.5)
    slope_ref[...] = below + expanded * bell


def hyper_wide(rows_in, open_rows, gains, triple_w, merge_w, expand_w, reduce_w, lengths):
    total, width = rows_in.shape
    block = min(256, total)
    units = expand_w.shape[1]
    bfloat = jnp.bfloat16
    single = jnp.float32

    def rows_of(columns):
        return pl.BlockSpec((block, columns), lambda at: (at, 0))

    def whole(array):
        return pl.BlockSpec(array.shape, lambda at: (0, 0), pipeline_mode=pl.Buffered(1))

    outs = [
        (width, bfloat),
        (3 * width, bfloat),
        (width, bfloat),
        (width, single),
        (width, bfloat),
        (units, bfloat),
        (units, single),
    ]
    return pl.pallas_call(
        hyper_wide_kernel,
        grid=(total // block,),
        in_specs=[rows_of(width), rows_of(1)]
        + [whole(array) for array in (gains, triple_w, merge_w, expand_w, reduce_w)]
        + [pl.BlockSpec((block // SUBWORD_SLOTS, 1), lambda at: (at, 0))],
        out_specs=[rows_of(columns) for columns, _ in outs]
        + [pl.BlockSpec((block // SUBWORD_SLOTS, width), lambda at: (at, 0))],
        out_shape=[jax.ShapeDtypeStruct((total, columns), kind) for columns, kind in outs]
        + [jax.ShapeDtypeStruct((total // SUBWORD_SLOTS, width), bfloat)],
        cost_estimate=cost(16 * total * width * units, 12 * total * units),
        compiler_params=pltpu.CompilerParams(vmem_limit_bytes=VMEM_LIMIT),
        name="hyper_wide",
    )(rows_in, open_rows, gains, triple_w, merge_w, expand_w, reduce_w, lengths)


def hyper_back_units_kernel(
    dp_size,
    pooled_refs,
    scale_ref,
    gains_ref,
    resid_ref,
    slope_ref,
    mixed_share_ref,
    second_share_ref,
    active_share_ref,
    merge_w_ref,
    expand_w_ref,
    reduce_w_ref,
    resid_out,
    mixed_out,
    early_out,
    gains_out,
    reduce_acc,
    expand_acc,
    merge_acc,
):
    bfloat = jnp.bfloat16
    step = pl.program_id(0)
    total, width = resid_ref.shape
    pooled_grad = sum(ref[...].astype(jnp.float32) for ref in pooled_refs)
    grid_grad = jnp.broadcast_to(
        pooled_grad[:, None, :], (total // SUBWORD_SLOTS, SUBWORD_SLOTS, width)
    ).reshape(total, width)
    grid_grad = grid_grad * scale_ref[...]
    reduce_in = grid_grad.astype(bfloat)
    expand_in = times_trans(reduce_in, reduce_w_ref[...]) * slope_ref[...]
    expand_in = expand_in.astype(bfloat)
    second_grad = times_trans(expand_in, expand_w_ref[...])
    normed, spread = centred(resid_ref[...])
    gain_two = (second_grad * normed).sum(axis=0, keepdims=True)
    resid_grad = grid_grad + centred_back(second_grad * gains_ref[1:2, :], normed, spread)
    resid_out[...] = resid_grad
    merge_in = resid_grad.astype(bfloat)
    mixed_out[...] = times_trans(merge_in, merge_w_ref[...]).astype(bfloat)

    @pl.when(step == 0)
    def _():
        for ref in (reduce_acc, expand_acc, merge_acc, gains_out):
            ref[...] = jnp.zeros_like(ref)

    gains_out[0:1, :] += gain_two
    reduce_acc[...] += trans_times(active_share_ref[...], reduce_in)
    expand_acc[...] += trans_times(second_share_ref[...], expand_in)
    merge_acc[...] += trans_times(mixed_share_ref[...], merge_in)

    @pl.when(step == pl.num_programs(0) - 1)
    def _():
        depth = expand_acc.shape[0] // dp_size
        deep = reduce_acc.shape[0] // expand_acc.shape[0]
        reduced = reduce_acc[...].astype(bfloat).reshape(dp_size, deep, depth, width)
        for at in range(deep):
            early_out[:, at * width : (at + 1) * width] = reduced[:, at].reshape(
                dp_size * depth, width
            )
        units = expand_acc.shape[1]
        early_out[:, deep * width : deep * width + units] = expand_acc[...].astype(bfloat)
        early_out[:, deep * width + units :] = merge_acc[...].astype(bfloat)


def hyper_back_slots_kernel(
    resid_grad_ref,
    mixed_grad_ref,
    rows_ref,
    open_ref,
    gains_ref,
    triple_ref,
    first_share_ref,
    triple_w_ref,
    rows_out,
    late_out,
    gains_out,
    triple_acc,
    triple_in,
):
    bfloat = jnp.bfloat16
    step = pl.program_id(0)
    total, width = rows_ref.shape
    count = min(128, total)
    for first in range(0, total, count):
        rows = slice(first, first + count)
        shut = slot_shut(open_ref, rows, count)
        query_grads = []
        for head in range(EH):
            queries, keys, values, probs = slot_probs(triple_ref, rows, head, shut)
            at = head * EHD
            grad = mixed_grad_ref[rows, at : at + EHD]
            prob_grad = times_trans(values, grad)
            delta = (probs * prob_grad).sum(axis=0, keepdims=True)
            score_grad = (probs * (prob_grad - delta)).astype(bfloat)
            query_grads.append(trans_times(keys, score_grad))
            key_grad = matmul(score_grad, queries) * EHD ** (-0.5)
            value_grad = matmul(probs.astype(bfloat), grad)
            triple_in[rows, width + at : width + at + EHD] = key_grad.astype(bfloat)
            triple_in[rows, 2 * width + at : 2 * width + at + EHD] = value_grad.astype(bfloat)
        query_grad = jnp.concatenate(query_grads, axis=0).T * EHD ** (-0.5)
        triple_in[rows, :width] = query_grad.astype(bfloat)
    triple_grad = triple_in[...]
    first_grad = times_trans(triple_grad, triple_w_ref[...])
    normed, spread = centred(rows_ref[...].astype(jnp.float32))
    gain_one = (first_grad * normed).sum(axis=0, keepdims=True)
    rows_grad = resid_grad_ref[...] + centred_back(first_grad * gains_ref[0:1, :], normed, spread)
    rows_out[...] = rows_grad.astype(bfloat)

    @pl.when(step == 0)
    def _():
        triple_acc[...] = jnp.zeros_like(triple_acc)
        gains_out[...] = jnp.zeros_like(gains_out)

    gains_out[0:1, :] += gain_one
    triple_acc[...] += trans_times(first_share_ref[...], triple_grad)

    @pl.when(step == pl.num_programs(0) - 1)
    def _():
        late_out[...] = triple_acc[...].astype(bfloat)


def row_block(columns, rows):
    return pl.BlockSpec((rows, columns), lambda at: (at, 0))


def whole_block(shape):
    return pl.BlockSpec(shape, lambda at: (0, 0), pipeline_mode=pl.Buffered(1))


def hyper_back_units(dp_size, pooled, scale, gains, resid, slope, shares, weights):
    total, width = resid.shape
    block = min(256, total)
    units = slope.shape[1]
    share_width = shares[0].shape[1]
    deep = shares[2].shape[1] // share_width
    bfloat = jnp.bfloat16
    single = jnp.float32

    def kernel(*refs):
        hyper_back_units_kernel(dp_size, refs[: len(pooled)], *refs[len(pooled) :])

    early_width = deep * width + units + width
    return pl.pallas_call(
        kernel,
        grid=(total // block,),
        in_specs=[row_block(width, block // SUBWORD_SLOTS)] * len(pooled)
        + [row_block(1, block), whole_block(gains.shape)]
        + [row_block(width, block), row_block(units, block)]
        + [row_block(array.shape[1], block) for array in shares]
        + [whole_block(array.shape) for array in weights],
        out_specs=[
            row_block(width, block),
            row_block(width, block),
            pl.BlockSpec((share_width, early_width), lambda at: (0, 0)),
            pl.BlockSpec((8, width), lambda at: (0, 0)),
        ],
        out_shape=[
            jax.ShapeDtypeStruct((total, width), single),
            jax.ShapeDtypeStruct((total, width), bfloat),
            jax.ShapeDtypeStruct((share_width, early_width), bfloat),
            jax.ShapeDtypeStruct((8, width), single),
        ],
        scratch_shapes=[
            pltpu.VMEM((deep * share_width, width), single),
            pltpu.VMEM((share_width, units), single),
            pltpu.VMEM((share_width, width), single),
        ],
        cost_estimate=cost(12 * total * width * units, 6 * total * units),
        compiler_params=pltpu.CompilerParams(vmem_limit_bytes=VMEM_LIMIT),
        name="hyper_back_units",
    )(*pooled, scale, gains, resid, slope, *shares, *weights)


def hyper_back_slots(resid_grad, mixed_grad, rows_in, open_rows, gains, triple, first_share, weight):
    total, width = rows_in.shape
    block = min(256, total)
    share_width = first_share.shape[1]
    bfloat = jnp.bfloat16
    single = jnp.float32
    return pl.pallas_call(
        hyper_back_slots_kernel,
        grid=(total // block,),
        in_specs=[row_block(width, block)] * 3
        + [row_block(1, block), whole_block(gains.shape), row_block(3 * width, block)]
        + [row_block(share_width, block), whole_block(weight.shape)],
        out_specs=[
            row_block(width, block),
            pl.BlockSpec((share_width, 3 * width), lambda at: (0, 0)),
            pl.BlockSpec((8, width), lambda at: (0, 0)),
        ],
        out_shape=[
            jax.ShapeDtypeStruct((total, width), bfloat),
            jax.ShapeDtypeStruct((share_width, 3 * width), bfloat),
            jax.ShapeDtypeStruct((8, width), single),
        ],
        scratch_shapes=[
            pltpu.VMEM((share_width, 3 * width), single),
            pltpu.VMEM((block, 3 * width), bfloat),
        ],
        cost_estimate=cost(40 * total * width * width, 8 * total * width),
        compiler_params=pltpu.CompilerParams(vmem_limit_bytes=VMEM_LIMIT),
        name="hyper_back_slots",
    )(resid_grad, mixed_grad, rows_in, open_rows, gains, triple, first_share, weight)


def per_device(
    subword_embedding_rows,
    entry_subword_index,
    entry_lengths,
    entry_counts,
    encoder_triple,
    encoder_merge,
    encoder_expand,
    encoder_reduce,
    embed_project,
    normone_gain,
    normtwo_gain,
    frozen_query,
    frozen_key,
    frozen_value,
    frozen_output,
    frozen_gate,
    frozen_upward,
    frozen_downward,
    prenorm_gain,
    midnorm_gain,
    text_tokens,
    cotangent,
):
    bfloat = jnp.bfloat16
    single = jnp.float32
    dp_size = lax.axis_size("dp")
    tensor_size = lax.axis_size("tensor")
    dp_at = lax.axis_index("dp")
    tensor_at = lax.axis_index("tensor")
    device_at = dp_at * tensor_size + tensor_at
    entries = entry_subword_index.shape[0]
    entry_total = entries * dp_size * tensor_size
    flat_rows = entries * SUBWORD_SLOTS
    table_rows = subword_embedding_rows.shape[0]
    model_width = embed_project.shape[1]

    with jax.named_scope("ids"):
        packed = jnp.concatenate(
            [entry_subword_index, entry_counts[:, None], entry_lengths[:, None]], axis=1
        )
        packed_width = packed.shape[1]
        first_weights = jnp.concatenate(
            [frozen_query, frozen_key, frozen_value, frozen_downward], axis=1
        )
        packed_dp = lax.all_gather(tie(packed, first_weights), "dp", axis=0, tiled=False)
    with jax.named_scope("first_weights"):
        first_weights = lax.all_gather(first_weights, "dp", axis=0, tiled=True)
        query_width = frozen_query.shape[1]
        key_width = frozen_key.shape[1]
        triple_width = query_width + 2 * key_width
        unit_width = frozen_gate.shape[1]
        full_downward = first_weights[:, triple_width:]
        second_weights = jnp.concatenate([frozen_gate, frozen_upward], axis=1)
    with jax.named_scope("lookup"):
        local_ids = packed_dp[:, :, :SUBWORD_SLOTS].reshape(-1) - dp_at * table_rows
        inside = (local_ids >= 0) & (local_ids < table_rows)
        served = jnp.take(subword_embedding_rows, jnp.clip(local_ids, 0, table_rows - 1), axis=0)
        served = jnp.where(inside[:, None], served, jnp.zeros((), bfloat))
        served_all = lax.all_to_all(
            served.reshape(dp_size, flat_rows, HYPER_WIDTH), "dp", 0, 0, tiled=True
        )
        rows_in = jnp.sum(served_all.astype(single), axis=0)
    with jax.named_scope("cot_ring"):
        cot_blocks = [cotangent, ring(cotangent)]
        length = text_tokens.shape[0] * tensor_size
        cosine, sine = rope_lanes(length)
        cot_blocks.append(ring(cot_blocks[-1]))
        rows_in, cosine, sine, second_weights, *cot_blocks = lax.optimization_barrier(
            (rows_in, cosine, sine, second_weights, *cot_blocks)
        )
        second_weights = lax.all_gather(second_weights, "dp", axis=0, tiled=True)
        packed_all = from_all(
            tie(jnp.concatenate([packed_dp.reshape(-1), text_tokens]), cot_blocks[1])
        )
    with jax.named_scope("hyper_wide"):
        rows_blocks = from_all(rows_in.astype(bfloat))
    with jax.named_scope("hyper_wide"):
        rows_wide = jnp.concatenate(in_order(rows_blocks, tensor_at), axis=0)
        packed_all = jnp.stack(in_order(packed_all, tensor_at))
        ids_size = dp_size * entries * packed_width
        packed_ids = packed_all[:, :ids_size].reshape(tensor_size, dp_size, entries, packed_width)
        lengths_wide = lax.dynamic_index_in_dim(packed_ids, dp_at, 1, keepdims=False)
        lengths_wide = lengths_wide[:, :, SUBWORD_SLOTS + 1].reshape(-1)
        valid_wide = jnp.arange(SUBWORD_SLOTS)[None, :] < lengths_wide[:, None]
        valid_wide = valid_wide.astype(single)
        counts_wide = lengths_wide.astype(single)[:, None]
        open_wide = valid_wide.reshape(-1, 1)
        scale_wide = (valid_wide / counts_wide).reshape(-1, 1)
        gain_pair = jnp.stack([normone_gain, normtwo_gain])
        encoders = (encoder_triple, encoder_merge, encoder_expand, encoder_reduce)
        first_in, triple, mixed, resid_one, second_in, activated, slope, dp_pooled = hyper_wide(
            rows_wide, open_wide, gain_pair, *encoders, counts_wide
        )
    with jax.named_scope("output_weights"):
        output_blocks = from_all(tie(frozen_output, dp_pooled))
    with jax.named_scope("pooled_gather"):
        all_pooled = lax.all_gather(dp_pooled, "dp", axis=0, tiled=True)
    with jax.named_scope("output_weights"):
        output_weights = jnp.concatenate(output_blocks, axis=1)
        output_weights, all_pooled = lax.optimization_barrier((output_weights, all_pooled))
        output_weights = lax.all_gather(
            tie(output_weights, first_weights), "dp", axis=0, tiled=True
        )
    with jax.named_scope("cot_ring"):
        cot_blocks.append(ring(tie(cot_blocks[-1], all_pooled)))
    with jax.named_scope("entry_vectors"):
        seq_tokens = packed_all[:, ids_size:].reshape(-1)
        all_vectors, seq_triple = entry(
            seq_tokens, all_pooled, embed_project, prenorm_gain, first_weights, triple_width
        )

    with jax.named_scope("attention_fwd"):
        block_rows = min(512, length)
        block_total = length // block_rows
        first_mixed, first_totals = attention(
            seq_triple, cosine, sine, query_width, 0, block_rows
        )

    with jax.named_scope("mlp_rows"):
        late_ids, late_tokens = tie_all(first_mixed, packed_ids, seq_tokens)
        late_ids = late_ids.transpose(1, 0, 2, 3).reshape(entry_total, packed_width)
        all_ids = late_ids[:, :SUBWORD_SLOTS].reshape(-1)
        all_weights = (1.0 / jnp.log(1.0 + late_ids[:, SUBWORD_SLOTS].astype(single))).astype(
            bfloat
        )
        rows_here = text_tokens.shape[0]
        seq_hot = (late_tokens[:, None] == jnp.arange(entry_total)[None, :]).astype(bfloat)
        seq_weight = matmul(seq_hot, all_weights[:, None])
        own_rows_here = jnp.arange(length) // rows_here == tensor_at
        own_weight = jnp.where(own_rows_here[:, None], seq_weight, 0.0)
        resid_in = matmul(seq_hot, all_vectors).astype(bfloat)
        per_block = block_rows // rows_here
        vectors = lax.dynamic_slice_in_dim(all_vectors, device_at * entries, entries, 0)

    with jax.named_scope("attention_fwd"):
        seq_triple = tie(seq_triple, resid_in)
        mixed_parts = [[first_mixed]]
        for first in range(block_rows, length, block_rows):
            lm_mixed, last_totals = attention(
                seq_triple, cosine, sine, query_width, first, block_rows
            )
            mixed_parts.append([lm_mixed])
    with jax.named_scope("mixed_ring"):
        for block_idx, parts in enumerate(mixed_parts):
            last_part = ring(parts[0], tensor_size - 1)
            parts.append(ring(parts[0]))
            for step in range(2, tensor_size - 1):
                parts.append(ring(parts[-1]))
            parts.append(last_part)

    def share_slice(values):
        rows, width = values.shape
        split = values.reshape(rows, dp_size, tensor_size, width // (dp_size * tensor_size))
        return lax.dynamic_index_in_dim(split, tensor_at, 2, keepdims=False).reshape(
            rows, width // tensor_size
        )

    def share(values, position):
        width = values.shape[1]
        depth = width // (dp_size * tensor_size)
        row = lax.broadcasted_iota(jnp.int32, (width, width // tensor_size), 0)
        column = lax.broadcasted_iota(jnp.int32, (width, width // tensor_size), 1)
        held = (column // depth * tensor_size + position) * depth + column % depth
        return matmul(values, (row == held).astype(bfloat)).astype(bfloat)

    with jax.named_scope("swiglu_grad"):
        late_cots = tie(cot_blocks, lm_mixed, mixed_parts[0][1])
        swiglu_grads = swiglu_products(late_cots, first_weights, triple_width, unit_width)

    with jax.named_scope("mlp"):
        places = lax.rem(tensor_at + tensor_size - jnp.arange(tensor_size), tensor_size)
        resid_blocks = []
        layer_parts = []
        mid_parts = []
        mixed_grads = []
        for block_idx, parts in enumerate(mixed_parts):
            last = block_idx == block_total - 1
            rows = slice(block_idx * block_rows, (block_idx + 1) * block_rows)
            if block_idx == 0:
                near = [[later[1], later[-1]] for later in mixed_parts[1:]]
                late_core = tie(lax.rem(dp_at, 2), lm_mixed)
                pooled_pairs = all_pooled.reshape(entry_total, dp_size // 2, 2, -1)
                pooled_kept, pooled_sent = [
                    lax.dynamic_index_in_dim(pooled_pairs, at, 2, keepdims=False).reshape(
                        entry_total, -1
                    )
                    for at in (late_core, 1 - late_core)
                ]
                parts, near, pooled_kept, pooled_sent = lax.optimization_barrier(
                    (parts, near, pooled_kept, pooled_sent)
                )
                for later, (below, above) in zip(mixed_parts[1:], near):
                    later[1], later[-1] = below, above
                    for step in range(2, tensor_size - 1):
                        later[step] = ring(later[step - 1])
            else:
                parts, layer_parts, mid_parts = lax.optimization_barrier(
                    (parts, layer_parts, mid_parts)
                )
            block_places = block_idx * per_block + jnp.arange(per_block)
            block_places = lax.rem(tensor_at + tensor_size - block_places, tensor_size)
            resid_mid, swiglu_low, mid_low, *mixed_part = mlp(
                jnp.concatenate([places, block_places]),
                block_idx,
                block_rows,
                resid_in,
                seq_weight,
                own_weight,
                cotangent,
                swiglu_grads,
                midnorm_gain,
                output_weights,
                second_weights,
                parts,
                not last,
            )
            resid_blocks.append(resid_mid)
            if not last:
                mixed_grads.append(
                    lax.psum_scatter(
                        mixed_part[0].reshape(-1, query_width),
                        "tensor",
                        scatter_dimension=0,
                        tiled=True,
                    )
                )
                layer_parts.append(times_trans(swiglu_low, full_downward).astype(bfloat))
                mid_parts.append(trans_times(seq_hot[rows], mid_low))
                continue
            carried = None
            for step in [*range(1, tensor_size), 0]:
                part = mixed_part[step]
                if step == 2:
                    mid_parts.append(trans_times(seq_hot[rows], mid_low))
                    carried, mid_parts = lax.optimization_barrier((carried, mid_parts))
                    swiglu_low = tie(swiglu_low, carried)
                if step == 3:
                    layer_parts.append(times_trans(swiglu_low, full_downward).astype(bfloat))
                    late_position = tie(tensor_at, mid_parts)
                    shares = [
                        share_slice(array) for array in (first_in, mixed, second_in)
                    ] + [share(activated, late_position)]
                    layer_cut = model_width // 2
                    layer_halves = [
                        jnp.concatenate([part[:, columns] for part in layer_parts], axis=0)
                        for columns in (slice(None, layer_cut), slice(layer_cut, None))
                    ]
                    carried, layer_halves, shares = lax.optimization_barrier(
                        (carried, layer_halves, shares)
                    )
                if step == 0:
                    pair_out = None
                    query_parts = []
                    for at, mixed_grad in enumerate(mixed_grads):
                        query_part, pair_out = attention_back(
                            seq_triple,
                            cosine,
                            sine,
                            mixed_grad,
                            first_mixed,
                            first_totals,
                            at * block_rows,
                            pair_out,
                        )
                        query_parts.append(query_part)
                    carried, pair_out = lax.optimization_barrier((carried, pair_out))
                if carried is not None:
                    part = (part.astype(single) + carried.astype(single)).astype(bfloat)
                if step > 0:
                    carried = ring(part)
            last_grad = part

    with jax.named_scope("layer_out"):
        layer_near, layer_far = layer_halves
        layer_near = lax.psum_scatter(
            tie(layer_near, last_grad), "tensor", scatter_dimension=0, tiled=True
        )
        blocks_of = [
            lax.dynamic_slice_in_dim(
                block, lax.rem(tensor_at * rows_here, block_rows), rows_here, 0
            )
            for block in resid_blocks
        ]
        resid_own = blocks_of[0]
        for block_idx in range(1, block_total):
            resid_own = jnp.where(
                tensor_at * rows_here // block_rows == block_idx, blocks_of[block_idx], resid_own
            )
    with jax.named_scope("attention_bwd"):
        query_part, pair_out = attention_back(
            seq_triple,
            cosine,
            sine,
            last_grad,
            lm_mixed,
            last_totals,
            length - block_rows,
            pair_out,
        )
        query_parts.append(query_part)

    with jax.named_scope("entry_bwd"):
        entry_part, pooled_part = entry_back(
            seq_tokens,
            all_vectors,
            prenorm_gain,
            first_weights,
            embed_project,
            pair_out,
            mid_parts,
            query_parts,
        )
        project_sent = trans_times(pooled_sent, entry_part).astype(bfloat)
        project_kept = trans_times(pooled_kept, entry_part)
        project_sent = lax.ppermute(project_sent, "dp", [(i, i ^ 1) for i in range(dp_size)])
        project_part = (project_kept + project_sent.astype(single)).astype(bfloat)
        pooled_shares, project_part = lax.optimization_barrier(
            (to_owners(pooled_part), project_part)
        )
        pooled_part = jnp.sum(pooled_shares.astype(single), axis=0).astype(bfloat)
        pooled_grads = from_all(pooled_part)

    with jax.named_scope("hyper_bwd"):
        project_shares = lax.all_to_all(
            project_part.reshape(dp_size // 2, -1, model_width),
            "dp",
            0,
            0,
            axis_index_groups=[list(range(first, dp_size, 2)) for first in range(2)],
            tiled=True,
        )
    with jax.named_scope("layer_out"):
        layer_far = lax.psum_scatter(
            tie(layer_far, pooled_grads, layer_near), "tensor", scatter_dimension=0, tiled=True
        )
        layer_final = resid_own + jnp.concatenate([layer_near, layer_far], axis=1).astype(single)
    with jax.named_scope("hyper_bwd"):
        resid_grad, mixed_grad, early, gain_two = hyper_back_units(
            dp_size,
            pooled_grads,
            scale_wide,
            gain_pair,
            resid_one,
            slope,
            shares[1:],
            encoders[1:],
        )
        resid_grad, early, project_shares = lax.optimization_barrier(
            (resid_grad, early, project_shares)
        )
        early = to_owners(early)
        rows_low, late, gain_one = hyper_back_slots(
            resid_grad,
            mixed_grad,
            rows_wide,
            open_wide,
            gain_pair,
            triple,
            shares[0],
            encoder_triple,
        )

    with jax.named_scope("grads_out"):
        rows_low, early, project_shares = lax.optimization_barrier(
            (rows_low, early, project_shares)
        )
        early = jnp.sum(early.astype(single), axis=0)
        project_grad = jnp.sum(project_shares.astype(single), axis=0).astype(bfloat)
        all_rows = lax.all_gather(rows_low, "dp", axis=0, tiled=True)
        late, project_grad = tie_all(rows_low, late, project_grad)
        project_grad = project_grad.reshape(tensor_size, -1, model_width)
        project_grad = lax.all_to_all(project_grad, "tensor", 0, 0, tiled=True)
        project_grad = jnp.sum(project_grad.astype(single), axis=0)
        own_rows = table_rows // tensor_size
        row_hot = (
            (jnp.arange(own_rows) + device_at * own_rows)[:, None] == all_ids[None, :]
        ).astype(bfloat)
        subword_grad = matmul(row_hot, all_rows)

        gain_grads = jnp.concatenate([gain_one[:1], gain_two[:1]], axis=0)
        gain_grads = gain_grads.reshape(2, dp_size, tensor_size, -1)
        gain_grads = lax.dynamic_index_in_dim(gain_grads, tensor_at, 2, keepdims=False)
        gain_grads = gain_grads.reshape(2, -1).transpose(1, 0).astype(bfloat)
        late = jnp.concatenate([late, jnp.pad(gain_grads, ((0, 0), (0, 126)))], axis=1)
        late = scatter_dp(late)
        depth = early.shape[0]
        deep = encoder_reduce.shape[0] // HYPER_WIDTH
        reduce_width = deep * HYPER_WIDTH
        expand_width = encoder_expand.shape[1]
        reduce_grad = early[:, :reduce_width].reshape(depth, deep, HYPER_WIDTH)
        reduce_grad = reduce_grad.transpose(1, 0, 2).reshape(deep * depth, HYPER_WIDTH)
        expand_grad = early[:, reduce_width : reduce_width + expand_width]
        merge_grad = early[:, reduce_width + expand_width :]
        grad_width = encoder_triple.shape[1]
    return (
        layer_final.astype(bfloat),
        vectors,
        subword_grad,
        late[:, :grad_width],
        merge_grad,
        expand_grad,
        reduce_grad,
        project_grad,
        late[:, grad_width],
        late[:, grad_width + 1],
    )


def solution(mesh):
    return jax.shard_map(
        per_device,
        mesh=mesh,
        in_specs=(
            P("dp", None),
            P(("dp", "tensor"), None),
            P(("dp", "tensor")),
            P(("dp", "tensor")),
            P(),
            P(),
            P(),
            P(),
            P(),
            P(),
            P(),
            P("dp", "tensor"),
            P("dp", "tensor"),
            P("dp", "tensor"),
            P("dp", "tensor"),
            P("dp", "tensor"),
            P("dp", "tensor"),
            P("dp", "tensor"),
            P(),
            P(),
            P(("dp", "tensor")),
            P(("dp", "tensor"), None),
        ),
        out_specs=(
            P(("dp", "tensor"), None),
            P(("dp", "tensor"), None),
            P(("dp", "tensor"), None),
            P(("dp", "tensor"), None),
            P(("dp", "tensor"), None),
            P(("dp", "tensor"), None),
            P(("dp", "tensor"), None),
            P(("dp", "tensor"), None),
            P(("dp", "tensor")),
            P(("dp", "tensor")),
        ),
        check_vma=False,
    )
```

```python
import math
from functools import partial

import jax
import jax.numpy as jnp
from jax import lax
from jax.experimental import pallas as pl
from jax.experimental.pallas import tpu as pltpu
from jax.sharding import PartitionSpec as P

HD = 64
HYPER_WIDTH = 512
EH = 8
EHD = 64
SUBWORD_SLOTS = 8


NEG = -1000000000.0
EPS = 1e-05
THETA = 10000.0
VMEM_LIMIT = 62 * 1024 * 1024


def layer_norm(values, gain):
    center = values - jnp.mean(values, axis=-1, keepdims=True)
    spread = jnp.mean(center * center, axis=-1, keepdims=True)
    return center * lax.rsqrt(spread + EPS) * gain


def rms_norm(values, gain):
    return values * lax.rsqrt(jnp.mean(values * values, axis=-1, keepdims=True) + EPS) * gain


def rope_tables(length, width):
    half_width = width // 2
    inverse = THETA ** (-(2.0 * jnp.arange(half_width, dtype=jnp.float32)) / width)
    angles = jnp.arange(length, dtype=jnp.float32)[:, None] * inverse[None, :]
    return (jnp.cos(angles), jnp.sin(angles))


def rotate(values, cosine, sine):
    half_width = values.shape[-1] // 2
    former = values[..., :half_width]
    latter = values[..., half_width:]
    return jnp.concatenate(
        [former * cosine - latter * sine, latter * cosine + former * sine], axis=-1
    )


def matmul(left, right):
    return jnp.dot(left, right, preferred_element_type=jnp.float32)


def times_trans(left, right):
    return lax.dot_general(
        left, right, (((1,), (1,)), ((), ())), preferred_element_type=jnp.float32
    )


def trans_times(left, right):
    return lax.dot_general(
        left, right, (((0,), (0,)), ((), ())), preferred_element_type=jnp.float32
    )


def ring(values, shift=1):
    size = lax.axis_size("tensor")
    return lax.ppermute(values, "tensor", [(i, (i + shift) % size) for i in range(size)])


def tie(values, *others):
    return lax.optimization_barrier((values, *others))[0]


def tie_all(first, *values):
    return lax.optimization_barrier((*values, first))[:-1]


def in_order(blocks, first):
    size = len(blocks)
    stacked = jnp.stack(blocks)
    return [
        lax.dynamic_index_in_dim(stacked, lax.rem(first - at + size, size), 0, keepdims=False)
        for at in range(size)
    ]


def to_owners(values):
    size = lax.axis_size("dp")
    blocks = values.reshape(size, values.shape[0] // size, values.shape[1])
    return lax.all_to_all(blocks, "dp", 0, 0, tiled=True)


def scatter_dp(values):
    return jnp.sum(to_owners(values).astype(jnp.float32), axis=0)


def from_all(values):
    return [values] + [ring(values, shift) for shift in range(1, lax.axis_size("tensor"))]


def cost(multiplies, values, transcendentals=0):
    return pl.CostEstimate(
        flops=2 * multiplies, bytes_accessed=values, transcendentals=transcendentals
    )


def rope_lanes(length):
    cosine, sine = rope_tables(length, HD)
    return (
        jnp.concatenate([cosine] * 4, axis=1),
        jnp.concatenate([-sine, sine, -sine, sine], axis=1),
    )


def swap(values):
    width = values.shape[1]
    lane = lax.broadcasted_iota(jnp.int32, values.shape, 1)
    ahead = pltpu.roll(values, width - HD // 2, 1)
    behind = pltpu.roll(values, HD // 2, 1)
    return jnp.where(lane % HD < HD // 2, ahead, behind)


def attention_operands(query_ref, pair_ref, cos_ref, sin_ref):
    bfloat = jnp.bfloat16
    cosine = cos_ref[...]
    sine = sin_ref[...]
    queries = query_ref[...]
    pair = pair_ref[...]
    queries = (queries * cosine + swap(queries) * sine).astype(bfloat)
    queries = queries * jnp.asarray(HD ** (-0.5), bfloat)
    keys = (pair * cosine + swap(pair) * sine).astype(bfloat)[:, :HD]
    return queries, keys, pair.astype(bfloat)[:, HD:]


def scores_by_key(keys, query_block, first):
    rows = query_block.shape[0]
    own = times_trans(keys[first : first + rows], query_block)
    key_at = lax.broadcasted_iota(jnp.int32, own.shape, 0)
    query_at = lax.broadcasted_iota(jnp.int32, own.shape, 1)
    parts = [jnp.where(query_at >= key_at, own, NEG)]
    if first > 0:
        parts.insert(0, times_trans(keys[:first], query_block))
    return parts


def attention_kernel(
    block_rows, base, query_ref, pair_ref, cos_ref, sin_ref, out_ref, total_ref
):
    queries, keys, values = attention_operands(query_ref, pair_ref, cos_ref, sin_ref)
    for first in range(base, queries.shape[0], block_rows):
        rows = slice(first, first + block_rows)
        heads = []
        for head in range(queries.shape[1] // HD):
            query_block = queries[rows, head * HD : (head + 1) * HD]
            parts = scores_by_key(keys, query_block, first)
            largest = parts[0].max(axis=0, keepdims=True)
            for part in parts[1:]:
                largest = jnp.maximum(largest, part.max(axis=0, keepdims=True))
            parts = [jnp.exp(part - largest) for part in parts]
            total = sum(part.sum(axis=0, keepdims=True) for part in parts)
            at = 0
            mixed = None
            for part in parts:
                here = trans_times(values[at : at + part.shape[0]], part.astype(jnp.bfloat16))
                mixed = here if mixed is None else mixed + here
                at += part.shape[0]
            mixed = mixed * (1.0 / total)
            out_rows = slice(first - base, first - base + block_rows)
            total_ref[0, head : head + 1, out_rows] = largest + jnp.log(total)
            heads.append(mixed)
        out_ref[out_rows, :] = jnp.concatenate(heads, axis=0).T.astype(jnp.bfloat16)


def attention_back_kernel(
    block_rows, base, query_ref, pair_ref, cos_ref, sin_ref, grad_ref, mixed_ref, total_ref, add_ref, query_out, pair_out, acc_ref
):
    bfloat = jnp.bfloat16
    queries, keys, values = attention_operands(query_ref, pair_ref, cos_ref, sin_ref)

    @pl.when(pl.program_id(0) == 0)
    def _():
        acc_ref[...] = jnp.zeros_like(acc_ref) if add_ref is None else add_ref[...]

    for first in range(base, queries.shape[0], block_rows):
        rows = slice(first, first + block_rows)
        out_rows = slice(first - base, first - base + block_rows)
        deltas = mixed_ref[out_rows, :].astype(jnp.float32) * grad_ref[out_rows, :].astype(
            jnp.float32
        )
        deltas = deltas.T
        heads = []
        for head in range(queries.shape[1] // HD):
            lanes = slice(head * HD, (head + 1) * HD)
            query_block = queries[rows, lanes]
            grad_block = grad_ref[out_rows, lanes]
            parts = scores_by_key(keys, query_block, first)
            row_total = total_ref[0, head : head + 1, out_rows]
            parts = [jnp.exp(part - row_total) for part in parts]
            delta = deltas[head * HD : (head + 1) * HD].sum(axis=0, keepdims=True)
            at = 0
            prob_grads = []
            for part in parts:
                prob_grads.append(times_trans(values[at : at + part.shape[0]], grad_block))
                at += part.shape[0]
            at = 0
            query_grad = None
            for part, prob_grad in zip(parts, prob_grads):
                here = slice(at, at + part.shape[0])
                score_grad = (part * (prob_grad - delta)).astype(bfloat)
                key_part = matmul(score_grad, query_block)
                value_part = matmul(part.astype(bfloat), grad_block)
                acc_ref[here, :] += jnp.concatenate([key_part, value_part], axis=1)
                query_part = trans_times(keys[here], score_grad)
                query_grad = query_part if query_grad is None else query_grad + query_part
                at += part.shape[0]
            heads.append(query_grad)
        grad = jnp.concatenate(heads, axis=0).T * HD ** (-0.5)
        grad = grad * cos_ref[rows, :] - swap(grad) * sin_ref[rows, :]
        query_out[out_rows, :] = grad.astype(bfloat)

    @pl.when(pl.program_id(0) == pl.num_programs(0) - 1)
    def _():
        total = acc_ref[...]
        if pair_out.dtype == jnp.float32:
            pair_out[...] = jnp.zeros_like(pair_out)
            pair_out[: total.shape[0], :] = total
            return
        turned = total * cos_ref[...] - swap(total) * sin_ref[...]
        lane = lax.broadcasted_iota(jnp.int32, total.shape, 1)
        pair_out[...] = jnp.where(lane < HD, turned, total).astype(bfloat)


def attention(seq_triple, cosine, sine, query_width, base, rows):
    pairs = query_width // (2 * HD)
    wide = 2 * HD
    keys = base + rows
    return pl.pallas_call(
        partial(attention_kernel, min(256, rows), base),
        grid=(pairs,),
        in_specs=[
            pl.BlockSpec((keys, wide), lambda at: (0, at)),
            pl.BlockSpec((keys, wide), lambda at: (0, pairs)),
            pl.BlockSpec((keys, wide), lambda at: (0, 0)),
            pl.BlockSpec((keys, wide), lambda at: (0, 0)),
        ],
        out_specs=[
            pl.BlockSpec((rows, wide), lambda at: (0, at)),
            pl.BlockSpec((1, 8, rows), lambda at: (at, 0, 0)),
        ],
        out_shape=[
            jax.ShapeDtypeStruct((rows, query_width), jnp.bfloat16),
            jax.ShapeDtypeStruct((pairs, 8, rows), jnp.float32),
        ],
        cost_estimate=cost(
            8 * query_width * rows * keys, 6 * query_width * keys, query_width * keys * 10
        ),
        compiler_params=pltpu.CompilerParams(vmem_limit_bytes=VMEM_LIMIT),
        name="attention",
    )(seq_triple, seq_triple, cosine, sine)


def attention_back(seq_triple, cosine, sine, mixed_grad, mixed, totals, base, before):
    length = seq_triple.shape[0]
    rows, query_width = mixed_grad.shape
    pairs = query_width // (2 * HD)
    wide = 2 * HD
    keys = base + rows
    last = keys == length
    specs = [
        pl.BlockSpec((keys, wide), lambda at: (0, at)),
        pl.BlockSpec((keys, wide), lambda at: (0, pairs)),
        pl.BlockSpec((keys, wide), lambda at: (0, 0)),
        pl.BlockSpec((keys, wide), lambda at: (0, 0)),
        pl.BlockSpec((rows, wide), lambda at: (0, at)),
        pl.BlockSpec((rows, wide), lambda at: (0, at)),
        pl.BlockSpec((1, 8, rows), lambda at: (at, 0, 0)),
    ]
    operands = [seq_triple, seq_triple, cosine, sine, mixed_grad, mixed, totals]
    if before is not None:
        specs.append(pl.BlockSpec((keys, wide), lambda at: (0, 0)))
        operands.append(before)

    def kernel(*refs):
        given = refs[: len(operands)]
        add_ref = None if before is None else given[-1]
        attention_back_kernel(
            min(256, rows), base, *given[:7], add_ref, *refs[len(operands) :]
        )

    return pl.pallas_call(
        kernel,
        grid=(pairs,),
        in_specs=specs,
        out_specs=[
            pl.BlockSpec((rows, wide), lambda at: (0, at)),
            pl.BlockSpec((length, wide), lambda at: (0, 0)),
        ],
        out_shape=[
            jax.ShapeDtypeStruct((rows, query_width), jnp.bfloat16),
            jax.ShapeDtypeStruct((length, wide), jnp.bfloat16 if last else jnp.float32),
        ],
        cost_estimate=cost(
            20 * query_width * rows * keys, 8 * query_width * length, query_width * keys * 10
        ),
        scratch_shapes=[pltpu.VMEM((keys, wide), jnp.float32)],
        compiler_params=pltpu.CompilerParams(vmem_limit_bytes=VMEM_LIMIT),
        name="attention_back",
    )(*operands)


def unit_scale(values):
    spread = lax.rsqrt(jnp.mean(values * values, axis=1, keepdims=True) + EPS)
    return values * spread, spread


def one_hot(places, first, shape, axis):
    at = lax.broadcasted_iota(jnp.int32, shape, axis) + first
    return jnp.where(places == at, 1.0, 0.0).astype(jnp.bfloat16)


def entry_kernel(
    tokens_ref, pooled_ref, project_ref, gain_ref, triple_w_ref, vectors_ref, seq_ref
):
    bfloat = jnp.bfloat16
    step = pl.program_id(0)
    vectors = matmul(pooled_ref[...], project_ref[...]).astype(bfloat)
    vectors_ref[...] = vectors
    normed, _ = unit_scale(vectors.astype(jnp.float32))
    triple = matmul((normed * gain_ref[...]).astype(bfloat), triple_w_ref[...])
    high = triple.astype(bfloat)
    rest = (triple - high.astype(jnp.float32)).astype(bfloat)
    count = vectors.shape[0]
    hot = one_hot(tokens_ref[...], step * count, (seq_ref.shape[0], count), 1)
    picked = matmul(hot, high) + matmul(hot, rest)

    @pl.when(step == 0)
    def _():
        seq_ref[...] = picked

    @pl.when(step > 0)
    def _():
        seq_ref[...] += picked


def entry(tokens, pooled, project, gain, weights, triple_width):
    total, inner = pooled.shape
    length = tokens.shape[0]
    width = project.shape[1]
    block = min(512, total)

    def whole(shape):
        return pl.BlockSpec(shape, lambda at: (0, 0), pipeline_mode=pl.Buffered(1))

    return pl.pallas_call(
        entry_kernel,
        grid=(total // block,),
        in_specs=[
            whole((length, 1)),
            pl.BlockSpec((block, inner), lambda at: (at, 0)),
            whole(project.shape),
            whole((1, width)),
            whole((width, triple_width)),
        ],
        out_specs=[
            pl.BlockSpec((block, width), lambda at: (at, 0)),
            pl.BlockSpec((length, triple_width), lambda at: (0, 0)),
        ],
        out_shape=[
            jax.ShapeDtypeStruct((total, width), jnp.bfloat16),
            jax.ShapeDtypeStruct((length, triple_width), jnp.float32),
        ],
        cost_estimate=cost(
            total * width * (inner + triple_width) + 2 * length * total * triple_width,
            4 * width * (inner + triple_width),
        ),
        compiler_params=pltpu.CompilerParams(vmem_limit_bytes=VMEM_LIMIT),
        name="entry",
    )(tokens[:, None], pooled, project, gain[None, :], weights)


def entry_back_kernel(
    tokens_ref,
    vectors_ref,
    gain_ref,
    triple_w_ref,
    project_ref,
    pair_ref,
    *refs,
):
    bfloat = jnp.bfloat16
    half = (len(refs) - 2) // 2
    mid_refs, query_refs = refs[:half], refs[half:-2]
    entry_ref, pooled_ref = refs[-2:]
    count = vectors_ref.shape[0]
    length = tokens_ref.shape[1]
    hot = one_hot(tokens_ref[...], pl.program_id(0) * count, (count, length), 0)
    at = 0
    query_out = None
    for ref in query_refs:
        here = matmul(hot[:, at : at + ref.shape[0]], ref[...])
        query_out = here if query_out is None else query_out + here
        at += ref.shape[0]
    pair_out = matmul(hot, pair_ref[...])
    query_width = query_out.shape[1]
    grad = times_trans(query_out.astype(bfloat), triple_w_ref[:, :query_width])
    grad = grad + times_trans(pair_out.astype(bfloat), triple_w_ref[:, query_width:])
    grad = grad * gain_ref[...]
    normed, spread = unit_scale(vectors_ref[...].astype(jnp.float32))
    grad = spread * (grad - normed * jnp.mean(grad * normed, axis=1, keepdims=True))
    entry_grad = (grad + sum(ref[...].astype(jnp.float32) for ref in mid_refs)).astype(bfloat)
    entry_ref[...] = entry_grad
    pooled_ref[...] = times_trans(entry_grad, project_ref[...]).astype(bfloat)


def entry_back(tokens, vectors, gain, weights, project, pair_out, mid_parts, query_parts):
    total, width = vectors.shape
    length = tokens.shape[0]
    block = min(256, total)
    triple_width = query_parts[0].shape[1] + pair_out.shape[1]
    inner = project.shape[0]

    def whole(shape):
        return pl.BlockSpec(shape, lambda at: (0, 0), pipeline_mode=pl.Buffered(1))

    def rows_of(columns):
        return pl.BlockSpec((block, columns), lambda at: (at, 0))

    return pl.pallas_call(
        entry_back_kernel,
        grid=(total // block,),
        in_specs=[
            whole((1, length)),
            rows_of(width),
            whole((1, width)),
            whole((width, triple_width)),
            whole(project.shape),
            whole(pair_out.shape),
        ]
        + [rows_of(width)] * len(mid_parts)
        + [whole(part.shape) for part in query_parts],
        out_specs=[rows_of(width), rows_of(inner)],
        out_shape=[
            jax.ShapeDtypeStruct((total, width), jnp.bfloat16),
            jax.ShapeDtypeStruct((total, inner), jnp.bfloat16),
        ],
        cost_estimate=cost(
            total * (length * triple_width + width * (inner + triple_width)),
            4 * width * (inner + triple_width) + 8 * total * width,
        ),
        compiler_params=pltpu.CompilerParams(vmem_limit_bytes=VMEM_LIMIT),
        name="entry_back",
    )(tokens[None, :], vectors, gain[None, :], weights, project, pair_out, *mid_parts, *query_parts)


def swiglu_grad_kernel(first, *refs):
    positions = (len(refs) - 3) // 3
    grads_from, weights_from = refs[:positions], refs[positions]
    outs = refs[positions + 1 : 2 * positions + 1]
    weights_ref, cots, arrived = refs[-positions - 2], refs[-positions - 1 : -1], refs[-1]
    unit_width = weights_ref.shape[1]
    copies = [
        pltpu.make_async_copy(
            weights_from.at[:, pl.ds(first, unit_width)], weights_ref, arrived.at[positions]
        )
    ]
    for at in range(positions):
        copies.append(pltpu.make_async_copy(grads_from[at], cots[at], arrived.at[at]))
    for copy in copies:
        copy.start()
    copies[0].wait()
    for at in range(positions):
        copies[at + 1].wait()
        outs[at][...] = matmul(cots[at][...], weights_ref[...])


def swiglu_products(cots, weights, first, unit_width):
    rows, width = cots[0].shape
    return pl.pallas_call(
        partial(swiglu_grad_kernel, first),
        in_specs=[pl.BlockSpec(memory_space=pl.ANY)] * (len(cots) + 1),
        out_specs=[pl.BlockSpec(memory_space=pltpu.VMEM)] * len(cots),
        out_shape=[jax.ShapeDtypeStruct((rows, unit_width), jnp.float32)] * len(cots),
        scratch_shapes=[pltpu.VMEM((width, unit_width), weights.dtype)]
        + [pltpu.VMEM((rows, width), cots[0].dtype)] * len(cots)
        + [pltpu.SemaphoreType.DMA((len(cots) + 1,))],
        cost_estimate=cost(len(cots) * rows * width * unit_width, 4 * width * unit_width),
        compiler_params=pltpu.CompilerParams(vmem_limit_bytes=VMEM_LIMIT),
        name="swiglu_products",
    )(*cots, weights)


def mlp_kernel(
    query_width,
    unit_width,
    positions,
    stacked,
    plan_ref,
    resid_in_ref,
    weight_ref,
    own_weight_ref,
    own_cot_ref,
    gain_ref,
    output_from,
    units_from,
    *refs,
):
    bfloat = jnp.bfloat16
    grads_from, mixed_refs, refs = refs[:positions], refs[positions : 2 * positions], refs[2 * positions :]
    resid_ref, swiglu_ref, mid_ref, *refs = refs
    part_refs, refs = refs[:-5], refs[-5:]
    output_ref, units_ref, swiglu_grad_ref, arrived, grad_arrived = refs
    grad_place = plan_ref[positions + pl.program_id(0)]
    for at, grad_from in enumerate(grads_from):
        copy = pltpu.make_async_copy(grad_from, swiglu_grad_ref, grad_arrived)
        pl.when(grad_place == at)(copy.start)
    gate_columns, upward_columns = [pl.ds(at * unit_width, unit_width) for at in range(2)]
    output_columns = [pl.ds(at * query_width, query_width) for at in range(positions)]
    copies = [
        pltpu.make_async_copy(
            output_from.at[:, columns], output_ref.at[:, columns], arrived.at[at]
        )
        for at, columns in enumerate(output_columns)
    ] + [
        pltpu.make_async_copy(
            units_from.at[:, columns], units_ref.at[:, columns], arrived.at[positions + at]
        )
        for at, columns in enumerate((gate_columns, upward_columns))
    ]

    def on_first(act):
        pl.when(pl.program_id(0) == 0)(act)

    @on_first
    def _():
        for copy in copies:
            copy.start()

    resid = resid_in_ref[...].astype(jnp.float32)
    for at, mixed_ref in enumerate(mixed_refs):
        on_first(copies[at].wait)
        columns = output_columns[at]
        resid = resid + times_trans(mixed_ref[...], output_ref[:, columns])
    resid_ref[...] = resid
    gain = gain_ref[...]
    spread = lax.rsqrt(jnp.mean(resid * resid, axis=1, keepdims=True) + EPS)
    normed = resid * spread
    seq_two = (normed * gain).astype(bfloat)
    on_first(copies[positions].wait)
    gate = matmul(seq_two, units_ref[:, gate_columns])
    on_first(copies[positions + 1].wait)
    upward = matmul(seq_two, units_ref[:, upward_columns])
    open_gate = jax.nn.sigmoid(gate)
    silu = gate * open_gate
    swiglu_ref[...] = (silu * upward).astype(bfloat)
    pltpu.make_async_copy(grads_from[0], swiglu_grad_ref, grad_arrived).wait()
    swiglu_grad = weight_ref[...] * swiglu_grad_ref[...]
    slope = open_gate * (1.0 + gate * (1.0 - open_gate))
    gate_grad = (swiglu_grad * upward * slope).astype(bfloat)
    upward_grad = (swiglu_grad * silu).astype(bfloat)
    grad = times_trans(gate_grad, units_ref[:, gate_columns])
    grad = grad + times_trans(upward_grad, units_ref[:, upward_columns])
    grad = grad * gain
    grad = spread * (grad - normed * jnp.mean(grad * normed, axis=1, keepdims=True))
    grad = grad + own_weight_ref[...] * own_cot_ref[...].astype(jnp.float32)
    mid_low = grad.astype(bfloat)
    mid_ref[...] = mid_low
    for at in range(positions):
        columns = output_columns[at]
        part = matmul(mid_low, output_ref[:, columns]).astype(bfloat)
        if stacked:
            part_refs[0][plan_ref[at]] = part
        else:
            part_refs[at][...] = part


def mlp(
    plan,
    block_idx,
    row_total,
    resid_in,
    weight,
    own_weight,
    own_cot,
    swiglu_grads,
    gain,
    output_w,
    units_w,
    mixed,
    stacked,
):
    width = resid_in.shape[1]
    unit_width = units_w.shape[1] // 2
    query_width = mixed[0].shape[1]
    positions = len(mixed)
    block = own_cot.shape[0]

    def rows_of(columns, first=0):
        return pl.BlockSpec((block, columns), lambda at, plan: (at + first, 0))

    first = block_idx * row_total // block
    part_shape = jax.ShapeDtypeStruct((row_total, query_width), jnp.bfloat16)
    part_specs = [rows_of(query_width)] * positions
    part_shapes = [part_shape] * positions
    if stacked:
        part_specs = [pl.BlockSpec((positions, block, query_width), lambda at, plan: (0, at, 0))]
        part_shapes = [
            jax.ShapeDtypeStruct((positions, row_total, query_width), jnp.bfloat16)
        ]

    def whole(shape):
        return pl.BlockSpec(shape, lambda at, plan: (0, 0), pipeline_mode=pl.Buffered(1))

    return pl.pallas_call(
        partial(mlp_kernel, query_width, unit_width, positions, stacked),
        grid_spec=pltpu.PrefetchScalarGridSpec(
            num_scalar_prefetch=1,
            grid=(row_total // block,),
            in_specs=[
                rows_of(width, first),
                rows_of(1, first),
                rows_of(1, first),
                whole((block, width)),
                whole((1, width)),
            ]
            + [pl.BlockSpec(memory_space=pl.ANY)] * (2 + positions)
            + [rows_of(query_width)] * positions,
            out_specs=[
                rows_of(width),
                rows_of(unit_width),
                rows_of(width),
            ]
            + part_specs,
            scratch_shapes=[
                pltpu.VMEM(output_w.shape, output_w.dtype),
                pltpu.VMEM(units_w.shape, units_w.dtype),
                pltpu.VMEM((block, unit_width), jnp.float32),
                pltpu.SemaphoreType.DMA((positions + 2,)),
                pltpu.SemaphoreType.DMA,
            ],
        ),
        out_shape=[
            jax.ShapeDtypeStruct((row_total, width), jnp.float32),
            jax.ShapeDtypeStruct((row_total, unit_width), jnp.bfloat16),
            jax.ShapeDtypeStruct((row_total, width), jnp.bfloat16),
        ]
        + part_shapes,
        cost_estimate=cost(
            row_total * width * (2 * width + 4 * unit_width),
            2 * width * (width + 2 * unit_width) + 16 * row_total * width,
        ),
        compiler_params=pltpu.CompilerParams(vmem_limit_bytes=VMEM_LIMIT),
        name="mlp",
    )(
        plan,
        resid_in,
        weight,
        own_weight,
        own_cot,
        gain[None, :],
        output_w,
        units_w,
        *swiglu_grads,
        *mixed,
    )


def centred(values):
    center = values - jnp.mean(values, axis=1, keepdims=True)
    spread = lax.rsqrt(jnp.mean(center * center, axis=1, keepdims=True) + EPS)
    return center * spread, spread


def centred_back(grad, normed, spread):
    return spread * (
        grad
        - jnp.mean(grad, axis=1, keepdims=True)
        - normed * jnp.mean(grad * normed, axis=1, keepdims=True)
    )


def slot_probs(triple_ref, rows, head, shut):
    wide = HYPER_WIDTH
    at = head * EHD
    queries = triple_ref[rows, at : at + EHD]
    keys = triple_ref[rows, wide + at : wide + at + EHD]
    values = triple_ref[rows, 2 * wide + at : 2 * wide + at + EHD]
    scores = jnp.where(shut, NEG, times_trans(keys, queries) * EHD ** (-0.5))
    parts = jnp.exp(scores - scores.max(axis=0, keepdims=True))
    return queries, keys, values, parts * (1.0 / parts.sum(axis=0, keepdims=True))


def slot_shut(open_ref, rows, count):
    key_entry = lax.broadcasted_iota(jnp.int32, (count, count), 0) // SUBWORD_SLOTS
    query_entry = lax.broadcasted_iota(jnp.int32, (count, count), 1) // SUBWORD_SLOTS
    return (key_entry != query_entry) | (open_ref[rows, :] == 0.0)


def hyper_wide_kernel(
    rows_ref,
    open_ref,
    gains_ref,
    triple_w_ref,
    merge_w_ref,
    expand_w_ref,
    reduce_w_ref,
    length_ref,
    first_ref,
    triple_ref,
    mixed_ref,
    resid_ref,
    second_ref,
    active_ref,
    slope_ref,
    pooled_ref,
):
    bfloat = jnp.bfloat16
    rows_in = rows_ref[...].astype(jnp.float32)
    first_in = (centred(rows_in)[0] * gains_ref[0:1, :]).astype(bfloat)
    first_ref[...] = first_in
    triple_ref[...] = matmul(first_in, triple_w_ref[...]).astype(bfloat)
    total = rows_in.shape[0]
    count = min(128, total)
    for first in range(0, total, count):
        rows = slice(first, first + count)
        shut = slot_shut(open_ref, rows, count)
        heads = []
        for head in range(EH):
            _, _, values, probs = slot_probs(triple_ref, rows, head, shut)
            heads.append(trans_times(values, probs.astype(bfloat)))
        mixed_ref[rows, :] = jnp.concatenate(heads, axis=0).T.astype(bfloat)
    resid_one = rows_in + matmul(mixed_ref[...], merge_w_ref[...])
    resid_ref[...] = resid_one
    second_in = (centred(resid_one)[0] * gains_ref[1:2, :]).astype(bfloat)
    second_ref[...] = second_in
    expanded = matmul(second_in, expand_w_ref[...])
    below = 0.5 * (1.0 + lax.erf(expanded * 0.5**0.5))
    active = (expanded * below).astype(bfloat)
    active_ref[...] = active
    resid_two = resid_one + matmul(active, reduce_w_ref[...])
    kept = jnp.where(open_ref[...] == 0.0, 0.0, resid_two)
    pooled = kept.reshape(total // SUBWORD_SLOTS, SUBWORD_SLOTS, kept.shape[1]).sum(axis=1)
    pooled_ref[...] = (pooled / length_ref[...]).astype(bfloat)
    bell = jnp.exp(-0.5 * expanded * expanded) * (2.0 * math.pi) ** (-0.5)
    slope_ref[...] = (below + expanded * bell).astype(bfloat)


def hyper_wide(rows_in, open_rows, gains, triple_w, merge_w, expand_w, reduce_w, lengths):
    total, width = rows_in.shape
    block = min(256, total)
    units = expand_w.shape[1]
    bfloat = jnp.bfloat16
    single = jnp.float32

    def rows_of(columns):
        return pl.BlockSpec((block, columns), lambda at: (at, 0))

    def whole(array):
        return pl.BlockSpec(array.shape, lambda at: (0, 0), pipeline_mode=pl.Buffered(1))

    outs = [
        (width, bfloat),
        (3 * width, bfloat),
        (width, bfloat),
        (width, single),
        (width, bfloat),
        (units, bfloat),
        (units, bfloat),
    ]
    return pl.pallas_call(
        hyper_wide_kernel,
        grid=(total // block,),
        in_specs=[rows_of(width), rows_of(1)]
        + [whole(array) for array in (gains, triple_w, merge_w, expand_w, reduce_w)]
        + [pl.BlockSpec((block // SUBWORD_SLOTS, 1), lambda at: (at, 0))],
        out_specs=[rows_of(columns) for columns, _ in outs]
        + [pl.BlockSpec((block // SUBWORD_SLOTS, width), lambda at: (at, 0))],
        out_shape=[jax.ShapeDtypeStruct((total, columns), kind) for columns, kind in outs]
        + [jax.ShapeDtypeStruct((total // SUBWORD_SLOTS, width), bfloat)],
        cost_estimate=cost(16 * total * width * units, 12 * total * units),
        compiler_params=pltpu.CompilerParams(vmem_limit_bytes=VMEM_LIMIT),
        name="hyper_wide",
    )(rows_in, open_rows, gains, triple_w, merge_w, expand_w, reduce_w, lengths)


def hyper_back_units_kernel(
    dp_size,
    pooled_refs,
    scale_ref,
    gains_ref,
    resid_ref,
    slope_ref,
    mixed_share_ref,
    second_share_ref,
    active_share_ref,
    merge_w_ref,
    expand_w_ref,
    reduce_w_ref,
    resid_out,
    mixed_out,
    early_out,
    gains_out,
    reduce_acc,
    expand_acc,
    merge_acc,
):
    bfloat = jnp.bfloat16
    step = pl.program_id(0)
    total, width = resid_ref.shape
    pooled_grad = sum(ref[...].astype(jnp.float32) for ref in pooled_refs)
    grid_grad = jnp.broadcast_to(
        pooled_grad[:, None, :], (total // SUBWORD_SLOTS, SUBWORD_SLOTS, width)
    ).reshape(total, width)
    grid_grad = grid_grad * scale_ref[...]
    reduce_in = grid_grad.astype(bfloat)
    expand_in = times_trans(reduce_in, reduce_w_ref[...]) * slope_ref[...].astype(jnp.float32)
    expand_in = expand_in.astype(bfloat)
    second_grad = times_trans(expand_in, expand_w_ref[...])
    normed, spread = centred(resid_ref[...])
    gain_two = (second_grad * normed).sum(axis=0, keepdims=True)
    resid_grad = grid_grad + centred_back(second_grad * gains_ref[1:2, :], normed, spread)
    resid_out[...] = resid_grad
    merge_in = resid_grad.astype(bfloat)
    mixed_out[...] = times_trans(merge_in, merge_w_ref[...]).astype(bfloat)

    @pl.when(step == 0)
    def _():
        for ref in (reduce_acc, expand_acc, merge_acc, gains_out):
            ref[...] = jnp.zeros_like(ref)

    gains_out[0:1, :] += gain_two
    reduce_acc[...] += trans_times(active_share_ref[...], reduce_in)
    expand_acc[...] += trans_times(second_share_ref[...], expand_in)
    merge_acc[...] += trans_times(mixed_share_ref[...], merge_in)

    @pl.when(step == pl.num_programs(0) - 1)
    def _():
        depth = expand_acc.shape[0] // dp_size
        deep = reduce_acc.shape[0] // expand_acc.shape[0]
        reduced = reduce_acc[...].astype(bfloat).reshape(dp_size, deep, depth, width)
        for at in range(deep):
            early_out[:, at * width : (at + 1) * width] = reduced[:, at].reshape(
                dp_size * depth, width
            )
        units = expand_acc.shape[1]
        early_out[:, deep * width : deep * width + units] = expand_acc[...].astype(bfloat)
        early_out[:, deep * width + units :] = merge_acc[...].astype(bfloat)


def hyper_back_slots_kernel(
    resid_grad_ref,
    mixed_grad_ref,
    rows_ref,
    open_ref,
    gains_ref,
    triple_ref,
    first_share_ref,
    triple_w_ref,
    rows_out,
    late_out,
    gains_out,
    triple_acc,
    triple_in,
):
    bfloat = jnp.bfloat16
    step = pl.program_id(0)
    total, width = rows_ref.shape
    count = min(128, total)
    for first in range(0, total, count):
        rows = slice(first, first + count)
        shut = slot_shut(open_ref, rows, count)
        query_grads = []
        for head in range(EH):
            queries, keys, values, probs = slot_probs(triple_ref, rows, head, shut)
            at = head * EHD
            grad = mixed_grad_ref[rows, at : at + EHD]
            prob_grad = times_trans(values, grad)
            delta = (probs * prob_grad).sum(axis=0, keepdims=True)
            score_grad = (probs * (prob_grad - delta)).astype(bfloat)
            query_grads.append(trans_times(keys, score_grad))
            key_grad = matmul(score_grad, queries) * EHD ** (-0.5)
            value_grad = matmul(probs.astype(bfloat), grad)
            triple_in[rows, width + at : width + at + EHD] = key_grad.astype(bfloat)
            triple_in[rows, 2 * width + at : 2 * width + at + EHD] = value_grad.astype(bfloat)
        query_grad = jnp.concatenate(query_grads, axis=0).T * EHD ** (-0.5)
        triple_in[rows, :width] = query_grad.astype(bfloat)
    triple_grad = triple_in[...]
    first_grad = times_trans(triple_grad, triple_w_ref[...])
    normed, spread = centred(rows_ref[...].astype(jnp.float32))
    gain_one = (first_grad * normed).sum(axis=0, keepdims=True)
    rows_grad = resid_grad_ref[...] + centred_back(first_grad * gains_ref[0:1, :], normed, spread)
    rows_out[...] = rows_grad.astype(bfloat)

    @pl.when(step == 0)
    def _():
        triple_acc[...] = jnp.zeros_like(triple_acc)
        gains_out[...] = jnp.zeros_like(gains_out)

    gains_out[0:1, :] += gain_one
    triple_acc[...] += trans_times(first_share_ref[...], triple_grad)

    @pl.when(step == pl.num_programs(0) - 1)
    def _():
        late_out[...] = triple_acc[...].astype(bfloat)


def row_block(columns, rows):
    return pl.BlockSpec((rows, columns), lambda at: (at, 0))


def whole_block(shape):
    return pl.BlockSpec(shape, lambda at: (0, 0), pipeline_mode=pl.Buffered(1))


def hyper_back_units(dp_size, pooled, scale, gains, resid, slope, shares, weights):
    total, width = resid.shape
    block = min(256, total)
    units = slope.shape[1]
    share_width = shares[0].shape[1]
    deep = shares[2].shape[1] // share_width
    bfloat = jnp.bfloat16
    single = jnp.float32

    def kernel(*refs):
        hyper_back_units_kernel(dp_size, refs[: len(pooled)], *refs[len(pooled) :])

    early_width = deep * width + units + width
    return pl.pallas_call(
        kernel,
        grid=(total // block,),
        in_specs=[row_block(width, block // SUBWORD_SLOTS)] * len(pooled)
        + [row_block(1, block), whole_block(gains.shape)]
        + [row_block(width, block), row_block(units, block)]
        + [row_block(array.shape[1], block) for array in shares]
        + [whole_block(array.shape) for array in weights],
        out_specs=[
            row_block(width, block),
            row_block(width, block),
            pl.BlockSpec((share_width, early_width), lambda at: (0, 0)),
            pl.BlockSpec((8, width), lambda at: (0, 0)),
        ],
        out_shape=[
            jax.ShapeDtypeStruct((total, width), single),
            jax.ShapeDtypeStruct((total, width), bfloat),
            jax.ShapeDtypeStruct((share_width, early_width), bfloat),
            jax.ShapeDtypeStruct((8, width), single),
        ],
        scratch_shapes=[
            pltpu.VMEM((deep * share_width, width), single),
            pltpu.VMEM((share_width, units), single),
            pltpu.VMEM((share_width, width), single),
        ],
        cost_estimate=cost(12 * total * width * units, 6 * total * units),
        compiler_params=pltpu.CompilerParams(vmem_limit_bytes=VMEM_LIMIT),
        name="hyper_back_units",
    )(*pooled, scale, gains, resid, slope, *shares, *weights)


def hyper_back_slots(resid_grad, mixed_grad, rows_in, open_rows, gains, triple, first_share, weight):
    total, width = rows_in.shape
    block = min(256, total)
    share_width = first_share.shape[1]
    bfloat = jnp.bfloat16
    single = jnp.float32
    return pl.pallas_call(
        hyper_back_slots_kernel,
        grid=(total // block,),
        in_specs=[row_block(width, block)] * 3
        + [row_block(1, block), whole_block(gains.shape), row_block(3 * width, block)]
        + [row_block(share_width, block), whole_block(weight.shape)],
        out_specs=[
            row_block(width, block),
            pl.BlockSpec((share_width, 3 * width), lambda at: (0, 0)),
            pl.BlockSpec((8, width), lambda at: (0, 0)),
        ],
        out_shape=[
            jax.ShapeDtypeStruct((total, width), bfloat),
            jax.ShapeDtypeStruct((share_width, 3 * width), bfloat),
            jax.ShapeDtypeStruct((8, width), single),
        ],
        scratch_shapes=[
            pltpu.VMEM((share_width, 3 * width), single),
            pltpu.VMEM((block, 3 * width), bfloat),
        ],
        cost_estimate=cost(40 * total * width * width, 8 * total * width),
        compiler_params=pltpu.CompilerParams(vmem_limit_bytes=VMEM_LIMIT),
        name="hyper_back_slots",
    )(resid_grad, mixed_grad, rows_in, open_rows, gains, triple, first_share, weight)


def per_device(
    subword_embedding_rows,
    entry_subword_index,
    entry_lengths,
    entry_counts,
    encoder_triple,
    encoder_merge,
    encoder_expand,
    encoder_reduce,
    embed_project,
    normone_gain,
    normtwo_gain,
    frozen_query,
    frozen_key,
    frozen_value,
    frozen_output,
    frozen_gate,
    frozen_upward,
    frozen_downward,
    prenorm_gain,
    midnorm_gain,
    text_tokens,
    cotangent,
):
    bfloat = jnp.bfloat16
    single = jnp.float32
    dp_size = lax.axis_size("dp")
    tensor_size = lax.axis_size("tensor")
    dp_at = lax.axis_index("dp")
    tensor_at = lax.axis_index("tensor")
    device_at = dp_at * tensor_size + tensor_at
    entries = entry_subword_index.shape[0]
    entry_total = entries * dp_size * tensor_size
    flat_rows = entries * SUBWORD_SLOTS
    table_rows = subword_embedding_rows.shape[0]
    model_width = embed_project.shape[1]

    with jax.named_scope("ids"):
        packed = jnp.concatenate(
            [entry_subword_index, entry_counts[:, None], entry_lengths[:, None]], axis=1
        )
        packed_width = packed.shape[1]
        first_weights = jnp.concatenate(
            [frozen_query, frozen_key, frozen_value, frozen_downward], axis=1
        )
        packed_dp = lax.all_gather(tie(packed, first_weights), "dp", axis=0, tiled=False)
    with jax.named_scope("first_weights"):
        first_weights = lax.all_gather(first_weights, "dp", axis=0, tiled=True)
        query_width = frozen_query.shape[1]
        key_width = frozen_key.shape[1]
        triple_width = query_width + 2 * key_width
        unit_width = frozen_gate.shape[1]
        full_downward = first_weights[:, triple_width:]
        second_weights = jnp.concatenate([frozen_gate, frozen_upward], axis=1)
    with jax.named_scope("lookup"):
        local_ids = packed_dp[:, :, :SUBWORD_SLOTS].reshape(-1) - dp_at * table_rows
        inside = (local_ids >= 0) & (local_ids < table_rows)
        served = jnp.take(subword_embedding_rows, jnp.clip(local_ids, 0, table_rows - 1), axis=0)
        served = jnp.where(inside[:, None], served, jnp.zeros((), bfloat))
        served_all = lax.all_to_all(
            served.reshape(dp_size, flat_rows, HYPER_WIDTH), "dp", 0, 0, tiled=True
        )
        rows_in = jnp.sum(served_all.astype(single), axis=0)
    with jax.named_scope("cot_ring"):
        cot_blocks = [cotangent, ring(cotangent)]
        length = text_tokens.shape[0] * tensor_size
        cosine, sine = rope_lanes(length)
        cot_blocks.append(ring(cot_blocks[-1]))
        rows_in, cosine, sine, second_weights, *cot_blocks = lax.optimization_barrier(
            (rows_in, cosine, sine, second_weights, *cot_blocks)
        )
        second_weights = lax.all_gather(second_weights, "dp", axis=0, tiled=True)
        packed_all = from_all(
            tie(jnp.concatenate([packed_dp.reshape(-1), text_tokens]), cot_blocks[1])
        )
    with jax.named_scope("hyper_wide"):
        rows_blocks = from_all(rows_in.astype(bfloat))
    with jax.named_scope("hyper_wide"):
        rows_wide = jnp.concatenate(in_order(rows_blocks, tensor_at), axis=0)
        packed_all = jnp.stack(in_order(packed_all, tensor_at))
        ids_size = dp_size * entries * packed_width
        packed_ids = packed_all[:, :ids_size].reshape(tensor_size, dp_size, entries, packed_width)
        lengths_wide = lax.dynamic_index_in_dim(packed_ids, dp_at, 1, keepdims=False)
        lengths_wide = lengths_wide[:, :, SUBWORD_SLOTS + 1].reshape(-1)
        valid_wide = jnp.arange(SUBWORD_SLOTS)[None, :] < lengths_wide[:, None]
        valid_wide = valid_wide.astype(single)
        counts_wide = lengths_wide.astype(single)[:, None]
        open_wide = valid_wide.reshape(-1, 1)
        scale_wide = (valid_wide / counts_wide).reshape(-1, 1)
        gain_pair = jnp.stack([normone_gain, normtwo_gain])
        encoders = (encoder_triple, encoder_merge, encoder_expand, encoder_reduce)
        first_in, triple, mixed, resid_one, second_in, activated, slope, dp_pooled = hyper_wide(
            rows_wide, open_wide, gain_pair, *encoders, counts_wide
        )
    with jax.named_scope("output_weights"):
        output_blocks = from_all(tie(frozen_output, dp_pooled))
    with jax.named_scope("pooled_gather"):
        all_pooled = lax.all_gather(dp_pooled, "dp", axis=0, tiled=True)
    with jax.named_scope("output_weights"):
        output_weights = jnp.concatenate(output_blocks, axis=1)
        output_weights, all_pooled = lax.optimization_barrier((output_weights, all_pooled))
        output_weights = lax.all_gather(
            tie(output_weights, first_weights), "dp", axis=0, tiled=True
        )
    with jax.named_scope("cot_ring"):
        cot_blocks.append(ring(tie(cot_blocks[-1], all_pooled)))
    with jax.named_scope("entry_vectors"):
        seq_tokens = packed_all[:, ids_size:].reshape(-1)
        all_vectors, seq_triple = entry(
            seq_tokens, all_pooled, embed_project, prenorm_gain, first_weights, triple_width
        )

    with jax.named_scope("attention_fwd"):
        block_rows = min(512, length)
        block_total = length // block_rows
        first_mixed, first_totals = attention(
            seq_triple, cosine, sine, query_width, 0, block_rows
        )

    with jax.named_scope("mlp_rows"):
        late_ids, late_tokens = tie_all(first_mixed, packed_ids, seq_tokens)
        late_ids = late_ids.transpose(1, 0, 2, 3).reshape(entry_total, packed_width)
        all_ids = late_ids[:, :SUBWORD_SLOTS].reshape(-1)
        all_weights = (1.0 / jnp.log(1.0 + late_ids[:, SUBWORD_SLOTS].astype(single))).astype(
            bfloat
        )
        rows_here = text_tokens.shape[0]
        seq_hot = (late_tokens[:, None] == jnp.arange(entry_total)[None, :]).astype(bfloat)
        seq_weight = matmul(seq_hot, all_weights[:, None])
        own_rows_here = jnp.arange(length) // rows_here == tensor_at
        own_weight = jnp.where(own_rows_here[:, None], seq_weight, 0.0)
        resid_in = matmul(seq_hot, all_vectors).astype(bfloat)
        per_block = block_rows // rows_here
        vectors = lax.dynamic_slice_in_dim(all_vectors, device_at * entries, entries, 0)

    with jax.named_scope("attention_fwd"):
        seq_triple = tie(seq_triple, resid_in)
        mixed_parts = [[first_mixed]]
        for first in range(block_rows, length, block_rows):
            lm_mixed, last_totals = attention(
                seq_triple, cosine, sine, query_width, first, block_rows
            )
            mixed_parts.append([lm_mixed])
    with jax.named_scope("mixed_ring"):
        for block_idx, parts in enumerate(mixed_parts):
            last_part = ring(parts[0], tensor_size - 1)
            parts.append(ring(parts[0]))
            for step in range(2, tensor_size - 1):
                parts.append(ring(parts[-1]))
            parts.append(last_part)

    def share_slice(values):
        rows, width = values.shape
        split = values.reshape(rows, dp_size, tensor_size, width // (dp_size * tensor_size))
        return lax.dynamic_index_in_dim(split, tensor_at, 2, keepdims=False).reshape(
            rows, width // tensor_size
        )

    def share(values, position):
        width = values.shape[1]
        depth = width // (dp_size * tensor_size)
        row = lax.broadcasted_iota(jnp.int32, (width, width // tensor_size), 0)
        column = lax.broadcasted_iota(jnp.int32, (width, width // tensor_size), 1)
        held = (column // depth * tensor_size + position) * depth + column % depth
        return matmul(values, (row == held).astype(bfloat)).astype(bfloat)

    with jax.named_scope("swiglu_grad"):
        late_cots = tie(cot_blocks, lm_mixed, mixed_parts[0][1])
        swiglu_grads = swiglu_products(late_cots, first_weights, triple_width, unit_width)

    with jax.named_scope("mlp"):
        places = lax.rem(tensor_at + tensor_size - jnp.arange(tensor_size), tensor_size)
        resid_blocks = []
        layer_parts = []
        mid_parts = []
        mixed_grads = []
        for block_idx, parts in enumerate(mixed_parts):
            last = block_idx == block_total - 1
            rows = slice(block_idx * block_rows, (block_idx + 1) * block_rows)
            if block_idx == 0:
                near = [[later[1], later[-1]] for later in mixed_parts[1:]]
                late_core = tie(lax.rem(dp_at, 2), lm_mixed)
                pooled_pairs = all_pooled.reshape(entry_total, dp_size // 2, 2, -1)
                pooled_kept, pooled_sent = [
                    lax.dynamic_index_in_dim(pooled_pairs, at, 2, keepdims=False).reshape(
                        entry_total, -1
                    )
                    for at in (late_core, 1 - late_core)
                ]
                parts, near, pooled_kept, pooled_sent = lax.optimization_barrier(
                    (parts, near, pooled_kept, pooled_sent)
                )
                for later, (below, above) in zip(mixed_parts[1:], near):
                    later[1], later[-1] = below, above
                    for step in range(2, tensor_size - 1):
                        later[step] = ring(later[step - 1])
            else:
                parts, layer_parts, mid_parts = lax.optimization_barrier(
                    (parts, layer_parts, mid_parts)
                )
            block_places = block_idx * per_block + jnp.arange(per_block)
            block_places = lax.rem(tensor_at + tensor_size - block_places, tensor_size)
            resid_mid, swiglu_low, mid_low, *mixed_part = mlp(
                jnp.concatenate([places, block_places]),
                block_idx,
                block_rows,
                resid_in,
                seq_weight,
                own_weight,
                cotangent,
                swiglu_grads,
                midnorm_gain,
                output_weights,
                second_weights,
                parts,
                not last,
            )
            resid_blocks.append(resid_mid)
            if not last:
                mixed_grads.append(
                    lax.psum_scatter(
                        mixed_part[0].reshape(-1, query_width),
                        "tensor",
                        scatter_dimension=0,
                        tiled=True,
                    )
                )
                layer_parts.append(times_trans(swiglu_low, full_downward).astype(bfloat))
                mid_parts.append(trans_times(seq_hot[rows], mid_low).astype(bfloat))
                continue
            carried = None
            for step in [*range(1, tensor_size), 0]:
                part = mixed_part[step]
                if step == 2:
                    mid_parts.append(trans_times(seq_hot[rows], mid_low).astype(bfloat))
                    carried, mid_parts = lax.optimization_barrier((carried, mid_parts))
                    swiglu_low = tie(swiglu_low, carried)
                if step == 3:
                    layer_parts.append(times_trans(swiglu_low, full_downward).astype(bfloat))
                    late_position = tie(tensor_at, mid_parts)
                    shares = [
                        share_slice(array) for array in (first_in, mixed, second_in)
                    ] + [share(activated, late_position)]
                    layer_cut = model_width // 2
                    layer_halves = [
                        jnp.concatenate([part[:, columns] for part in layer_parts], axis=0)
                        for columns in (slice(None, layer_cut), slice(layer_cut, None))
                    ]
                    carried, layer_halves, shares = lax.optimization_barrier(
                        (carried, layer_halves, shares)
                    )
                if step == 0:
                    pair_out = None
                    query_parts = []
                    for at, mixed_grad in enumerate(mixed_grads):
                        query_part, pair_out = attention_back(
                            seq_triple,
                            cosine,
                            sine,
                            mixed_grad,
                            first_mixed,
                            first_totals,
                            at * block_rows,
                            pair_out,
                        )
                        query_parts.append(query_part)
                    carried, pair_out = lax.optimization_barrier((carried, pair_out))
                if carried is not None:
                    part = (part.astype(single) + carried.astype(single)).astype(bfloat)
                if step > 0:
                    carried = ring(part)
            last_grad = part

    with jax.named_scope("layer_out"):
        layer_near, layer_far = layer_halves
        layer_near = lax.psum_scatter(
            tie(layer_near, last_grad), "tensor", scatter_dimension=0, tiled=True
        )
        blocks_of = [
            lax.dynamic_slice_in_dim(
                block, lax.rem(tensor_at * rows_here, block_rows), rows_here, 0
            )
            for block in resid_blocks
        ]
        resid_own = blocks_of[0]
        for block_idx in range(1, block_total):
            resid_own = jnp.where(
                tensor_at * rows_here // block_rows == block_idx, blocks_of[block_idx], resid_own
            )
    with jax.named_scope("attention_bwd"):
        query_part, pair_out = attention_back(
            seq_triple,
            cosine,
            sine,
            last_grad,
            lm_mixed,
            last_totals,
            length - block_rows,
            pair_out,
        )
        query_parts.append(query_part)

    with jax.named_scope("entry_bwd"):
        entry_part, pooled_part = entry_back(
            seq_tokens,
            all_vectors,
            prenorm_gain,
            first_weights,
            embed_project,
            pair_out,
            mid_parts,
            query_parts,
        )
        project_sent = trans_times(pooled_sent, entry_part).astype(bfloat)
        project_kept = trans_times(pooled_kept, entry_part)
        project_sent = lax.ppermute(project_sent, "dp", [(i, i ^ 1) for i in range(dp_size)])
        project_part = (project_kept + project_sent.astype(single)).astype(bfloat)
        pooled_shares, project_part = lax.optimization_barrier(
            (to_owners(pooled_part), project_part)
        )
        pooled_part = jnp.sum(pooled_shares.astype(single), axis=0).astype(bfloat)
        pooled_grads = from_all(pooled_part)

    with jax.named_scope("hyper_bwd"):
        project_shares = lax.all_to_all(
            project_part.reshape(dp_size // 2, -1, model_width),
            "dp",
            0,
            0,
            axis_index_groups=[list(range(first, dp_size, 2)) for first in range(2)],
            tiled=True,
        )
    with jax.named_scope("layer_out"):
        layer_far = lax.psum_scatter(
            tie(layer_far, pooled_grads, layer_near), "tensor", scatter_dimension=0, tiled=True
        )
        layer_final = resid_own + jnp.concatenate([layer_near, layer_far], axis=1).astype(single)
    with jax.named_scope("hyper_bwd"):
        resid_grad, mixed_grad, early, gain_two = hyper_back_units(
            dp_size,
            pooled_grads,
            scale_wide,
            gain_pair,
            resid_one,
            slope,
            shares[1:],
            encoders[1:],
        )
        resid_grad, early, project_shares = lax.optimization_barrier(
            (resid_grad, early, project_shares)
        )
        early = to_owners(early)
        rows_low, late, gain_one = hyper_back_slots(
            resid_grad,
            mixed_grad,
            rows_wide,
            open_wide,
            gain_pair,
            triple,
            shares[0],
            encoder_triple,
        )

    with jax.named_scope("grads_out"):
        rows_low, early, project_shares = lax.optimization_barrier(
            (rows_low, early, project_shares)
        )
        early = jnp.sum(early.astype(single), axis=0)
        project_grad = jnp.sum(project_shares.astype(single), axis=0).astype(bfloat)
        all_rows = lax.all_gather(rows_low, "dp", axis=0, tiled=True)
        late, project_grad = tie_all(rows_low, late, project_grad)
        project_grad = project_grad.reshape(tensor_size, -1, model_width)
        project_grad = lax.all_to_all(project_grad, "tensor", 0, 0, tiled=True)
        project_grad = jnp.sum(project_grad.astype(single), axis=0)
        own_rows = table_rows // tensor_size
        row_hot = (
            (jnp.arange(own_rows) + device_at * own_rows)[:, None] == all_ids[None, :]
        ).astype(bfloat)
        subword_grad = matmul(row_hot, all_rows)

        gain_grads = jnp.concatenate([gain_one[:1], gain_two[:1]], axis=0)
        gain_grads = gain_grads.reshape(2, dp_size, tensor_size, -1)
        gain_grads = lax.dynamic_index_in_dim(gain_grads, tensor_at, 2, keepdims=False)
        gain_grads = gain_grads.reshape(2, -1).transpose(1, 0).astype(bfloat)
        late = jnp.concatenate([late, jnp.pad(gain_grads, ((0, 0), (0, 126)))], axis=1)
        late = scatter_dp(late)
        depth = early.shape[0]
        deep = encoder_reduce.shape[0] // HYPER_WIDTH
        reduce_width = deep * HYPER_WIDTH
        expand_width = encoder_expand.shape[1]
        reduce_grad = early[:, :reduce_width].reshape(depth, deep, HYPER_WIDTH)
        reduce_grad = reduce_grad.transpose(1, 0, 2).reshape(deep * depth, HYPER_WIDTH)
        expand_grad = early[:, reduce_width : reduce_width + expand_width]
        merge_grad = early[:, reduce_width + expand_width :]
        grad_width = encoder_triple.shape[1]
    return (
        layer_final.astype(bfloat),
        vectors,
        subword_grad,
        late[:, :grad_width],
        merge_grad,
        expand_grad,
        reduce_grad,
        project_grad,
        late[:, grad_width],
        late[:, grad_width + 1],
    )


def solution(mesh):
    return jax.shard_map(
        per_device,
        mesh=mesh,
        in_specs=(
            P("dp", None),
            P(("dp", "tensor"), None),
            P(("dp", "tensor")),
            P(("dp", "tensor")),
            P(),
            P(),
            P(),
            P(),
            P(),
            P(),
            P(),
            P("dp", "tensor"),
            P("dp", "tensor"),
            P("dp", "tensor"),
            P("dp", "tensor"),
            P("dp", "tensor"),
            P("dp", "tensor"),
            P("dp", "tensor"),
            P(),
            P(),
            P(("dp", "tensor")),
            P(("dp", "tensor"), None),
        ),
        out_specs=(
            P(("dp", "tensor"), None),
            P(("dp", "tensor"), None),
            P(("dp", "tensor"), None),
            P(("dp", "tensor"), None),
            P(("dp", "tensor"), None),
            P(("dp", "tensor"), None),
            P(("dp", "tensor"), None),
            P(("dp", "tensor"), None),
            P(("dp", "tensor")),
            P(("dp", "tensor")),
        ),
        check_vma=False,
    )
```
